256 devices in a mesh: lat: 8 (over y, x_hi), lon: 32 (over z, x_lo, core).
Axes of the slice: x: 4 (x_hi: 2, x_lo: 2; x = x_hi * 2 + x_lo), y: 4, z: 8, core: 2. Of those that a mesh axis runs over, the one named last changes fastest.
Arguments:
- tokens: bfloat16 [2, 48, 384, 192], P(None, 'lat', 'lon'), may hold values from -6 to 6
- grad_mixed: bfloat16 [2, 48, 384, 192], P(None, 'lat', 'lon'), may hold values from -6 to 6
- w_qkv: bfloat16 [2, 192, 576], replicated, may hold values from -0.4375 to 0.4375
- w_proj: bfloat16 [2, 192, 192], replicated, may hold values from -0.4375 to 0.4375
- w_up: bfloat16 [2, 192, 768], replicated, may hold values from -0.4375 to 0.4375
- w_down: bfloat16 [2, 768, 192], replicated, may hold values from -0.21875 to 0.21875
- gains: float32 [2, 2, 192], replicated, may hold values from 0.5 to 1.5
- bias_table: float32 [2, 1, 8, 6, 3312], P(None, None, 'lat'), may hold values from -300 to 300
- rel_index: int32 [144, 144], replicated, may hold values from 0 to 3311
- mask_ids: int32 [48], P('lat'), may hold values from 0 to 15, never falling along the last dimension, each value on 1 to 6 neighbouring positions
Outputs:
- mixed: bfloat16 [2, 48, 384, 192], P(None, 'lat', 'lon')
- grad_tokens: bfloat16 [2, 48, 384, 192], P(None, 'lat', 'lon')
- grad_qkv: float32 [2, 192, 576], P(None, None, 'lon')
- grad_proj: float32 [2, 192, 192], P(None, None, 'lon')
- grad_up: float32 [2, 192, 768], P(None, None, 'lon')
- grad_down: float32 [2, 768, 192], P(None, None, 'lon')
- grad_table: float32 [2, 1, 8, 6, 3312], P(None, None, 'lat')
The draws below stay inside these ranges and needn't reach their ends.
Inputs may be any that keep to these rules, and one draw needn't show every extreme that they name: `mask_ids`: ids never fall along the rows; a run of one id covers at most 6 rows.
All inputs are finite; a program needn't handle non-finite values.
Results may differ from the reference program's by a relative error of at most 0.04.
Values may be sent and summed in bfloat16 or wider, within the bound.
A program may use at most 64 MiB of HBM per device.

```python
import math
import jax
import jax.numpy as jnp
import numpy as np
from jax import lax

C = 192
HEADS = 6
LEVELS = 2
WIN_TOK = 144
POS = 3312
NLAT = 48
NLON = 384
LAT_WINS = 8
LEV_WINS = 1


def draw_bias_table(key, part):
    key = jax.random.fold_in(key, 7)
    shape = (2, LEV_WINS, LAT_WINS, HEADS, POS)
    base = jax.random.normal(key, shape, jnp.float32)
    return base


def set_ends(values, key, least, largest):
    index_at = [jax.random.randint(jax.random.fold_in(key, axis), (), 0, length) for axis, length in enumerate(values.shape)]
    longest = values.shape.index(max(values.shape))
    beside = index_at[:longest] + [(index_at[longest] + 1) % values.shape[longest]] + index_at[longest + 1:]
    return values.at[tuple(index_at)].set(least).at[tuple(beside)].set(largest)


def strengthened(entries, stream_key, source, target, shards_of, factor):
    owner, partner = [(jnp.arange(entries.shape[axis_at]) // (entries.shape[axis_at] // shards_of)).reshape([-1 if axis == axis_at else 1 for axis in range(entries.ndim)]) for axis_at in (source, target)]
    chosen = jax.random.permutation(stream_key, shards_of)[partner]
    strong = (owner == chosen) | (owner == (partner + shards_of // 2) % shards_of)
    return jnp.where(strong, factor * entries, entries)


def block_scale(stream_key, dims, cuts, least, top_value):
    loudness = 1.0
    for axis_at, shards_of in cuts:
        heights = jax.random.uniform(jax.random.fold_in(jax.random.fold_in(stream_key, 6), axis_at), (shards_of,), jnp.float32, least / len(cuts), top_value / len(cuts))
        loudness = loudness * jnp.repeat(jnp.exp(heights), dims[axis_at] // shards_of).reshape((-1,) + (1,) * (len(dims) - 1 - axis_at))
    return loudness


def split_up(count, total, most, skew):
    loads = [(1 << 20) // math.isqrt(standing ** skew) + 1 for standing in range(2, count + 1)]
    rest, counts = total - most - (count - 1), [1] * (count - 1)
    while rest > 0:
        free = [i for i in range(count - 1) if counts[i] < most]
        pool, budget = sum([loads[i] for i in free]), rest
        for i in free:
            more = min(most - counts[i], max(1, budget * loads[i] // pool), rest)
            counts[i] = counts[i] + more
            rest = rest - more
    return np.array([most] + counts)


def uneven(key, number_of, total, reach, lean):
    if number_of == 2:
        one = jax.random.randint(key, (), max(1, total - reach), min(reach, total - 1) + 1)
        return jnp.stack([one, total - one])
    lengths = jnp.asarray(split_up(number_of, total, reach, lean), jnp.int32)
    twos = (number_of - 1) // 2
    giver, receiver = lengths[1:1 + 2 * twos:2], lengths[2:2 + 2 * twos:2]
    room = jnp.minimum(giver - 1, reach - receiver)
    passed = jax.random.randint(jax.random.fold_in(key, 1), (twos,), 0, 1 << 20) % (room + 1)
    lengths = lengths.at[1:1 + 2 * twos:2].set(giver - passed).at[2:2 + 2 * twos:2].set(receiver + passed)
    return lengths[jax.random.permutation(jax.random.fold_in(key, 2), number_of)]


def noise(rng, shape, scale, most, shards=(), kind=jnp.bfloat16):
    loudness = block_scale(rng, shape, shards, -0.22, 0.18) if shards else 1.0
    entries = jax.random.normal(rng, shape, jnp.float32) * scale * loudness
    return jnp.minimum(jnp.maximum(entries, -most), most).astype(kind)


def heavy_noise(stream_key, shape, deviation, bound, pieces, heavy, kind=jnp.bfloat16):
    array = deviation * jax.random.normal(stream_key, shape, jnp.float32)
    if pieces:
        array = array * block_scale(stream_key, shape, pieces, -0.22, 0.18)
    return jnp.clip(strengthened(array, jax.random.fold_in(stream_key, 3), *heavy), -bound, bound).astype(kind)


def setup_inputs(seed: int = 0) -> dict:
    keys = jax.random.split(jax.random.key(seed), 11)
    tokens = noise(keys[0], (LEVELS, NLAT, NLON, C), 1.0, 6.0, ((1, 8), (2, 32)))
    grad_mixed = heavy_noise(keys[1], (LEVELS, NLAT, NLON, C), 1.0, 6.0, ((1, 8), (2, 32)), (2, 3, 32, 2.75))
    w_qkv = noise(keys[2], (2, C, 3 * C), C ** -0.5, 0.4375)
    w_proj = noise(keys[3], (2, C, C), C ** -0.5, 0.4375)
    w_up = noise(keys[4], (2, C, 4 * C), C ** -0.5, 0.4375)
    w_down = noise(keys[5], (2, 4 * C, C), (4 * C) ** -0.5, 0.21875)
    gains = jnp.clip(1.0 + 0.1 * jax.random.normal(keys[6], (2, 2, C), jnp.float32), 0.5, 1.5)
    bias_table = draw_bias_table(jax.random.fold_in(keys[10], 71), 0)
    rel_index = set_ends(jax.random.randint(keys[8], (WIN_TOK, WIN_TOK), 0, POS), jax.random.fold_in(keys[8], 1), 0, POS - 1).astype(jnp.int32)
    mask_ids = jnp.searchsorted(jnp.cumsum(uneven(keys[9], NLAT // 3, NLAT, 6, 0)), jnp.arange(NLAT), side="right").astype(jnp.int32)
    return dict(tokens=tokens, grad_mixed=grad_mixed, w_qkv=w_qkv, w_proj=w_proj, w_up=w_up, w_down=w_down, gains=gains, bias_table=bias_table, rel_index=rel_index, mask_ids=mask_ids)


EPS = 1e-05
NEGATIVE = -1e+30

def to_windows(field):
    levels, n_rows, n_cols, n_feat = field.shape
    blocks = field.reshape(levels // 2, 2, n_rows // 6, 6, n_cols // 12, 12, n_feat)
    blocks = blocks.transpose(0, 2, 4, 1, 3, 5, 6)
    return blocks.reshape(levels // 2, n_rows // 6, n_cols // 12, 144, n_feat)

def from_windows(windows):
    lev_win, lat_win, lon_win, tok_win, n_feat = windows.shape
    blocks = windows.reshape(lev_win, lat_win, lon_win, 2, 6, 12, n_feat)
    blocks = blocks.transpose(0, 3, 1, 4, 2, 5, 6)
    return blocks.reshape(lev_win * 2, lat_win * 6, lon_win * 12, n_feat)

def window_mask(levels, lat_ids, shifted):
    places = jnp.arange(144, dtype=jnp.int32)
    level_off = places // 72
    row_off = places // 12 % 6
    level_of = 2 * jnp.arange(levels // 2, dtype=jnp.int32)[:, None] + level_off[None, :]
    region = jnp.where(level_of < levels - 2, 0, jnp.where(level_of < levels - 1, 1, 2))
    row_ids = lat_ids.reshape(-1, 6)[:, row_off]
    same_level = region[:, :, None] == region[:, None, :]
    same_row = row_ids[:, :, None] == row_ids[:, None, :]
    allowed = same_level[:, None] & same_row[None]
    if not shifted:
        allowed = jnp.ones_like(allowed)
    return allowed

def norm_rows(inner, gain):
    center = inner - lax.optimization_barrier(jnp.mean(inner, axis=-1, keepdims=True))
    spread = lax.optimization_barrier(jnp.mean(center * center, axis=-1, keepdims=True))
    return center * lax.rsqrt(spread + EPS) * gain

def matmul(left, right):
    return jnp.dot(left, right, preferred_element_type=jnp.float32)

def mat_tn(left, right):
    return lax.dot_general(left, right, (((0,), (0,)), ((), ())), preferred_element_type=jnp.float32)

def mat_nt(left, right):
    return lax.dot_general(left, right, (((1,), (1,)), ((), ())), preferred_element_type=jnp.float32)

def attend(qkv, bias, allowed):
    lev_win, lat_win, lon_win, n_tok, triple = qkv.shape
    n_feat = triple // 3
    unpacked = qkv.astype(jnp.float32).reshape(lev_win, lat_win, lon_win, n_tok, 3, HEADS, n_feat // HEADS)
    q_heads = unpacked[:, :, :, :, 0]
    k_heads = unpacked[:, :, :, :, 1]
    v_heads = unpacked[:, :, :, :, 2]
    scaling = (n_feat // HEADS) ** (-0.5)
    score_mat = jnp.einsum('abcshe,abcthe->abchst', q_heads, k_heads) * scaling + bias[:, :, None]
    score_mat = jnp.where(allowed[:, :, None, None], score_mat, NEGATIVE)
    row_max = lax.optimization_barrier(jnp.max(score_mat, axis=-1, keepdims=True))
    exp_scores = jnp.exp(score_mat - row_max)
    att_probs = exp_scores / lax.optimization_barrier(jnp.sum(exp_scores, axis=-1, keepdims=True))
    att_weights = att_probs.astype(jnp.bfloat16)
    attended = jnp.einsum('abchst,abcthe->abcshe', att_weights.astype(jnp.float32), v_heads)
    attended = attended.reshape(lev_win, lat_win, lon_win, n_tok, n_feat).astype(jnp.bfloat16)
    return (attended, (att_probs, att_weights, q_heads, k_heads, v_heads))

def attend_back(grad_att, att_saved):
    att_probs, att_weights, q_heads, k_heads, v_heads = att_saved
    lev_win, lat_win, lon_win, n_tok, n_feat = grad_att.shape
    grad_heads = grad_att.astype(jnp.float32).reshape(lev_win, lat_win, lon_win, n_tok, HEADS, n_feat // HEADS)
    scaling = (n_feat // HEADS) ** (-0.5)
    grad_probs = jnp.einsum('abcshe,abcthe->abchst', grad_heads, v_heads)
    grad_v = jnp.einsum('abchst,abcshe->abcthe', att_weights.astype(jnp.float32), grad_heads)
    grad_scores = att_probs * (grad_probs - lax.optimization_barrier(jnp.sum(grad_probs * att_probs, axis=-1, keepdims=True)))
    grad_q = jnp.einsum('abchst,abcthe->abcshe', grad_scores, k_heads) * scaling
    grad_k = jnp.einsum('abchst,abcshe->abcthe', grad_scores, q_heads) * scaling
    grad_qkv = jnp.stack([grad_q, grad_k, grad_v], axis=4)
    grad_qkv = grad_qkv.reshape(lev_win, lat_win, lon_win, n_tok, 3 * n_feat).astype(jnp.bfloat16)
    return (grad_qkv, lax.optimization_barrier(jnp.sum(grad_scores, axis=2)))

def block_forward(windows, weights, bias, allowed):
    w_qkv, w_proj, w_up, w_down, gains = weights
    win_shape = windows.shape
    n_feat = win_shape[-1]
    flat_in = windows.reshape(-1, n_feat)
    qkv = matmul(flat_in, w_qkv).astype(jnp.bfloat16).reshape(win_shape[:-1] + (3 * n_feat,))
    attended, att_saved = attend(qkv, bias, allowed)
    flat_att = attended.reshape(-1, n_feat)
    pre_norm = matmul(flat_att, w_proj)
    middle = (flat_in.astype(jnp.float32) + norm_rows(pre_norm, gains[0])).astype(jnp.bfloat16)
    up_out = matmul(middle, w_up)
    hidden = jax.nn.gelu(up_out, approximate=False).astype(jnp.bfloat16)
    down_out = matmul(hidden, w_down)
    result = (middle.astype(jnp.float32) + norm_rows(down_out, gains[1])).astype(jnp.bfloat16)
    saved = (flat_in, flat_att, pre_norm, middle, up_out, hidden, down_out, att_saved)
    return (result.reshape(win_shape), saved)

def block_backward(grad_res, saved, weights):
    w_qkv, w_proj, w_up, w_down, gains = weights
    flat_in, flat_att, pre_norm, middle, up_out, hidden, down_out, att_saved = saved
    win_shape = grad_res.shape
    n_feat = win_shape[-1]
    grad_out = grad_res.reshape(-1, n_feat).astype(jnp.float32)
    pullback = jax.vjp(lambda inner: norm_rows(inner, gains[1]), down_out)[1]
    grad_down_out = pullback(grad_out)[0].astype(jnp.bfloat16)
    d_down = mat_tn(hidden, grad_down_out)
    grad_hidden = mat_nt(grad_down_out, w_down)
    pullback = jax.vjp(lambda inner: jax.nn.gelu(inner, approximate=False), up_out)[1]
    grad_up_out = pullback(grad_hidden)[0].astype(jnp.bfloat16)
    d_up = mat_tn(middle, grad_up_out)
    grad_middle = grad_out + mat_nt(grad_up_out, w_up)
    pullback = jax.vjp(lambda inner: norm_rows(inner, gains[0]), pre_norm)[1]
    grad_pre = pullback(grad_middle)[0].astype(jnp.bfloat16)
    d_proj = mat_tn(flat_att, grad_pre)
    grad_att = mat_nt(grad_pre, w_proj).astype(jnp.bfloat16).reshape(win_shape)
    grad_qkv, grad_bias = attend_back(grad_att, att_saved)
    flat_grad = grad_qkv.reshape(-1, 3 * n_feat)
    d_qkv = mat_tn(flat_in, flat_grad)
    grad_in = (grad_middle + mat_nt(flat_grad, w_qkv)).astype(jnp.bfloat16).reshape(win_shape)
    return (grad_in, (d_qkv, d_proj, d_up, d_down), grad_bias)

def expand_bias(table_part, rel_index):
    return jnp.take(table_part, rel_index, axis=3)

def fold_bias(grad_bias, rel_index, n_pos):
    lead_shape = grad_bias.shape[:3]
    flat_grad = grad_bias.reshape(lead_shape + (-1,))
    empty = jnp.zeros(lead_shape + (n_pos,), jnp.float32)
    return empty.at[:, :, :, rel_index.reshape(-1)].add(flat_grad)

def reference(tokens, grad_mixed, w_qkv, w_proj, w_up, w_down, gains, bias_table, rel_index, mask_ids):
    levels, n_lat, n_lon, n_feat = tokens.shape
    n_bands = n_lat // 6
    n_pos = bias_table.shape[-1]
    weights_one = (w_qkv[0], w_proj[0], w_up[0], w_down[0], gains[0])
    weights_two = (w_qkv[1], w_proj[1], w_up[1], w_down[1], gains[1])

    def bands_of(field):
        return field.reshape(levels, n_bands, 6, n_lon, n_feat).transpose(1, 0, 2, 3, 4)

    def join_bands(stacked):
        return stacked.transpose(1, 0, 2, 3, 4).reshape(levels, n_lat, n_lon, n_feat)
    tables = jnp.moveaxis(bias_table, 2, 0)[:, :, :, None]
    band_ids = mask_ids.reshape(n_bands, 6)

    def first_forward(inputs):
        band, table_part, lat_ids = inputs
        allowed = window_mask(levels, lat_ids, False)
        bias = expand_bias(table_part[0], rel_index)
        return from_windows(block_forward(to_windows(band), weights_one, bias, allowed)[0])
    first = join_bands(lax.map(first_forward, (bands_of(tokens), tables, band_ids)))
    shifted = jnp.roll(first, (-1, -3, -6), axis=(0, 1, 2))
    grad_shifted = jnp.roll(grad_mixed, (-1, -3, -6), axis=(0, 1, 2))

    def make_pass(weights, which, shifted_flag):

        def one_pass(inputs):
            band, grad_band, table_part, lat_ids = inputs
            allowed = window_mask(levels, lat_ids, shifted_flag)
            bias = expand_bias(table_part[which], rel_index)
            result, saved = block_forward(to_windows(band), weights, bias, allowed)
            grad_in, partials, grad_bias = block_backward(to_windows(grad_band), saved, weights)
            return (from_windows(result), from_windows(grad_in), partials, fold_bias(grad_bias, rel_index, n_pos))
        return one_pass
    second, grad_second, parts_two, table_two = lax.map(make_pass(weights_two, 1, True), (bands_of(shifted), bands_of(grad_shifted), tables, band_ids))
    mixed = jnp.roll(join_bands(second), (1, 3, 6), axis=(0, 1, 2))
    grad_first = jnp.roll(join_bands(grad_second), (1, 3, 6), axis=(0, 1, 2))
    unused, grad_in, parts_one, table_one = lax.map(make_pass(weights_one, 0, False), (bands_of(tokens), bands_of(grad_first), tables, band_ids))
    grad_tokens = join_bands(grad_in)
    grads = [jnp.stack([lax.optimization_barrier(jnp.sum(part_one, axis=0)), lax.optimization_barrier(jnp.sum(part_two, axis=0))]) for part_one, part_two in zip(parts_one, parts_two)]
    table_grad = jnp.stack([table_g[:, :, 0].transpose(1, 0, 2, 3) for table_g in (table_one, table_two)])
    return (mixed, grad_tokens, grads[0], grads[1], grads[2], grads[3], table_grad)
```

```python
import functools

import jax
import jax.numpy as jnp
import numpy as np
from jax import lax
from jax.experimental import pallas as pl
from jax.experimental.pallas import tpu as pltpu
from jax.sharding import PartitionSpec as P

HEADS = 6
C = 192
TOK = 144
POS = 3312
EPS = 1e-05
NEGATIVE = -1e30
SCALE = 32 ** -0.5
BF = jnp.bfloat16
F32 = jnp.float32
MESH = pl.DeviceIdType.MESH
ROWS = 168
TAIL = 144
N_SEMS = 92


def index_rows():
    rows = np.full((16, 768), -1, np.int32)
    tok = np.arange(TOK)
    level, row, col = tok // 72, tok // 12 % 6, tok % 12
    place = 24 * row + 2 * col + level
    own = 18 * level + row % 3 * 6 + col % 6
    other = 18 * (1 - level) + row % 3 * 6 + col % 6
    low = 48 * (2 * (row // 3) + col // 6)
    high = 48 * (2 * (1 - row // 3) + 1 - col // 6)
    rows[0, place] = tok
    rows[1, tok] = place
    rows[2, tok] = high + own
    rows[3, low + other] = tok
    rows[4, tok] = low + own
    rows[5, high + other] = tok
    rows[6, high + other] = place
    rows[10, place] = high + own
    for piece in range(32):
        for i in range(18):
            rows[7, 24 * piece + i] = 18 * piece + i
        for i in range(6):
            rows[8, 24 * piece + 18 + i] = 6 * piece + i
            rows[9, 8 * piece + i] = 6 * piece + i
    return rows


def dot(a, b):
    return jnp.dot(a, b, preferred_element_type=F32)


def dot_nt(a, b):
    return lax.dot_general(a, b, (((1,), (1,)), ((), ())), preferred_element_type=F32)


def dot_tn(a, b):
    return lax.dot_general(a, b, (((0,), (0,)), ((), ())), preferred_element_type=F32)


def norm_parts(v):
    center = v - jnp.mean(v, axis=-1, keepdims=True)
    spread = jnp.mean(center * center, axis=-1, keepdims=True)
    inverse = lax.rsqrt(spread + EPS)
    return center * inverse, inverse


def norm_back(grad, unit, inverse):
    along = jnp.mean(grad * unit, axis=-1, keepdims=True)
    return inverse * (grad - jnp.mean(grad, axis=-1, keepdims=True) - unit * along)


def kernel(
    n_lat, n_lon,
    rel_hbm, table_hbm, const_hbm, tok_hbm, gmix_hbm, wqkv_hbm, wproj_hbm, gains_hbm, wup_hbm, wdown_hbm, ids_ref,
    mixed_ref, gtok_ref, wg_ref, tgrad_ref,
    rel_ref, table_ref, const_ref, tok_ref, gmix_ref, wqkv_ref, wproj_ref, gains_ref, wup_ref, wdown_ref, load_sem,
    x_ref, qkv_ref, qm_ref, s_ref, p_ref, att_ref, u1_ref, i1_ref, mid_ref, gp_ref, hid_ref, u2_ref, i2_ref,
    gup_ref, gam_ref, ds_ref, idx_ref, low_ref, oht_ref, tabf_ref, tab_ref, bias_ref, btail_ref, pk_ref, gall_ref, acc_ref,
    l_ref, r_ref, o1_ref, o3_ref,
    hs_ref, hr_ref,
    sb_ref, rc_ref, wa_ref, rx_ref, wc_ref, rz_ref, wd_ref, wl_ref,
    tb_ref, tr1_ref, t1_ref, tr2_ref, t2_ref, t3_ref, t4_ref,
    ssem, rsem,
):
    loads = [
        pltpu.make_async_copy(src, dst, load_sem.at[k])
        for k, (src, dst) in enumerate([
            (rel_hbm, rel_ref), (table_hbm, table_ref), (const_hbm, const_ref), (tok_hbm, tok_ref), (gmix_hbm, gmix_ref),
            (wqkv_hbm, wqkv_ref), (wproj_hbm, wproj_ref), (gains_hbm, gains_ref), (wup_hbm, wup_ref), (wdown_hbm, wdown_ref),
        ])
    ]
    for load in loads:
        load.start()
    ny, nz = n_lat // 2, n_lon // 4
    lat, lon = lax.axis_index("lat"), lax.axis_index("lon")
    y, xh = lat // 2, lat % 2
    z, xl, co = lon // 4, lon // 2 % 2, lon % 2
    x = xh * 2 + xl
    lon_pair = [
        (z * 4 + ((xl + (k >> 1)) % 2) * 2 + (co + (k & 1)) % 2, (xl + (k >> 1)) % 2, (co + (k & 1)) % 2)
        for k in range(4)
    ]
    ahead = [((lat + n_lat - a) % n_lat, (lon + n_lon - b) % n_lon) for a in (0, 1) for b in (0, 1)]
    back = [((lat + a) % n_lat, (lon + b) % n_lon) for a in (0, 1) for b in (0, 1)]
    z_lons = [(z + k) % nz * 4 + xl * 2 + co for k in range(nz)]

    greeted = [((lat + k) % n_lat, lon) for k in range(1, n_lat)]
    greeted += [(lat, z_lons[k]) for k in range(1, nz)]
    greeted += [(lat, lon_pair[k][0]) for k in (1, 3)]
    greeted += [((lat + k) % n_lat, lon_pair[2][0]) for k in range(n_lat)]
    greeted += [ahead[1], ahead[3], back[1], back[3]]
    barrier = pltpu.get_barrier_semaphore()
    for device in greeted:
        pl.semaphore_signal(barrier, inc=1, device_id=device, device_id_type=MESH)

    sems = iter(range(N_SEMS))
    sent = []

    def push(src, dst, device):
        k = next(sems)
        copy = pltpu.make_async_remote_copy(
            src_ref=src, dst_ref=dst, send_sem=ssem.at[k], recv_sem=rsem.at[k], device_id=device, device_id_type=MESH
        )
        copy.start()
        sent.append(copy)
        return copy

    def arrive(copies):
        for copy in copies:
            copy.wait_recv()

    def onehot(n_rows, n_lanes, which):
        place = lax.broadcasted_iota(jnp.int32, (n_rows, n_lanes), 0)
        return jnp.where(place == const_ref[which : which + 1, :n_lanes], 1.0, 0.0).astype(BF)

    def moved(matrix, value):
        return dot(matrix, value).astype(BF)

    lane = lax.broadcasted_iota(jnp.int32, (1, C), 1)
    head_lanes = [(lane >= 32 * h) & (lane < 32 * h + 32) for h in range(HEADS)]

    def of_head(value, h):
        return jnp.where(head_lanes[h], value, jnp.zeros_like(value))

    def pack_tail(value, h):
        pk_ref[h, 0:TOK, 0:16] = value
        total = pk_ref[h, pl.ds(0, 24, stride=8), :]
        for j in range(1, 8):
            total = total + pltpu.roll(pk_ref[h, pl.ds(j, 24, stride=8), :], 16 * j, 1)
        return total

    def unpack_tail(value, k):
        for j in range(8):
            rolled = pltpu.roll(value, (128 - 16 * j) % 128, 1)
            btail_ref[k, pl.ds(j, 24, stride=8), :] = rolled

    def gather_biases():
        place = lax.broadcasted_iota(jnp.int32, (256, 128), 0).astype(BF)
        one, zero = jnp.ones((256, 128), BF), jnp.zeros((256, 128), BF)

        def step(i, carry):
            index = idx_ref[pl.ds(pl.multiple_of(i * 8, 8), 8), :]
            low, high = (index & 255).astype(F32), index >> 8
            picks = []
            for r in range(8):
                row = jnp.broadcast_to(low[r : r + 1, :], (16, 128)).astype(BF)
                picks.append(jnp.where(place == jnp.concatenate([row] * 16, axis=0), one, zero))
            rows = dot(tab_ref[...], jnp.concatenate(picks, axis=1))
            for r in range(8):
                high_row = jnp.broadcast_to(high[r : r + 1, :], (16, 128))
                found = jnp.zeros((16, 128), F32)
                for part in range(13):
                    coarse = rows[16 * part : 16 * part + 16, 128 * r : 128 * r + 128]
                    fine = rows[208 + 16 * part : 224 + 16 * part, 128 * r : 128 * r + 128]
                    found = jnp.where(high_row == part, coarse + fine, found)
                bias_ref[pl.ds(pl.multiple_of(i * 128 + r * 16, 16), 16), :] = found
            return carry

        lax.fori_loop(0, ROWS // 8, step, 0)
        for b in range(2):
            for h in range(HEADS):
                unpack_tail(bias_ref[pl.ds(16 * TAIL + 8 * b + h, 24, stride=16), :], 6 * b + h)

    def expand_index():
        place = lax.broadcasted_iota(jnp.int32, (128, 256), 1).astype(BF)
        one, zero = jnp.ones((128, 256), BF), jnp.zeros((128, 256), BF)

        def step(i, carry):
            block = low_ref[i]
            for r in range(8):
                span = pl.ds(pl.multiple_of(i * 1024 + r * 128, 128), 128)
                column = jnp.broadcast_to(block[:, r : r + 1], (128, 128)).astype(BF)
                oht_ref[span, :] = jnp.where(place == jnp.concatenate([column] * 2, axis=1), one, zero)
            return carry

        lax.fori_loop(0, ROWS // 8, step, 0)

    def fold_tables():
        acc_ref[...] = jnp.zeros_like(acc_ref)

        def step(i, carry):
            high = idx_ref[pl.ds(pl.multiple_of(i * 8, 8), 8), :] >> 8
            left = [[] for _ in range(26)]
            for r in range(8):
                high_row = jnp.broadcast_to(high[r : r + 1, :], (8, 128))
                for b in range(2):
                    grads = gall_ref[b, pl.ds(pl.multiple_of(i * 64 + r * 8, 8), 8), :]
                    for part in range(13):
                        left[13 * b + part].append(jnp.where(high_row == part, grads, 0.0))
            left = jnp.concatenate([jnp.concatenate(rows, axis=1) for rows in left], axis=0).astype(BF)
            acc_ref[...] += dot(left, oht_ref[pl.ds(pl.multiple_of(i * 1024, 1024), 1024), :])
            return carry

        lax.fori_loop(0, ROWS // 8, step, 0)

    def region_codes(place):
        code = jnp.zeros_like(place)
        for part in range(12):
            value = ids_ref[part % 6] + 64 * (part // 6)
            code = jnp.where(place >= 12 * part, value, code)
        return code

    def forward(b):
        tokens = x_ref[b]
        qkv_ref[b] = dot(tokens, wqkv_ref[b]).astype(BF)
        q, k, v = (qkv_ref[b, :, C * i : C * i + C] for i in range(3))
        for h in range(HEADS):
            qm_ref[b, TOK * h : TOK * h + TOK, :] = of_head(q, h)
        s_ref[...] = dot_nt(qm_ref[b], k)
        if b == 1:
            codes_s = region_codes(lax.broadcasted_iota(jnp.int32, (TOK, 1), 0))
            codes_t = region_codes(lax.broadcasted_iota(jnp.int32, (1, TOK), 1))
            allowed = codes_s == codes_t
        for h in range(HEADS):
            span = pl.ds(TOK * h, TOK)
            main = bias_ref[pl.ds(8 * b + h, TOK, stride=16), :]
            bias = jnp.concatenate([main, btail_ref[6 * b + h, 0:TOK, 0:16]], axis=1)
            scores = s_ref[span, :] * SCALE + bias
            if b == 1:
                scores = jnp.where(allowed, scores, NEGATIVE)
            powers = jnp.exp(scores - jnp.max(scores, axis=-1, keepdims=True))
            probs = powers * (1.0 / jnp.sum(powers, axis=-1, keepdims=True))
            p_ref[b, span, :] = probs.astype(BF)
        attended = jnp.zeros((TOK, C), F32)
        for h in range(HEADS):
            attended = jnp.where(head_lanes[h], dot(p_ref[b, TOK * h : TOK * h + TOK, :], v), attended)
        attended = attended.astype(BF)
        att_ref[b] = attended
        unit, inverse = norm_parts(dot(attended, wproj_ref[b]))
        u1_ref[b], i1_ref[b] = unit, inverse
        middle = (tokens.astype(F32) + unit * gains_ref[b, 0:1, :]).astype(BF)
        mid_ref[b] = middle
        for part in range(3):
            cols = pl.ds(256 * part, 256)
            up = dot(middle, wup_ref[b, :, cols])
            phi = 0.5 + 0.5 * lax.erf(up * (0.5**0.5))
            hid_ref[b, :, cols] = (up * phi).astype(BF)
            gp_ref[b, :, cols] = phi + up * (0.3989422804014327 * jnp.exp(-0.5 * up * up))
        unit, inverse = norm_parts(dot_nt(hid_ref[b], wdown_ref[b]))
        u2_ref[b], i2_ref[b] = unit, inverse
        return (middle.astype(F32) + unit * gains_ref[b, 1:2, :]).astype(BF)

    def backward(b, grad, between):
        grad = grad.astype(F32)
        grad_down = norm_back(grad * gains_ref[b, 1:2, :], u2_ref[b], i2_ref[b]).astype(BF)
        for part in range(3):
            cols = pl.ds(256 * part, 256)
            grad_hidden = dot(grad_down, wdown_ref[b, :, cols])
            gup_ref[b, :, cols] = (grad_hidden * gp_ref[b, :, cols]).astype(BF)
        grad_middle = grad + dot_nt(gup_ref[b], wup_ref[b])
        between()
        grad_pre = norm_back(grad_middle * gains_ref[b, 0:1, :], u1_ref[b], i1_ref[b]).astype(BF)
        grad_att = dot_nt(grad_pre, wproj_ref[b]).astype(BF)
        for h in range(HEADS):
            gam_ref[TOK * h : TOK * h + TOK, :] = of_head(grad_att, h)
        q, k, v = (qkv_ref[b, :, C * i : C * i + C] for i in range(3))
        s_ref[...] = dot_nt(gam_ref[...], v)
        between()
        for h in range(HEADS):
            span = pl.ds(TOK * h, TOK)
            probs = p_ref[b, span, :].astype(F32)
            grad_probs = s_ref[span, :]
            grad_scores = probs * (grad_probs - jnp.sum(grad_probs * probs, axis=-1, keepdims=True))
            ds_ref[span, :] = grad_scores.astype(BF)
            gall_ref[b, pl.ds(h, TOK, stride=8), :] = grad_scores[:, 0:128]
            gall_ref[b, pl.ds(8 * TAIL + h, 24, stride=8), :] = pack_tail(grad_scores[:, 128:TOK], h)
        between()
        grad_q = jnp.zeros((TOK, C), F32)
        for h in range(HEADS):
            grad_q = jnp.where(head_lanes[h], dot(ds_ref[TOK * h : TOK * h + TOK, :], k), grad_q)
        grad_k = dot_tn(ds_ref[...], qm_ref[b])
        grad_v = dot_tn(p_ref[b], gam_ref[...])
        grad_qkv = jnp.concatenate([grad_q * SCALE, grad_k * SCALE, grad_v], axis=1).astype(BF)
        grad_in = (grad_middle + dot_nt(grad_qkv, wqkv_ref[b])).astype(BF)
        return grad_in, grad_down, grad_pre, grad_qkv

    def weight_grads(b, grad_down, grad_pre, grad_qkv):
        l_ref[0:TOK, :] = moved(grad_qkv, onehot(3 * C, 768, 7))
        l_ref[TOK : 2 * TOK, :] = moved(grad_pre, onehot(C, 768, 8))
        l_ref[2 * TOK : 3 * TOK, :] = gup_ref[b]
        tokens, middle = x_ref[b], mid_ref[b]
        r_ref[0:TOK, 0:128] = tokens[:, 0:128]
        r_ref[0:TOK, 256:320] = tokens[:, 128:C]
        r_ref[TOK : 2 * TOK, 0:128] = att_ref[b, :, 0:128]
        r_ref[TOK : 2 * TOK, 256:320] = att_ref[b, :, 128:C]
        r_ref[2 * TOK : 3 * TOK, 128:256] = middle[:, 0:128]
        r_ref[2 * TOK : 3 * TOK, 320:384] = middle[:, 128:C]
        o1_ref[...] = dot_tn(l_ref[...], r_ref[...])
        o3_ref[...] = dot_tn(moved(grad_down, onehot(C, 256, 9)), hid_ref[b])
        rows = 128 // n_lat
        for piece in range(32):
            units = [o1_ref[24 * piece + 8 * i : 24 * piece + 8 * i + 8, 128 * m : 128 * m + 128] for m in range(3) for i in range(3)]
            units += [o3_ref[8 * piece : 8 * piece + 8, 128 * i : 128 * i + 128] for i in range(6)]
            units += [jnp.zeros((8, 128), F32)]
            for tile in range(8):
                pair = jnp.concatenate([units[2 * tile], units[2 * tile + 1]], axis=0).astype(BF)
                at, off = 16 * tile // rows, 16 * tile % rows
                across = at % 2 * 2 + piece // 2 % 2
                sb_ref[b, piece % 2, at // 2, across, piece // 4, off : off + 16, :] = pair

    class Sum:
        def __init__(self, b):
            self.b = b
            self.copies = []
            self.steps = [self.core, self.along_xy, self.along_z, self.share, self.done]

        def next(self):
            if self.steps:
                self.steps.pop(0)()

        def core(self):
            self.copies = [push(sb_ref.at[self.b, 1 - co], rc_ref.at[self.b], (lat, lon + 1 - 2 * co))]

        def along_xy(self):
            b = self.b
            arrive(self.copies)
            wa_ref[b] = (sb_ref[b, co].astype(F32) + rc_ref[b].astype(F32)).astype(BF)
            self.copies = []
            for k in range(1, 4 * ny):
                its_y, its_x = (y + k // 4) % ny, (x + k % 4) % 4
                device = (its_y * 2 + its_x // 2, z * 4 + its_x % 2 * 2 + co)
                self.copies.append(push(wa_ref.at[b, its_y, its_x], rx_ref.at[b, k - 1], device))

        def along_z(self):
            b = self.b
            arrive(self.copies)
            total = wa_ref[b, y, x].astype(F32)
            for k in range(4 * ny - 1):
                total = total + rx_ref[b, k].astype(F32)
            wc_ref[b] = total.astype(BF)
            self.copies = []
            for k in range(1, nz):
                self.copies.append(push(wc_ref.at[b, (z + k) % nz], rz_ref.at[b, k - 1], (lat, z_lons[k])))

        def share(self):
            b = self.b
            arrive(self.copies)
            total = wc_ref[b, z].astype(F32)
            for k in range(nz - 1):
                total = total + rz_ref[b, k].astype(F32)
            wd_ref[b] = total.astype(BF)
            self.copies = []
            for k in range(1, n_lat):
                self.copies.append(push(wd_ref.at[b], wl_ref.at[b, lat], ((lat + k) % n_lat, lon)))
            wl_ref[b, lat] = wd_ref[b]

        def done(self):
            arrive(self.copies)
            wg_ref[self.b] = wl_ref[self.b]

    class TableSum:
        def __init__(self):
            self.copies = []
            self.steps = [self.pair, self.along_z, self.share_z, self.share_pair, self.done]

        def next(self):
            if self.steps:
                self.steps.pop(0)()

        def pair(self):
            for part in range(26):
                row, lanes = 8 * (part // 2), slice(128 * (part % 2), 128 * (part % 2) + 128)
                both = jnp.concatenate([acc_ref[row : row + 8, lanes], acc_ref[104 + row : 112 + row, lanes]], axis=0)
                tb_ref[part // 16, part // 8 % 2, part % 8] = both.astype(BF)
            for part in range(26, 32):
                tb_ref[part // 16, part // 8 % 2, part % 8] = jnp.zeros((16, 128), BF)
            for k in range(1, 4):
                device, its_xl, its_co = lon_pair[k]
                self.copies.append(push(tb_ref.at[its_co, its_xl], tr1_ref.at[k - 1], (lat, device)))

        def along_z(self):
            arrive(self.copies)
            total = tb_ref[co, xl].astype(F32)
            for k in range(3):
                total = total + tr1_ref[k].astype(F32)
            t1_ref[...] = total.astype(BF)
            self.copies = []
            for k in range(1, nz):
                self.copies.append(push(t1_ref.at[(z + k) % nz], tr2_ref.at[k - 1], (lat, z_lons[k])))

        def share_z(self):
            arrive(self.copies)
            total = t1_ref[z].astype(F32)
            for k in range(nz - 1):
                total = total + tr2_ref[k].astype(F32)
            t2_ref[...] = total.astype(BF)
            self.copies = []
            for k in range(1, nz):
                self.copies.append(push(t2_ref, t3_ref.at[z], (lat, z_lons[k])))
            t3_ref[z] = t2_ref[...]

        def share_pair(self):
            arrive(self.copies)
            self.copies = []
            for k in range(1, 4):
                self.copies.append(push(t3_ref, t4_ref.at[co, xl], (lat, lon_pair[k][0])))
            t4_ref[co, xl] = t3_ref[...]

        def done(self):
            arrive(self.copies)
            tgrad_ref[...] = t4_ref[...]

    def send_quarters(which, devices):
        copies = []
        for quarter in range(1, 4):
            copies.append(push(hs_ref.at[which, quarter], hr_ref.at[which, quarter], devices[quarter]))
        hr_ref[which, 0] = hs_ref[which, 0]
        return copies

    pk_ref[...] = jnp.zeros_like(pk_ref)
    gall_ref[...] = jnp.zeros_like(gall_ref)
    r_ref[...] = jnp.zeros_like(r_ref)
    loads[0].wait()
    idx_ref[0:TOK, :] = rel_ref[:, 0:128]
    idx_ref[TAIL:ROWS, :] = pack_tail(rel_ref[:, 128:TOK].astype(F32), 0).astype(jnp.int32)
    idx_ref[TAIL + 18 : ROWS, :] = jnp.full((ROWS - TAIL - 18, 128), -1, jnp.int32)
    low = (idx_ref[...] & 255).astype(F32).T
    for i in range(ROWS // 8):
        low_ref[i] = low[:, 8 * i : 8 * i + 8]
    loads[1].wait()
    tabf_ref[...] = jnp.zeros_like(tabf_ref)
    for b in range(2):
        for part in range(13):
            width = min(256, POS - 256 * part)
            tabf_ref[16 * part + 8 * b : 16 * part + 8 * b + 6, 0:width] = table_ref[
                6 * b : 6 * b + 6, 0, 256 * part : 256 * part + width
            ]
    table = tabf_ref[...]
    coarse = table.astype(BF)
    tab_ref[0:208, :] = coarse
    tab_ref[208:416, :] = (table - coarse.astype(F32)).astype(BF)
    gather_biases()
    for load in loads[2:]:
        load.wait()
    x_ref[0] = moved(onehot(TOK, TOK, 0), tok_ref[...].reshape(TOK, C))
    hs_ref[0] = moved(onehot(192, TOK, 10), gmix_ref[...].reshape(TOK, C)).reshape(4, 48, C)

    first = forward(0)
    hs_ref[1] = moved(onehot(192, TOK, 2), first).reshape(4, 48, C)
    pl.semaphore_wait(barrier, len(greeted))
    copies_x = send_quarters(1, ahead)
    copies_g = send_quarters(0, ahead)
    expand_index()
    arrive(copies_x)
    arrive(copies_g)
    come = onehot(TOK, 192, 3)
    x_ref[1] = moved(come, hr_ref[1].reshape(192, C))
    grad_shifted = moved(come, hr_ref[0].reshape(192, C))

    second = forward(1)
    hs_ref[2] = moved(onehot(192, TOK, 4), second).reshape(4, 48, C)
    grad_second, *rest = backward(1, grad_shifted, lambda: None)
    hs_ref[3] = moved(onehot(192, TOK, 4), grad_second).reshape(4, 48, C)
    copies_s = send_quarters(3, back)
    copies_m = send_quarters(2, back)
    weight_grads(1, *rest)
    sum_two = Sum(1)
    sum_two.next()

    arrive(copies_s)
    grad_first = moved(onehot(TOK, 192, 5), hr_ref[3].reshape(192, C))
    grad_in, *rest = backward(0, grad_first, sum_two.next)
    weight_grads(0, *rest)
    sum_one = Sum(0)
    sum_one.next()
    sum_one.next()
    fold_tables()
    sum_table = TableSum()
    sum_table.next()
    arrive(copies_m)
    mixed_ref[...] = moved(onehot(TOK, 192, 6), hr_ref[2].reshape(192, C)).reshape(72, 2, C)
    gtok_ref[...] = moved(onehot(TOK, TOK, 1), grad_in).reshape(72, 2, C)
    for _ in range(5):
        sum_one.next()
        sum_table.next()
        sum_two.next()
    for copy in sent:
        copy.wait_send()


def finish(mixed_in, gtok_in, wg_in, table_in, mixed_ref, gtok_ref, qkv_ref, proj_ref, up_ref, down_ref, table_ref):
    mixed_ref[...] = mixed_in[...]
    gtok_ref[...] = gtok_in[...]
    for b in range(2):
        rows = wg_in[b].reshape(128, 128).astype(F32)
        qkv_ref[:, b, 0:128] = rows[0:18, :]
        qkv_ref[:, b, 128:C] = rows[48:66, 0:64]
        proj_ref[:, b, 0:128] = rows[18:24, :]
        proj_ref[:, b, 128:C] = rows[66:72, 0:64]
        up_ref[b, :, 0:128] = rows[24:48, :]
        up_ref[b, :, 128:C] = rows[48:72, 64:128]
        for i in range(6):
            down_ref[:, b, 128 * i : 128 * i + 128] = rows[72 + 8 * i : 78 + 8 * i, :]
    for part in range(26):
        tile = table_in[part // 16, part // 8 % 2, part % 8].astype(F32)
        width = min(128, POS - 128 * part)
        for b in range(2):
            table_ref[6 * b : 6 * b + 6, 0, 128 * part : 128 * part + width] = tile[8 * b : 8 * b + 6, 0:width]


def per_device(tokens, grad_mixed, w_qkv, w_proj, w_up, w_down, gains, bias_table, rel_index, mask_ids):
    n_lat, n_lon = lax.axis_size("lat"), lax.axis_size("lon")
    ny, nz, rows = n_lat // 2, n_lon // 4, 128 // n_lat
    vmem = pl.BlockSpec(memory_space=pltpu.VMEM)
    smem = pl.BlockSpec(memory_space=pltpu.SMEM)

    def buf(*shape, dtype=BF):
        return pltpu.VMEM(shape, dtype)

    scratch = [
        buf(TOK, TOK, dtype=jnp.int32), buf(12, 1, POS, dtype=F32), buf(16, 768, dtype=jnp.int32),
        buf(72, 2, C), buf(72, 2, C), buf(2, C, 3 * C), buf(2, C, C), buf(2, 2, C, dtype=F32), buf(2, C, 768), buf(2, C, 768),
        pltpu.SemaphoreType.DMA((10,)),
        buf(2, TOK, C), buf(2, TOK, 3 * C), buf(2, 6 * TOK, C), buf(6 * TOK, TOK, dtype=F32),
        buf(2, 6 * TOK, TOK), buf(2, TOK, C), buf(2, TOK, C, dtype=F32), buf(2, TOK, 1, dtype=F32), buf(2, TOK, C),
        buf(2, TOK, 768, dtype=F32), buf(2, TOK, 768), buf(2, TOK, C, dtype=F32), buf(2, TOK, 1, dtype=F32),
        buf(2, TOK, 768), buf(6 * TOK, C), buf(6 * TOK, TOK),
        buf(ROWS, 128, dtype=jnp.int32), buf(ROWS // 8, 128, 8, dtype=F32), buf(128 * ROWS, 256), buf(208, 256, dtype=F32),
        buf(416, 256), buf(16 * ROWS, 128, dtype=F32), buf(12, 192, 128, dtype=F32), buf(6, 192, 128, dtype=F32),
        buf(2, 8 * ROWS, 128, dtype=F32), buf(208, 256, dtype=F32),
        buf(3 * TOK, 768), buf(3 * TOK, 384), buf(768, 384, dtype=F32), buf(256, 768, dtype=F32),
        buf(4, 4, 48, C), buf(4, 4, 48, C),
        buf(2, 2, ny, 4, nz, rows, 128), buf(2, ny, 4, nz, rows, 128), buf(2, ny, 4, nz, rows, 128),
        buf(2, 4 * ny - 1, nz, rows, 128),
        buf(2, nz, rows, 128), buf(2, nz - 1, rows, 128), buf(2, rows, 128), buf(2, n_lat, rows, 128),
        buf(2, 2, 8, 16, 128), buf(3, 8, 16, 128), buf(8, 16, 128), buf(7, 16, 128), buf(16, 128),
        buf(8, 16, 128), buf(2, 2, 8, 16, 128),
        pltpu.SemaphoreType.DMA((N_SEMS,)), pltpu.SemaphoreType.DMA((N_SEMS,)),
    ]
    results = pl.pallas_call(
        functools.partial(kernel, n_lat, n_lon),
        out_shape=(
            jax.ShapeDtypeStruct((72, 2, C), BF),
            jax.ShapeDtypeStruct((72, 2, C), BF),
            jax.ShapeDtypeStruct((2, n_lat, rows, 128), BF),
            jax.ShapeDtypeStruct((2, 2, 8, 16, 128), BF),
        ),
        in_specs=[pl.BlockSpec(memory_space=pltpu.HBM)] * 10 + [smem],
        out_specs=[vmem] * 4,
        scratch_shapes=scratch,
        compiler_params=pltpu.CompilerParams(
            collective_id=0, has_side_effects=True, vmem_limit_bytes=60 * 1024 * 1024
        ),
    )(
        rel_index,
        bias_table.reshape(12, 1, POS),
        jnp.asarray(index_rows()),
        tokens.transpose(1, 2, 0, 3).reshape(72, 2, C),
        grad_mixed.transpose(1, 2, 0, 3).reshape(72, 2, C),
        w_qkv, w_proj, gains, w_up, w_down.transpose(0, 2, 1),
        mask_ids,
    )
    mixed, grad_tokens, qkv, proj, up, down, table = pl.pallas_call(
        finish,
        out_shape=(
            jax.ShapeDtypeStruct((72, 2, C), BF),
            jax.ShapeDtypeStruct((72, 2, C), BF),
            jax.ShapeDtypeStruct((18, 2, C), F32),
            jax.ShapeDtypeStruct((6, 2, C), F32),
            jax.ShapeDtypeStruct((2, 24, C), F32),
            jax.ShapeDtypeStruct((6, 2, 768), F32),
            jax.ShapeDtypeStruct((12, 1, POS), F32),
        ),
        in_specs=[vmem] * 4,
        out_specs=[vmem] * 7,
        compiler_params=pltpu.CompilerParams(vmem_limit_bytes=60 * 1024 * 1024),
    )(*results)

    def field(value):
        return value.reshape(6, 12, 2, C).transpose(2, 0, 1, 3)

    return (
        field(mixed),
        field(grad_tokens),
        qkv.transpose(1, 2, 0),
        proj.transpose(1, 2, 0),
        up.transpose(0, 2, 1),
        down.transpose(1, 2, 0),
        table.reshape(2, 1, 1, 6, POS),
    )


def solution(mesh):
    field = P(None, "lat", "lon", None)
    table = P(None, None, "lat", None, None)
    in_specs = (field, field, P(), P(), P(), P(), P(), table, P(), P("lat"))
    columns = P(None, None, "lon")
    out_specs = (field, field, columns, columns, columns, columns, table)
    return jax.shard_map(per_device, mesh=mesh, in_specs=in_specs, out_specs=out_specs, check_vma=False)
```

```python
import functools

import jax
import jax.numpy as jnp
import numpy as np
from jax import lax
from jax.experimental import pallas as pl
from jax.experimental.pallas import tpu as pltpu
from jax.sharding import PartitionSpec as P

HEADS = 6
C = 192
TOK = 144
POS = 3312
EPS = 1e-05
NEGATIVE = -1e30
SCALE = 32 ** -0.5
BF = jnp.bfloat16
F32 = jnp.float32
MESH = pl.DeviceIdType.MESH
ROWS = 168
TAIL = 144
N_SEMS = 92


def index_rows():
    rows = np.full((16, 768), -1, np.int32)
    tok = np.arange(TOK)
    level, row, col = tok // 72, tok // 12 % 6, tok % 12
    place = 24 * row + 2 * col + level
    own = 18 * level + row % 3 * 6 + col % 6
    other = 18 * (1 - level) + row % 3 * 6 + col % 6
    low = 48 * (2 * (row // 3) + col // 6)
    high = 48 * (2 * (1 - row // 3) + 1 - col // 6)
    rows[0, place] = tok
    rows[1, tok] = place
    rows[2, tok] = high + own
    rows[3, low + other] = tok
    rows[4, tok] = low + own
    rows[5, high + other] = tok
    rows[6, high + other] = place
    rows[10, place] = high + own
    return rows


def permutations():
    qkv = np.zeros((3 * C, 768), np.float32)
    proj = np.zeros((C, 768), np.float32)
    down = np.zeros((C, 256), np.float32)
    for piece in range(32):
        for i in range(18):
            qkv[18 * piece + i, 24 * piece + i] = 1
        for i in range(6):
            proj[6 * piece + i, 24 * piece + 18 + i] = 1
            down[6 * piece + i, 8 * piece + i] = 1
    return tuple(jnp.asarray(matrix, BF) for matrix in (qkv, proj, down))


def dot(a, b):
    return jnp.dot(a, b, preferred_element_type=F32)


def dot_nt(a, b):
    return lax.dot_general(a, b, (((1,), (1,)), ((), ())), preferred_element_type=F32)


def dot_tn(a, b):
    return lax.dot_general(a, b, (((0,), (0,)), ((), ())), preferred_element_type=F32)


def norm_parts(v):
    center = v - jnp.mean(v, axis=-1, keepdims=True)
    spread = jnp.mean(center * center, axis=-1, keepdims=True)
    inverse = lax.rsqrt(spread + EPS)
    return center * inverse, inverse


def norm_back(grad, unit, inverse):
    along = jnp.mean(grad * unit, axis=-1, keepdims=True)
    return inverse * (grad - jnp.mean(grad, axis=-1, keepdims=True) - unit * along)


def kernel(
    n_lat, n_lon,
    rel_hbm, table_hbm, const_hbm, tok_hbm, gmix_hbm, wqkv_hbm, wproj_hbm, gains_hbm, wup_hbm, wdown_hbm, pq_hbm, pp_hbm, pd_hbm, ids_ref,
    mixed_ref, gtok_ref, wg_ref, tgrad_ref,
    rel_ref, table_ref, const_ref, tok_ref, gmix_ref, wqkv_ref, wproj_ref, gains_ref, wup_ref, wdown_ref, pq_ref, pp_ref, pd_ref, load_sem,
    x_ref, qkv_ref, qm_ref, s_ref, p_ref, att_ref, u1_ref, i1_ref, mid_ref, gp_ref, hid_ref, u2_ref, i2_ref,
    gup_ref, gam_ref, ds_ref, idx_ref, low_ref, oht_ref, tabf_ref, tab_ref, bias_ref, btail_ref, pk_ref, gall_ref, acc_ref,
    l_ref, r_ref, o1_ref, o3_ref,
    hs_ref, hr_ref,
    sb_ref, rc_ref, wa_ref, rx_ref, wc_ref, rz_ref, wd_ref, wl_ref,
    tb_ref, tr1_ref, t1_ref, tr2_ref, t2_ref, t3_ref, t4_ref,
    ssem, rsem,
):
    loads = [
        pltpu.make_async_copy(src, dst, load_sem.at[k])
        for k, (src, dst) in enumerate([
            (rel_hbm, rel_ref), (table_hbm, table_ref), (const_hbm, const_ref), (tok_hbm, tok_ref), (gmix_hbm, gmix_ref),
            (wqkv_hbm, wqkv_ref), (wproj_hbm, wproj_ref), (gains_hbm, gains_ref), (wup_hbm, wup_ref), (wdown_hbm, wdown_ref),
            (pq_hbm, pq_ref), (pp_hbm, pp_ref), (pd_hbm, pd_ref),
        ])
    ]
    for load in loads:
        load.start()
    ny, nz = n_lat // 2, n_lon // 4
    lat, lon = lax.axis_index("lat"), lax.axis_index("lon")
    y, xh = lat // 2, lat % 2
    z, xl, co = lon // 4, lon // 2 % 2, lon % 2
    x = xh * 2 + xl
    lon_pair = [
        (z * 4 + ((xl + (k >> 1)) % 2) * 2 + (co + (k & 1)) % 2, (xl + (k >> 1)) % 2, (co + (k & 1)) % 2)
        for k in range(4)
    ]
    ahead = [((lat + n_lat - a) % n_lat, (lon + n_lon - b) % n_lon) for a in (0, 1) for b in (0, 1)]
    back = [((lat + a) % n_lat, (lon + b) % n_lon) for a in (0, 1) for b in (0, 1)]
    z_lons = [(z + k) % nz * 4 + xl * 2 + co for k in range(nz)]

    greeted = [((lat + k) % n_lat, lon) for k in range(1, n_lat)]
    greeted += [(lat, z_lons[k]) for k in range(1, nz)]
    greeted += [(lat, lon_pair[k][0]) for k in (1, 3)]
    greeted += [((lat + k) % n_lat, lon_pair[2][0]) for k in range(n_lat)]
    greeted += [ahead[1], ahead[3], back[1], back[3]]
    barrier = pltpu.get_barrier_semaphore()
    for device in greeted:
        pl.semaphore_signal(barrier, inc=1, device_id=device, device_id_type=MESH)

    sems = iter(range(N_SEMS))
    sent = []

    def push(src, dst, device):
        k = next(sems)
        copy = pltpu.make_async_remote_copy(
            src_ref=src, dst_ref=dst, send_sem=ssem.at[k], recv_sem=rsem.at[k], device_id=device, device_id_type=MESH
        )
        copy.start()
        sent.append(copy)
        return copy

    def arrive(copies):
        for copy in copies:
            copy.wait_recv()

    def onehot(n_rows, n_lanes, which):
        place = lax.broadcasted_iota(jnp.int32, (n_rows, n_lanes), 0)
        return jnp.where(place == const_ref[which : which + 1, :n_lanes], 1.0, 0.0).astype(BF)

    def moved(matrix, value):
        return dot(matrix, value).astype(BF)

    lane = lax.broadcasted_iota(jnp.int32, (1, C), 1)
    head_lanes = [(lane >= 32 * h) & (lane < 32 * h + 32) for h in range(HEADS)]

    def of_head(value, h):
        return jnp.where(head_lanes[h], value, jnp.zeros_like(value))

    def pack_tail(value, h):
        pk_ref[h, 0:TOK, 0:16] = value
        total = pk_ref[h, pl.ds(0, 24, stride=8), :]
        for j in range(1, 8):
            total = total + pltpu.roll(pk_ref[h, pl.ds(j, 24, stride=8), :], 16 * j, 1)
        return total

    def unpack_tail(value, k):
        for j in range(8):
            rolled = pltpu.roll(value, (128 - 16 * j) % 128, 1)
            btail_ref[k, pl.ds(j, 24, stride=8), :] = rolled

    def gather_bias(b):
        place = lax.broadcasted_iota(jnp.int32, (256, 128), 0).astype(BF)
        place_t = lax.broadcasted_iota(jnp.int32, (128, 256), 1).astype(BF)
        one, zero = jnp.ones((256, 128), BF), jnp.zeros((256, 128), BF)
        one_t, zero_t = jnp.ones((128, 256), BF), jnp.zeros((128, 256), BF)

        def step(i, carry):
            index = idx_ref[pl.ds(pl.multiple_of(i * 8, 8), 8), :]
            low, high = (index & 255).astype(F32), index >> 8
            picks = []
            for r in range(8):
                row = jnp.broadcast_to(low[r : r + 1, :], (16, 128)).astype(BF)
                picks.append(jnp.where(place == jnp.concatenate([row] * 16, axis=0), one, zero))
            rows = dot(tab_ref[b], jnp.concatenate(picks, axis=1))
            for r in range(8):
                high_row = jnp.broadcast_to(high[r : r + 1, :], (8, 128))
                found = jnp.zeros((8, 128), F32)
                for part in range(13):
                    coarse = rows[8 * part : 8 * part + 8, 128 * r : 128 * r + 128]
                    fine = rows[104 + 8 * part : 112 + 8 * part, 128 * r : 128 * r + 128]
                    found = jnp.where(high_row == part, coarse + fine, found)
                bias_ref[b, pl.ds(pl.multiple_of(i * 64 + r * 8, 8), 8), :] = found
            if b == 0:
                block = low_ref[i]
                for r in range(8):
                    span = pl.ds(pl.multiple_of(i * 1024 + r * 128, 128), 128)
                    column = jnp.broadcast_to(block[:, r : r + 1], (128, 128)).astype(BF)
                    oht_ref[span, :] = jnp.where(place_t == jnp.concatenate([column] * 2, axis=1), one_t, zero_t)
            return carry

        lax.fori_loop(0, ROWS // 8, step, 0)
        for h in range(HEADS):
            unpack_tail(bias_ref[b, pl.ds(8 * TAIL + h, 24, stride=8), :], 6 * b + h)

    def fold_tables(start, stop):
        def step(i, carry):
            high = idx_ref[pl.ds(pl.multiple_of(i * 8, 8), 8), :] >> 8
            left = [[] for _ in range(26)]
            for r in range(8):
                high_row = jnp.broadcast_to(high[r : r + 1, :], (8, 128))
                for b in range(2):
                    grads = gall_ref[b, pl.ds(pl.multiple_of(i * 64 + r * 8, 8), 8), :]
                    for part in range(13):
                        left[13 * b + part].append(jnp.where(high_row == part, grads, 0.0))
            left = jnp.concatenate([jnp.concatenate(rows, axis=1) for rows in left], axis=0).astype(BF)
            acc_ref[...] += dot(left, oht_ref[pl.ds(pl.multiple_of(i * 1024, 1024), 1024), :])
            return carry

        lax.fori_loop(start, stop, step, 0)

    def region_codes(place):
        code = jnp.zeros_like(place)
        for part in range(12):
            value = ids_ref[part % 6] + 64 * (part // 6)
            code = jnp.where(place >= 12 * part, value, code)
        return code

    def forward(b):
        tokens = x_ref[b]
        qkv_ref[b] = dot(tokens, wqkv_ref[b]).astype(BF)
        q, k, v = (qkv_ref[b, :, C * i : C * i + C] for i in range(3))
        for h in range(HEADS):
            qm_ref[b, TOK * h : TOK * h + TOK, :] = of_head(q, h)
        s_ref[...] = dot_nt(qm_ref[b], k)
        if b == 1:
            codes_s = region_codes(lax.broadcasted_iota(jnp.int32, (TOK, 1), 0))
            codes_t = region_codes(lax.broadcasted_iota(jnp.int32, (1, TOK), 1))
            allowed = codes_s == codes_t
        for h in range(HEADS):
            span = pl.ds(TOK * h, TOK)
            main = bias_ref[b, pl.ds(h, TOK, stride=8), :]
            bias = jnp.concatenate([main, btail_ref[6 * b + h, 0:TOK, 0:16]], axis=1)
            scores = s_ref[span, :] * SCALE + bias
            if b == 1:
                scores = jnp.where(allowed, scores, NEGATIVE)
            powers = jnp.exp(scores - jnp.max(scores, axis=-1, keepdims=True))
            probs = powers * (1.0 / jnp.sum(powers, axis=-1, keepdims=True))
            p_ref[b, span, :] = probs.astype(BF)
        attended = jnp.zeros((TOK, C), F32)
        for h in range(HEADS):
            attended = jnp.where(head_lanes[h], dot(p_ref[b, TOK * h : TOK * h + TOK, :], v), attended)
        attended = attended.astype(BF)
        att_ref[b] = attended
        unit, inverse = norm_parts(dot(attended, wproj_ref[b]))
        u1_ref[b], i1_ref[b] = unit, inverse
        middle = (tokens.astype(F32) + unit * gains_ref[b, 0:1, :]).astype(BF)
        mid_ref[b] = middle
        for part in range(3):
            cols = pl.ds(256 * part, 256)
            up = dot(middle, wup_ref[b, :, cols])
            phi = 0.5 + 0.5 * lax.erf(up * (0.5**0.5))
            hid_ref[b, :, cols] = (up * phi).astype(BF)
            gp_ref[b, :, cols] = phi + up * (0.3989422804014327 * jnp.exp(-0.5 * up * up))
        unit, inverse = norm_parts(dot_nt(hid_ref[b], wdown_ref[b]))
        u2_ref[b], i2_ref[b] = unit, inverse
        return (middle.astype(F32) + unit * gains_ref[b, 1:2, :]).astype(BF)

    def backward(b, grad, between=lambda: None):
        grad = grad.astype(F32)
        grad_down = norm_back(grad * gains_ref[b, 1:2, :], u2_ref[b], i2_ref[b]).astype(BF)
        for part in range(3):
            cols = pl.ds(256 * part, 256)
            grad_hidden = dot(grad_down, wdown_ref[b, :, cols])
            gup_ref[b, :, cols] = (grad_hidden * gp_ref[b, :, cols]).astype(BF)
        grad_middle = grad + dot_nt(gup_ref[b], wup_ref[b])
        between()
        grad_pre = norm_back(grad_middle * gains_ref[b, 0:1, :], u1_ref[b], i1_ref[b]).astype(BF)
        grad_att = dot_nt(grad_pre, wproj_ref[b]).astype(BF)
        for h in range(HEADS):
            gam_ref[TOK * h : TOK * h + TOK, :] = of_head(grad_att, h)
        q, k, v = (qkv_ref[b, :, C * i : C * i + C] for i in range(3))
        s_ref[...] = dot_nt(gam_ref[...], v)
        for h in range(HEADS):
            span = pl.ds(TOK * h, TOK)
            probs = p_ref[b, span, :].astype(F32)
            grad_probs = s_ref[span, :]
            grad_scores = probs * (grad_probs - jnp.sum(grad_probs * probs, axis=-1, keepdims=True))
            ds_ref[span, :] = grad_scores.astype(BF)
            gall_ref[b, pl.ds(h, TOK, stride=8), :] = grad_scores[:, 0:128]
            gall_ref[b, pl.ds(8 * TAIL + h, 24, stride=8), :] = pack_tail(grad_scores[:, 128:TOK], h)
        grad_q = jnp.zeros((TOK, C), F32)
        for h in range(HEADS):
            grad_q = jnp.where(head_lanes[h], dot(ds_ref[TOK * h : TOK * h + TOK, :], k), grad_q)
        grad_k = dot_tn(ds_ref[...], qm_ref[b])
        grad_v = dot_tn(p_ref[b], gam_ref[...])
        grad_qkv = jnp.concatenate([grad_q * SCALE, grad_k * SCALE, grad_v], axis=1).astype(BF)
        grad_in = (grad_middle + dot_nt(grad_qkv, wqkv_ref[b])).astype(BF)
        return grad_in, grad_down, grad_pre, grad_qkv

    def weight_grads(b, grad_down, grad_pre, grad_qkv):
        l_ref[0:TOK, :] = moved(grad_qkv, pq_ref[...])
        l_ref[TOK : 2 * TOK, :] = moved(grad_pre, pp_ref[...])
        l_ref[2 * TOK : 3 * TOK, :] = gup_ref[b]
        tokens, middle = x_ref[b], mid_ref[b]
        r_ref[0:TOK, 0:128] = tokens[:, 0:128]
        r_ref[0:TOK, 256:320] = tokens[:, 128:C]
        r_ref[TOK : 2 * TOK, 0:128] = att_ref[b, :, 0:128]
        r_ref[TOK : 2 * TOK, 256:320] = att_ref[b, :, 128:C]
        r_ref[2 * TOK : 3 * TOK, 128:256] = middle[:, 0:128]
        r_ref[2 * TOK : 3 * TOK, 320:384] = middle[:, 128:C]
        o1_ref[...] = dot_tn(l_ref[...], r_ref[...])
        o3_ref[...] = dot_tn(moved(grad_down, pd_ref[...]), hid_ref[b])
        rows = 128 // n_lat
        for piece in range(32):
            units = [o1_ref[24 * piece + 8 * i : 24 * piece + 8 * i + 8, 128 * m : 128 * m + 128] for m in range(3) for i in range(3)]
            units += [o3_ref[8 * piece : 8 * piece + 8, 128 * i : 128 * i + 128] for i in range(6)]
            units += [jnp.zeros((8, 128), F32)]
            for tile in range(8):
                pair = jnp.concatenate([units[2 * tile], units[2 * tile + 1]], axis=0).astype(BF)
                at, off = 16 * tile // rows, 16 * tile % rows
                across = at % 2 * 2 + piece // 2 % 2
                sb_ref[b, piece % 2, at // 2, across, piece // 4, off : off + 16, :] = pair

    class Sum:
        def __init__(self, b):
            self.b = b
            self.copies = []
            self.steps = [self.core, self.along_xy, self.along_z, self.share, self.done]

        def next(self):
            if self.steps:
                self.steps.pop(0)()

        def core(self):
            self.copies = [push(sb_ref.at[self.b, 1 - co], rc_ref.at[self.b], (lat, lon + 1 - 2 * co))]

        def along_xy(self):
            b = self.b
            arrive(self.copies)
            wa_ref[b] = (sb_ref[b, co].astype(F32) + rc_ref[b].astype(F32)).astype(BF)
            self.copies = []
            for k in range(1, 4 * ny):
                its_y, its_x = (y + k // 4) % ny, (x + k % 4) % 4
                device = (its_y * 2 + its_x // 2, z * 4 + its_x % 2 * 2 + co)
                self.copies.append(push(wa_ref.at[b, its_y, its_x], rx_ref.at[b, k - 1], device))

        def along_z(self):
            b = self.b
            arrive(self.copies)
            total = wa_ref[b, y, x].astype(F32)
            for k in range(4 * ny - 1):
                total = total + rx_ref[b, k].astype(F32)
            wc_ref[b] = total.astype(BF)
            self.copies = []
            for k in range(1, nz):
                self.copies.append(push(wc_ref.at[b, (z + k) % nz], rz_ref.at[b, k - 1], (lat, z_lons[k])))

        def share(self):
            b = self.b
            arrive(self.copies)
            total = wc_ref[b, z].astype(F32)
            for k in range(nz - 1):
                total = total + rz_ref[b, k].astype(F32)
            wd_ref[b] = total.astype(BF)
            self.copies = []
            for k in range(1, n_lat):
                self.copies.append(push(wd_ref.at[b], wl_ref.at[b, lat], ((lat + k) % n_lat, lon)))
            wl_ref[b, lat] = wd_ref[b]

        def done(self):
            arrive(self.copies)
            wg_ref[self.b] = wl_ref[self.b]

    class TableSum:
        def __init__(self):
            self.copies = []
            self.steps = [self.pair, self.along_z, self.share_z, self.share_pair, self.done]

        def next(self):
            if self.steps:
                self.steps.pop(0)()

        def pair(self):
            for part in range(26):
                row, lanes = 8 * (part // 2), slice(128 * (part % 2), 128 * (part % 2) + 128)
                both = jnp.concatenate([acc_ref[row : row + 8, lanes], acc_ref[104 + row : 112 + row, lanes]], axis=0)
                tb_ref[part // 16, part // 8 % 2, part % 8] = both.astype(BF)
            for part in range(26, 32):
                tb_ref[part // 16, part // 8 % 2, part % 8] = jnp.zeros((16, 128), BF)
            for k in range(1, 4):
                device, its_xl, its_co = lon_pair[k]
                self.copies.append(push(tb_ref.at[its_co, its_xl], tr1_ref.at[k - 1], (lat, device)))

        def along_z(self):
            arrive(self.copies)
            total = tb_ref[co, xl].astype(F32)
            for k in range(3):
                total = total + tr1_ref[k].astype(F32)
            t1_ref[...] = total.astype(BF)
            self.copies = []
            for k in range(1, nz):
                self.copies.append(push(t1_ref.at[(z + k) % nz], tr2_ref.at[k - 1], (lat, z_lons[k])))

        def share_z(self):
            arrive(self.copies)
            total = t1_ref[z].astype(F32)
            for k in range(nz - 1):
                total = total + tr2_ref[k].astype(F32)
            t2_ref[...] = total.astype(BF)
            self.copies = []
            for k in range(1, nz):
                self.copies.append(push(t2_ref, t3_ref.at[z], (lat, z_lons[k])))
            t3_ref[z] = t2_ref[...]

        def share_pair(self):
            arrive(self.copies)
            self.copies = []
            for k in range(1, 4):
                self.copies.append(push(t3_ref, t4_ref.at[co, xl], (lat, lon_pair[k][0])))
            t4_ref[co, xl] = t3_ref[...]

        def done(self):
            arrive(self.copies)
            tgrad_ref[...] = t4_ref[...]

    def send_quarters(which, devices):
        copies = []
        for quarter in range(1, 4):
            copies.append(push(hs_ref.at[which, quarter], hr_ref.at[which, quarter], devices[quarter]))
        hr_ref[which, 0] = hs_ref[which, 0]
        return copies

    pk_ref[...] = jnp.zeros_like(pk_ref)
    gall_ref[...] = jnp.zeros_like(gall_ref)
    r_ref[...] = jnp.zeros_like(r_ref)
    loads[0].wait()
    idx_ref[0:TOK, :] = rel_ref[:, 0:128]
    idx_ref[TAIL:ROWS, :] = pack_tail(rel_ref[:, 128:TOK].astype(F32), 0).astype(jnp.int32)
    idx_ref[TAIL + 18 : ROWS, :] = jnp.full((ROWS - TAIL - 18, 128), -1, jnp.int32)
    low = (idx_ref[...] & 255).astype(F32).T
    for i in range(ROWS // 8):
        low_ref[i] = low[:, 8 * i : 8 * i + 8]
    loads[1].wait()
    tabf_ref[...] = jnp.zeros_like(tabf_ref)
    for b in range(2):
        for part in range(13):
            width = min(256, POS - 256 * part)
            tabf_ref[b, 8 * part : 8 * part + 6, 0:width] = table_ref[6 * b : 6 * b + 6, 0, 256 * part : 256 * part + width]
        table = tabf_ref[b]
        coarse = table.astype(BF)
        tab_ref[b, 0:104, :] = coarse
        tab_ref[b, 104:208, :] = (table - coarse.astype(F32)).astype(BF)
    gather_bias(0)
    for load in loads[2:]:
        load.wait()
    x_ref[0] = moved(onehot(TOK, TOK, 0), tok_ref[...].reshape(TOK, C))
    hs_ref[0] = moved(onehot(192, TOK, 10), gmix_ref[...].reshape(TOK, C)).reshape(4, 48, C)

    first = forward(0)
    hs_ref[1] = moved(onehot(192, TOK, 2), first).reshape(4, 48, C)
    pl.semaphore_wait(barrier, len(greeted))
    copies_x = send_quarters(1, ahead)
    copies_g = send_quarters(0, ahead)
    gather_bias(1)
    acc_ref[...] = jnp.zeros_like(acc_ref)
    arrive(copies_x)
    arrive(copies_g)
    come = onehot(TOK, 192, 3)
    x_ref[1] = moved(come, hr_ref[1].reshape(192, C))
    grad_shifted = moved(come, hr_ref[0].reshape(192, C))

    second = forward(1)
    hs_ref[2] = moved(onehot(192, TOK, 4), second).reshape(4, 48, C)
    grad_second, *rest = backward(1, grad_shifted)
    hs_ref[3] = moved(onehot(192, TOK, 4), grad_second).reshape(4, 48, C)
    copies_s = send_quarters(3, back)
    copies_m = send_quarters(2, back)
    weight_grads(1, *rest)
    sum_two = Sum(1)
    sum_two.next()

    arrive(copies_s)
    grad_first = moved(onehot(TOK, 192, 5), hr_ref[3].reshape(192, C))
    grad_in, *rest = backward(0, grad_first, sum_two.next)
    weight_grads(0, *rest)
    sum_one = Sum(0)
    sum_table = TableSum()
    sum_one.next()
    sum_two.next()
    fold_tables(0, 9)
    sum_one.next()
    fold_tables(9, ROWS // 8)
    sum_table.next()
    sum_two.next()
    arrive(copies_m)
    mixed_ref[...] = moved(onehot(TOK, 192, 6), hr_ref[2].reshape(192, C)).reshape(72, 2, C)
    gtok_ref[...] = moved(onehot(TOK, TOK, 1), grad_in).reshape(72, 2, C)
    sum_table.next()
    sum_two.next()
    sum_table.next()
    sum_one.next()
    sum_table.next()
    sum_one.next()
    sum_table.next()
    sum_one.next()
    for copy in sent:
        copy.wait_send()


def finish(mixed_in, gtok_in, wg_in, table_in, mixed_ref, gtok_ref, qkv_ref, proj_ref, up_ref, down_ref, table_ref):
    mixed_ref[...] = mixed_in[...]
    gtok_ref[...] = gtok_in[...]
    for b in range(2):
        rows = wg_in[b].reshape(128, 128).astype(F32)
        qkv_ref[:, b, 0:128] = rows[0:18, :]
        qkv_ref[:, b, 128:C] = rows[48:66, 0:64]
        proj_ref[:, b, 0:128] = rows[18:24, :]
        proj_ref[:, b, 128:C] = rows[66:72, 0:64]
        up_ref[b, :, 0:128] = rows[24:48, :]
        up_ref[b, :, 128:C] = rows[48:72, 64:128]
        for i in range(6):
            down_ref[:, b, 128 * i : 128 * i + 128] = rows[72 + 8 * i : 78 + 8 * i, :]
    for part in range(26):
        tile = table_in[part // 16, part // 8 % 2, part % 8].astype(F32)
        width = min(128, POS - 128 * part)
        for b in range(2):
            table_ref[6 * b : 6 * b + 6, 0, 128 * part : 128 * part + width] = tile[8 * b : 8 * b + 6, 0:width]


def per_device(tokens, grad_mixed, w_qkv, w_proj, w_up, w_down, gains, bias_table, rel_index, mask_ids):
    n_lat, n_lon = lax.axis_size("lat"), lax.axis_size("lon")
    ny, nz, rows = n_lat // 2, n_lon // 4, 128 // n_lat
    vmem = pl.BlockSpec(memory_space=pltpu.VMEM)
    smem = pl.BlockSpec(memory_space=pltpu.SMEM)

    def buf(*shape, dtype=BF):
        return pltpu.VMEM(shape, dtype)

    scratch = [
        buf(TOK, TOK, dtype=jnp.int32), buf(12, 1, POS, dtype=F32), buf(16, 768, dtype=jnp.int32),
        buf(72, 2, C), buf(72, 2, C), buf(2, C, 3 * C), buf(2, C, C), buf(2, 2, C, dtype=F32), buf(2, C, 768), buf(2, C, 768),
        buf(3 * C, 768), buf(C, 768), buf(C, 256),
        pltpu.SemaphoreType.DMA((13,)),
        buf(2, TOK, C), buf(2, TOK, 3 * C), buf(2, 6 * TOK, C), buf(6 * TOK, TOK, dtype=F32),
        buf(2, 6 * TOK, TOK), buf(2, TOK, C), buf(2, TOK, C, dtype=F32), buf(2, TOK, 1, dtype=F32), buf(2, TOK, C),
        buf(2, TOK, 768, dtype=F32), buf(2, TOK, 768), buf(2, TOK, C, dtype=F32), buf(2, TOK, 1, dtype=F32),
        buf(2, TOK, 768), buf(6 * TOK, C), buf(6 * TOK, TOK),
        buf(ROWS, 128, dtype=jnp.int32), buf(ROWS // 8, 128, 8, dtype=F32), buf(128 * ROWS, 256), buf(2, 104, 256, dtype=F32),
        buf(2, 208, 256), buf(2, 8 * ROWS, 128, dtype=F32), buf(12, 192, 128, dtype=F32), buf(6, 192, 128, dtype=F32),
        buf(2, 8 * ROWS, 128, dtype=F32), buf(208, 256, dtype=F32),
        buf(3 * TOK, 768), buf(3 * TOK, 384), buf(768, 384, dtype=F32), buf(256, 768, dtype=F32),
        buf(4, 4, 48, C), buf(4, 4, 48, C),
        buf(2, 2, ny, 4, nz, rows, 128), buf(2, ny, 4, nz, rows, 128), buf(2, ny, 4, nz, rows, 128),
        buf(2, 4 * ny - 1, nz, rows, 128),
        buf(2, nz, rows, 128), buf(2, nz - 1, rows, 128), buf(2, rows, 128), buf(2, n_lat, rows, 128),
        buf(2, 2, 8, 16, 128), buf(3, 8, 16, 128), buf(8, 16, 128), buf(7, 16, 128), buf(16, 128),
        buf(8, 16, 128), buf(2, 2, 8, 16, 128),
        pltpu.SemaphoreType.DMA((N_SEMS,)), pltpu.SemaphoreType.DMA((N_SEMS,)),
    ]
    results = pl.pallas_call(
        functools.partial(kernel, n_lat, n_lon),
        out_shape=(
            jax.ShapeDtypeStruct((72, 2, C), BF),
            jax.ShapeDtypeStruct((72, 2, C), BF),
            jax.ShapeDtypeStruct((2, n_lat, rows, 128), BF),
            jax.ShapeDtypeStruct((2, 2, 8, 16, 128), BF),
        ),
        in_specs=[pl.BlockSpec(memory_space=pltpu.HBM)] * 13 + [smem],
        out_specs=[vmem] * 4,
        scratch_shapes=scratch,
        compiler_params=pltpu.CompilerParams(
            collective_id=0, has_side_effects=True, vmem_limit_bytes=60 * 1024 * 1024
        ),
    )(
        rel_index,
        bias_table.reshape(12, 1, POS),
        jnp.asarray(index_rows()),
        tokens.transpose(1, 2, 0, 3).reshape(72, 2, C),
        grad_mixed.transpose(1, 2, 0, 3).reshape(72, 2, C),
        w_qkv, w_proj, gains, w_up, w_down.transpose(0, 2, 1),
        *permutations(),
        mask_ids,
    )
    mixed, grad_tokens, qkv, proj, up, down, table = pl.pallas_call(
        finish,
        out_shape=(
            jax.ShapeDtypeStruct((72, 2, C), BF),
            jax.ShapeDtypeStruct((72, 2, C), BF),
            jax.ShapeDtypeStruct((18, 2, C), F32),
            jax.ShapeDtypeStruct((6, 2, C), F32),
            jax.ShapeDtypeStruct((2, 24, C), F32),
            jax.ShapeDtypeStruct((6, 2, 768), F32),
            jax.ShapeDtypeStruct((12, 1, POS), F32),
        ),
        in_specs=[vmem] * 4,
        out_specs=[vmem] * 7,
        compiler_params=pltpu.CompilerParams(vmem_limit_bytes=60 * 1024 * 1024),
    )(*results)

    def field(value):
        return value.reshape(6, 12, 2, C).transpose(2, 0, 1, 3)

    return (
        field(mixed),
        field(grad_tokens),
        qkv.transpose(1, 2, 0),
        proj.transpose(1, 2, 0),
        up.transpose(0, 2, 1),
        down.transpose(1, 2, 0),
        table.reshape(2, 1, 1, 6, POS),
    )


def solution(mesh):
    field = P(None, "lat", "lon", None)
    table = P(None, None, "lat", None, None)
    in_specs = (field, field, P(), P(), P(), P(), P(), table, P(), P("lat"))
    columns = P(None, None, "lon")
    out_specs = (field, field, columns, columns, columns, columns, table)
    return jax.shard_map(per_device, mesh=mesh, in_specs=in_specs, out_specs=out_specs, check_vma=False)
```

```python
import functools

import jax
import jax.numpy as jnp
import numpy as np
from jax import lax
from jax.experimental import pallas as pl
from jax.experimental.pallas import tpu as pltpu
from jax.sharding import PartitionSpec as P

HEADS = 6
C = 192
TOK = 144
POS = 3312
EPS = 1e-05
NEGATIVE = -1e30
SCALE = 32 ** -0.5
BF = jnp.bfloat16
F32 = jnp.float32
MESH = pl.DeviceIdType.MESH
ROWS = 192
TAIL = 144
N_SEMS = 94


def index_rows():
    rows = np.full((16, 768), -1, np.int32)
    tok = np.arange(TOK)
    level, row, col = tok // 72, tok // 12 % 6, tok % 12
    place = 24 * row + 2 * col + level
    own = 18 * level + row % 3 * 6 + col % 6
    other = 18 * (1 - level) + row % 3 * 6 + col % 6
    low = 48 * (2 * (row // 3) + col // 6)
    high = 48 * (2 * (1 - row // 3) + 1 - col // 6)
    rows[0, place] = tok
    rows[1, tok] = place
    rows[2, tok] = high + own
    rows[3, low + other] = tok
    rows[4, tok] = low + own
    rows[5, high + other] = tok
    rows[6, high + other] = place
    rows[10, place] = high + own
    return rows


def permutations():
    qkv = np.zeros((3 * C, 768), np.float32)
    proj = np.zeros((C, 768), np.float32)
    down = np.zeros((C, 256), np.float32)
    for piece in range(32):
        for i in range(18):
            qkv[18 * piece + i, 24 * piece + i] = 1
        for i in range(6):
            proj[6 * piece + i, 24 * piece + 18 + i] = 1
            down[6 * piece + i, 8 * piece + i] = 1
    return tuple(jnp.asarray(matrix, BF) for matrix in (qkv, proj, down))


def dot(a, b):
    return jnp.dot(a, b, preferred_element_type=F32)


def dot_nt(a, b):
    return lax.dot_general(a, b, (((1,), (1,)), ((), ())), preferred_element_type=F32)


def dot_tn(a, b):
    return lax.dot_general(a, b, (((0,), (0,)), ((), ())), preferred_element_type=F32)


def norm_parts(v):
    center = v - jnp.mean(v, axis=-1, keepdims=True)
    spread = jnp.mean(center * center, axis=-1, keepdims=True)
    inverse = lax.rsqrt(spread + EPS)
    return center * inverse, inverse


def norm_back(grad, unit, inverse):
    along = jnp.mean(grad * unit, axis=-1, keepdims=True)
    return inverse * (grad - jnp.mean(grad, axis=-1, keepdims=True) - unit * along)


def kernel(
    n_lat, n_lon,
    rel_hbm, table_hbm, const_hbm, tok_hbm, gmix_hbm, wqkv_hbm, wproj_hbm, gains_hbm, wup_hbm, wdown_hbm, pq_hbm, pp_hbm, pd_hbm, ids_ref,
    mixed_ref, gtok_ref, wg_ref, tgrad_ref,
    rel_ref, table_ref, const_ref, tok_ref, gmix_ref, wqkv_ref, wproj_ref, gains_ref, wup_ref, wdown_ref, pq_ref, pp_ref, pd_ref, load_sem,
    x_ref, qkv_ref, km_ref, vm_ref, s_ref, p_ref, att_ref, u1_ref, i1_ref, mid_ref, gp_ref, hid_ref, u2_ref, i2_ref,
    gup_ref, ds_ref, idx_ref, low_ref, tabf_ref, tab_ref, bias_ref, btail_ref, pk_ref, gall_ref, gsend_ref, grecv_ref, acc_ref,
    l_ref, r_ref, o1_ref, o3_ref,
    hs_ref, hr_ref,
    sb_ref, rc_ref, wa_ref, rx_ref, wc_ref, rz_ref, wd_ref, wl_ref,
    tb_ref, tr1_ref, t1_ref, tr2_ref, t2_ref, t3_ref, t4_ref,
    ssem, rsem,
):
    loads = [
        pltpu.make_async_copy(src, dst, load_sem.at[k])
        for k, (src, dst) in enumerate([
            (rel_hbm, rel_ref), (table_hbm, table_ref), (const_hbm, const_ref), (tok_hbm, tok_ref), (gmix_hbm, gmix_ref),
            (wqkv_hbm, wqkv_ref), (wproj_hbm, wproj_ref), (gains_hbm, gains_ref), (wup_hbm, wup_ref), (wdown_hbm, wdown_ref),
            (pq_hbm, pq_ref), (pp_hbm, pp_ref), (pd_hbm, pd_ref),
        ])
    ]
    for load in loads:
        load.start()
    ny, nz = n_lat // 2, n_lon // 4
    lat, lon = lax.axis_index("lat"), lax.axis_index("lon")
    y, xh = lat // 2, lat % 2
    z, xl, co = lon // 4, lon // 2 % 2, lon % 2
    x = xh * 2 + xl
    lon_pair = [
        (z * 4 + ((xl + (k >> 1)) % 2) * 2 + (co + (k & 1)) % 2, (xl + (k >> 1)) % 2, (co + (k & 1)) % 2)
        for k in range(4)
    ]
    ahead = [((lat + n_lat - a) % n_lat, (lon + n_lon - b) % n_lon) for a in (0, 1) for b in (0, 1)]
    back = [((lat + a) % n_lat, (lon + b) % n_lon) for a in (0, 1) for b in (0, 1)]
    z_lons = [(z + k) % nz * 4 + xl * 2 + co for k in range(nz)]

    greeted = [((lat + k) % n_lat, lon) for k in range(1, n_lat)]
    greeted += [(lat, z_lons[k]) for k in range(1, nz)]
    greeted += [(lat, lon_pair[k][0]) for k in (1, 3)]
    greeted += [((lat + k) % n_lat, lon_pair[2][0]) for k in range(n_lat)]
    greeted += [ahead[1], ahead[3], back[1], back[3]]
    barrier = pltpu.get_barrier_semaphore()
    for device in greeted:
        pl.semaphore_signal(barrier, inc=1, device_id=device, device_id_type=MESH)

    sems = iter(range(N_SEMS))
    sent = []

    def push(src, dst, device):
        k = next(sems)
        copy = pltpu.make_async_remote_copy(
            src_ref=src, dst_ref=dst, send_sem=ssem.at[k], recv_sem=rsem.at[k], device_id=device, device_id_type=MESH
        )
        copy.start()
        sent.append(copy)
        return copy

    def arrive(copies):
        for copy in copies:
            copy.wait_recv()

    def onehot(n_rows, n_lanes, which):
        place = lax.broadcasted_iota(jnp.int32, (n_rows, n_lanes), 0)
        return jnp.where(place == const_ref[which : which + 1, :n_lanes], 1.0, 0.0).astype(BF)

    def moved(matrix, value):
        return dot(matrix, value).astype(BF)

    lane = lax.broadcasted_iota(jnp.int32, (1, C), 1)
    head_lanes = [(lane >= 32 * h) & (lane < 32 * h + 32) for h in range(HEADS)]

    def of_head(value, h):
        return jnp.where(head_lanes[h], value, jnp.zeros_like(value))

    def pack_tail(value, h):
        pk_ref[h, 0:TOK, 0:16] = value
        total = pk_ref[h, pl.ds(0, 24, stride=8), :]
        for j in range(1, 8):
            total = total + pltpu.roll(pk_ref[h, pl.ds(j, 24, stride=8), :], 16 * j, 1)
        return total

    def unpack_tail(value, k):
        for j in range(8):
            rolled = pltpu.roll(value, (128 - 16 * j) % 128, 1)
            btail_ref[k, pl.ds(j, 24, stride=8), :] = rolled

    def gather_bias(b):
        place = lax.broadcasted_iota(jnp.int32, (256, 128), 0).astype(BF)
        one, zero = jnp.ones((256, 128), BF), jnp.zeros((256, 128), BF)

        def step(i, carry):
            for m in range(3):
                group = i * 3 + m
                index = idx_ref[pl.ds(pl.multiple_of(group * 8, 8), 8), :]
                low, high = (index & 255).astype(F32), index >> 8
                picks = []
                for r in range(8):
                    row = jnp.broadcast_to(low[r : r + 1, :], (16, 128)).astype(BF)
                    picks.append(jnp.where(place == jnp.concatenate([row] * 16, axis=0), one, zero))
                rows = dot(tab_ref[b], jnp.concatenate(picks, axis=1))
                for r in range(8):
                    high_row = jnp.broadcast_to(high[r : r + 1, :], (8, 128))
                    found = jnp.zeros((8, 128), F32)
                    for part in range(13):
                        coarse = rows[8 * part : 8 * part + 8, 128 * r : 128 * r + 128]
                        fine = rows[104 + 8 * part : 112 + 8 * part, 128 * r : 128 * r + 128]
                        found = jnp.where(high_row == part, coarse + fine, found)
                    bias_ref[pl.ds(pl.multiple_of(group * 64 + r * 8, 8), 8), :] = found
            return carry

        lax.fori_loop(0, 7, step, 0)
        for h in range(HEADS):
            unpack_tail(bias_ref[pl.ds(8 * TAIL + h, 24, stride=8), :], h)

    half = ROWS // 2

    def share_scores(b):
        gsend_ref[b] = gall_ref[b, pl.ds((1 - co) * 8 * half, 8 * half), :].astype(BF)
        return [push(gsend_ref.at[b], grecv_ref.at[b], (lat, lon + 1 - 2 * co))]

    def add_scores(b, copies):
        arrive(copies)
        mine = pl.ds(co * 8 * half, 8 * half)
        gall_ref[b, mine, :] = gall_ref[b, mine, :] + grecv_ref[b].astype(F32)

    def fold_tables(start, stop):
        place = lax.broadcasted_iota(jnp.int32, (128, 256), 1).astype(BF)
        one, zero = jnp.ones((128, 256), BF), jnp.zeros((128, 256), BF)

        def step(i, carry):
            total = acc_ref[...]
            for m in range(3):
                group = co * (half // 8) + i * 3 + m
                high = idx_ref[pl.ds(pl.multiple_of(group * 8, 8), 8), :] >> 8
                block = low_ref[group]
                left, right = [[] for _ in range(26)], []
                for r in range(8):
                    high_row = jnp.broadcast_to(high[r : r + 1, :], (8, 128))
                    hits = [high_row == part for part in range(13)]
                    for b in range(2):
                        grads = gall_ref[b, pl.ds(pl.multiple_of(group * 64 + r * 8, 8), 8), :]
                        for part in range(13):
                            left[13 * b + part].append(jnp.where(hits[part], grads, 0.0))
                    column = jnp.broadcast_to(block[:, r : r + 1], (128, 128)).astype(BF)
                    right.append(jnp.where(place == jnp.concatenate([column] * 2, axis=1), one, zero))
                left = jnp.concatenate([jnp.concatenate(rows, axis=1) for rows in left], axis=0).astype(BF)
                total = total + dot(left, jnp.concatenate(right, axis=0))
            acc_ref[...] = total
            return carry

        lax.fori_loop(start, stop, step, 0)

    def region_codes(place):
        code = jnp.zeros_like(place)
        for part in range(12):
            value = ids_ref[part % 6] + 64 * (part // 6)
            code = jnp.where(place >= 12 * part, value, code)
        return code

    def forward(b):
        tokens = x_ref[b]
        qkv_ref[b] = dot(tokens, wqkv_ref[b]).astype(BF)
        q, k, v = (qkv_ref[b, :, C * i : C * i + C] for i in range(3))
        for h in range(HEADS):
            km_ref[b, TOK * h : TOK * h + TOK, :] = of_head(k, h)
            vm_ref[b, TOK * h : TOK * h + TOK, :] = of_head(v, h)
        s_ref[...] = dot_nt(km_ref[b], q)
        if b == 1:
            codes_t = region_codes(lax.broadcasted_iota(jnp.int32, (TOK, 1), 0))
            codes_s = region_codes(lax.broadcasted_iota(jnp.int32, (1, TOK), 1))
            allowed = codes_s == codes_t
        for h in range(HEADS):
            span = pl.ds(TOK * h, TOK)
            bias = jnp.concatenate([bias_ref[pl.ds(h, TOK, stride=8), :], btail_ref[h, 0:TOK, 0:16]], axis=1)
            scores = s_ref[span, :] * SCALE + bias
            if b == 1:
                scores = jnp.where(allowed, scores, NEGATIVE)
            powers = jnp.exp(scores - jnp.max(scores, axis=0, keepdims=True))
            probs = powers * (1.0 / jnp.sum(powers, axis=0, keepdims=True))
            p_ref[b, span, :] = probs.astype(BF)
        attended = dot_tn(p_ref[b], vm_ref[b]).astype(BF)
        att_ref[b] = attended
        unit, inverse = norm_parts(dot(attended, wproj_ref[b]))
        u1_ref[b], i1_ref[b] = unit, inverse
        middle = (tokens.astype(F32) + unit * gains_ref[b, 0:1, :]).astype(BF)
        mid_ref[b] = middle
        for part in range(3):
            cols = pl.ds(256 * part, 256)
            up = dot(middle, wup_ref[b, :, cols])
            phi = 0.5 + 0.5 * lax.erf(up * (0.5**0.5))
            hid_ref[b, :, cols] = (up * phi).astype(BF)
            gp_ref[b, :, cols] = phi + up * (0.3989422804014327 * jnp.exp(-0.5 * up * up))
        unit, inverse = norm_parts(dot_nt(hid_ref[b], wdown_ref[b]))
        u2_ref[b], i2_ref[b] = unit, inverse
        return (middle.astype(F32) + unit * gains_ref[b, 1:2, :]).astype(BF)

    def backward(b, grad, between=lambda: None):
        grad = grad.astype(F32)
        grad_down = norm_back(grad * gains_ref[b, 1:2, :], u2_ref[b], i2_ref[b]).astype(BF)
        for part in range(3):
            cols = pl.ds(256 * part, 256)
            grad_hidden = dot(grad_down, wdown_ref[b, :, cols])
            gup_ref[b, :, cols] = (grad_hidden * gp_ref[b, :, cols]).astype(BF)
        grad_middle = grad + dot_nt(gup_ref[b], wup_ref[b])
        between()
        grad_pre = norm_back(grad_middle * gains_ref[b, 0:1, :], u1_ref[b], i1_ref[b]).astype(BF)
        grad_att = dot_nt(grad_pre, wproj_ref[b]).astype(BF)
        q = qkv_ref[b, :, 0:C]
        s_ref[...] = dot_nt(vm_ref[b], grad_att)
        for h in range(HEADS):
            span = pl.ds(TOK * h, TOK)
            probs = p_ref[b, span, :].astype(F32)
            grad_probs = s_ref[span, :]
            grad_scores = probs * (grad_probs - jnp.sum(grad_probs * probs, axis=0, keepdims=True))
            ds_ref[span, :] = grad_scores.astype(BF)
            gall_ref[b, pl.ds(h, TOK, stride=8), :] = grad_scores[:, 0:128]
            gall_ref[b, pl.ds(8 * TAIL + h, 24, stride=8), :] = pack_tail(grad_scores[:, 128:TOK], h)
        grad_q = dot_tn(ds_ref[...], km_ref[b])
        grad_k, grad_v = jnp.zeros((TOK, C), F32), jnp.zeros((TOK, C), F32)
        for h in range(HEADS):
            span = pl.ds(TOK * h, TOK)
            grad_k = jnp.where(head_lanes[h], dot(ds_ref[span, :], q), grad_k)
            grad_v = jnp.where(head_lanes[h], dot(p_ref[b, span, :], grad_att), grad_v)
        grad_qkv = jnp.concatenate([grad_q * SCALE, grad_k * SCALE, grad_v], axis=1).astype(BF)
        grad_in = (grad_middle + dot_nt(grad_qkv, wqkv_ref[b])).astype(BF)
        return grad_in, grad_down, grad_pre, grad_qkv

    def weight_grads(b, grad_down, grad_pre, grad_qkv):
        l_ref[0:TOK, :] = moved(grad_qkv, pq_ref[...])
        l_ref[TOK : 2 * TOK, :] = moved(grad_pre, pp_ref[...])
        l_ref[2 * TOK : 3 * TOK, :] = gup_ref[b]
        tokens, middle = x_ref[b], mid_ref[b]
        r_ref[0:TOK, 0:128] = tokens[:, 0:128]
        r_ref[0:TOK, 256:320] = tokens[:, 128:C]
        r_ref[TOK : 2 * TOK, 0:128] = att_ref[b, :, 0:128]
        r_ref[TOK : 2 * TOK, 256:320] = att_ref[b, :, 128:C]
        r_ref[2 * TOK : 3 * TOK, 128:256] = middle[:, 0:128]
        r_ref[2 * TOK : 3 * TOK, 320:384] = middle[:, 128:C]
        o1_ref[...] = dot_tn(l_ref[...], r_ref[...])
        o3_ref[...] = dot_tn(moved(grad_down, pd_ref[...]), hid_ref[b])
        rows = 128 // n_lat
        for piece in range(32):
            units = [o1_ref[24 * piece + 8 * i : 24 * piece + 8 * i + 8, 128 * m : 128 * m + 128] for m in range(3) for i in range(3)]
            units += [o3_ref[8 * piece : 8 * piece + 8, 128 * i : 128 * i + 128] for i in range(6)]
            units += [jnp.zeros((8, 128), F32)]
            for tile in range(8):
                pair = jnp.concatenate([units[2 * tile], units[2 * tile + 1]], axis=0).astype(BF)
                at, off = 16 * tile // rows, 16 * tile % rows
                across = at % 2 * 2 + piece // 2 % 2
                sb_ref[b, piece % 2, at // 2, across, piece // 4, off : off + 16, :] = pair

    class Sum:
        def __init__(self, b):
            self.b = b
            self.copies = []
            self.steps = [self.core, self.along_xy, self.along_z, self.share, self.done]

        def next(self):
            if self.steps:
                self.steps.pop(0)()

        def core(self):
            self.copies = [push(sb_ref.at[self.b, 1 - co], rc_ref.at[self.b], (lat, lon + 1 - 2 * co))]

        def along_xy(self):
            b = self.b
            arrive(self.copies)
            wa_ref[b] = (sb_ref[b, co].astype(F32) + rc_ref[b].astype(F32)).astype(BF)
            self.copies = []
            for k in range(1, 4 * ny):
                its_y, its_x = (y + k // 4) % ny, (x + k % 4) % 4
                device = (its_y * 2 + its_x // 2, z * 4 + its_x % 2 * 2 + co)
                self.copies.append(push(wa_ref.at[b, its_y, its_x], rx_ref.at[b, k - 1], device))

        def along_z(self):
            b = self.b
            arrive(self.copies)
            total = wa_ref[b, y, x].astype(F32)
            for k in range(4 * ny - 1):
                total = total + rx_ref[b, k].astype(F32)
            wc_ref[b] = total.astype(BF)
            self.copies = []
            for k in range(1, nz):
                self.copies.append(push(wc_ref.at[b, (z + k) % nz], rz_ref.at[b, k - 1], (lat, z_lons[k])))

        def share(self):
            b = self.b
            arrive(self.copies)
            total = wc_ref[b, z].astype(F32)
            for k in range(nz - 1):
                total = total + rz_ref[b, k].astype(F32)
            wd_ref[b] = total.astype(BF)
            self.copies = []
            for k in range(1, n_lat):
                self.copies.append(push(wd_ref.at[b], wl_ref.at[b, lat], ((lat + k) % n_lat, lon)))
            wl_ref[b, lat] = wd_ref[b]

        def done(self):
            arrive(self.copies)
            wg_ref[self.b] = wl_ref[self.b]

    class TableSum:
        def __init__(self):
            self.copies = []
            self.steps = [self.pair, self.along_z, self.share_z, self.share_pair, self.done]

        def next(self):
            if self.steps:
                self.steps.pop(0)()

        def pair(self):
            for part in range(26):
                row, lanes = 8 * (part // 2), slice(128 * (part % 2), 128 * (part % 2) + 128)
                both = jnp.concatenate([acc_ref[row : row + 8, lanes], acc_ref[104 + row : 112 + row, lanes]], axis=0)
                tb_ref[part // 16, part // 8 % 2, part % 8] = both.astype(BF)
            for part in range(26, 32):
                tb_ref[part // 16, part // 8 % 2, part % 8] = jnp.zeros((16, 128), BF)
            for k in range(1, 4):
                device, its_xl, its_co = lon_pair[k]
                self.copies.append(push(tb_ref.at[its_co, its_xl], tr1_ref.at[k - 1], (lat, device)))

        def along_z(self):
            arrive(self.copies)
            total = tb_ref[co, xl].astype(F32)
            for k in range(3):
                total = total + tr1_ref[k].astype(F32)
            t1_ref[...] = total.astype(BF)
            self.copies = []
            for k in range(1, nz):
                self.copies.append(push(t1_ref.at[(z + k) % nz], tr2_ref.at[k - 1], (lat, z_lons[k])))

        def share_z(self):
            arrive(self.copies)
            total = t1_ref[z].astype(F32)
            for k in range(nz - 1):
                total = total + tr2_ref[k].astype(F32)
            t2_ref[...] = total.astype(BF)
            self.copies = []
            for k in range(1, nz):
                self.copies.append(push(t2_ref, t3_ref.at[z], (lat, z_lons[k])))
            t3_ref[z] = t2_ref[...]

        def share_pair(self):
            arrive(self.copies)
            self.copies = []
            for k in range(1, 4):
                self.copies.append(push(t3_ref, t4_ref.at[co, xl], (lat, lon_pair[k][0])))
            t4_ref[co, xl] = t3_ref[...]

        def done(self):
            arrive(self.copies)
            tgrad_ref[...] = t4_ref[...]

    def send_quarters(which, devices):
        copies = []
        for quarter in range(1, 4):
            copies.append(push(hs_ref.at[which, quarter], hr_ref.at[which, quarter], devices[quarter]))
        hr_ref[which, 0] = hs_ref[which, 0]
        return copies

    pk_ref[...] = jnp.zeros_like(pk_ref)
    gall_ref[...] = jnp.zeros_like(gall_ref)
    r_ref[...] = jnp.zeros_like(r_ref)
    loads[0].wait()
    relative = rel_ref[...].astype(F32).T
    idx_ref[0:TOK, :] = relative[:, 0:128].astype(jnp.int32)
    idx_ref[TAIL : TAIL + 24, :] = pack_tail(relative[:, 128:TOK], 0).astype(jnp.int32)
    idx_ref[TAIL + 18 : ROWS, :] = jnp.full((ROWS - TAIL - 18, 128), -1, jnp.int32)
    low = (idx_ref[...] & 255).astype(F32).T
    for i in range(ROWS // 8):
        low_ref[i] = low[:, 8 * i : 8 * i + 8]
    loads[1].wait()
    tabf_ref[...] = jnp.zeros_like(tabf_ref)
    for b in range(2):
        for part in range(13):
            width = min(256, POS - 256 * part)
            tabf_ref[b, 8 * part : 8 * part + 6, 0:width] = table_ref[6 * b : 6 * b + 6, 0, 256 * part : 256 * part + width]
        table = tabf_ref[b]
        coarse = table.astype(BF)
        tab_ref[b, 0:104, :] = coarse
        tab_ref[b, 104:208, :] = (table - coarse.astype(F32)).astype(BF)
    gather_bias(0)
    for load in loads[2:]:
        load.wait()
    x_ref[0] = moved(onehot(TOK, TOK, 0), tok_ref[...].reshape(TOK, C))
    hs_ref[0] = moved(onehot(192, TOK, 10), gmix_ref[...].reshape(TOK, C)).reshape(4, 48, C)

    first = forward(0)
    hs_ref[1] = moved(onehot(192, TOK, 2), first).reshape(4, 48, C)
    pl.semaphore_wait(barrier, len(greeted))
    copies_x = send_quarters(1, ahead)
    copies_g = send_quarters(0, ahead)
    gather_bias(1)
    acc_ref[...] = jnp.zeros_like(acc_ref)
    arrive(copies_x)
    arrive(copies_g)
    come = onehot(TOK, 192, 3)
    x_ref[1] = moved(come, hr_ref[1].reshape(192, C))
    grad_shifted = moved(come, hr_ref[0].reshape(192, C))

    second = forward(1)
    hs_ref[2] = moved(onehot(192, TOK, 4), second).reshape(4, 48, C)
    grad_second, *rest = backward(1, grad_shifted)
    hs_ref[3] = moved(onehot(192, TOK, 4), grad_second).reshape(4, 48, C)
    copies_s = send_quarters(3, back)
    copies_m = send_quarters(2, back)
    copies_two = share_scores(1)
    weight_grads(1, *rest)
    sum_two = Sum(1)
    sum_two.next()

    arrive(copies_s)
    grad_first = moved(onehot(TOK, 192, 5), hr_ref[3].reshape(192, C))
    grad_in, *rest = backward(0, grad_first, sum_two.next)
    copies_one = share_scores(0)
    weight_grads(0, *rest)
    sum_one = Sum(0)
    sum_table = TableSum()
    sum_one.next()
    sum_two.next()
    add_scores(1, copies_two)
    add_scores(0, copies_one)
    fold_tables(0, 2)
    sum_one.next()
    fold_tables(2, 4)
    sum_table.next()
    sum_two.next()
    arrive(copies_m)
    mixed_ref[...] = moved(onehot(TOK, 192, 6), hr_ref[2].reshape(192, C)).reshape(72, 2, C)
    gtok_ref[...] = moved(onehot(TOK, TOK, 1), grad_in).reshape(72, 2, C)
    sum_table.next()
    sum_two.next()
    sum_table.next()
    sum_one.next()
    sum_table.next()
    sum_one.next()
    sum_table.next()
    sum_one.next()
    for copy in sent:
        copy.wait_send()


def finish(mixed_in, gtok_in, wg_in, table_in, mixed_ref, gtok_ref, qkv_ref, proj_ref, up_ref, down_ref, table_ref):
    mixed_ref[...] = mixed_in[...]
    gtok_ref[...] = gtok_in[...]
    for b in range(2):
        rows = wg_in[b].reshape(128, 128).astype(F32)
        qkv_ref[:, b, 0:128] = rows[0:18, :]
        qkv_ref[:, b, 128:C] = rows[48:66, 0:64]
        proj_ref[:, b, 0:128] = rows[18:24, :]
        proj_ref[:, b, 128:C] = rows[66:72, 0:64]
        up_ref[b, :, 0:128] = rows[24:48, :]
        up_ref[b, :, 128:C] = rows[48:72, 64:128]
        for i in range(6):
            down_ref[:, b, 128 * i : 128 * i + 128] = rows[72 + 8 * i : 78 + 8 * i, :]
    for part in range(26):
        tile = table_in[part // 16, part // 8 % 2, part % 8].astype(F32)
        width = min(128, POS - 128 * part)
        for b in range(2):
            table_ref[6 * b : 6 * b + 6, 0, 128 * part : 128 * part + width] = tile[8 * b : 8 * b + 6, 0:width]


def per_device(tokens, grad_mixed, w_qkv, w_proj, w_up, w_down, gains, bias_table, rel_index, mask_ids):
    n_lat, n_lon = lax.axis_size("lat"), lax.axis_size("lon")
    ny, nz, rows = n_lat // 2, n_lon // 4, 128 // n_lat
    vmem = pl.BlockSpec(memory_space=pltpu.VMEM)
    smem = pl.BlockSpec(memory_space=pltpu.SMEM)

    def buf(*shape, dtype=BF):
        return pltpu.VMEM(shape, dtype)

    scratch = [
        buf(TOK, TOK, dtype=jnp.int32), buf(12, 1, POS, dtype=F32), buf(16, 768, dtype=jnp.int32),
        buf(72, 2, C), buf(72, 2, C), buf(2, C, 3 * C), buf(2, C, C), buf(2, 2, C, dtype=F32), buf(2, C, 768), buf(2, C, 768),
        buf(3 * C, 768), buf(C, 768), buf(C, 256),
        pltpu.SemaphoreType.DMA((13,)),
        buf(2, TOK, C), buf(2, TOK, 3 * C), buf(2, 6 * TOK, C), buf(2, 6 * TOK, C), buf(6 * TOK, TOK, dtype=F32),
        buf(2, 6 * TOK, TOK), buf(2, TOK, C), buf(2, TOK, C, dtype=F32), buf(2, TOK, 1, dtype=F32), buf(2, TOK, C),
        buf(2, TOK, 768, dtype=F32), buf(2, TOK, 768), buf(2, TOK, C, dtype=F32), buf(2, TOK, 1, dtype=F32),
        buf(2, TOK, 768), buf(6 * TOK, TOK),
        buf(ROWS, 128, dtype=jnp.int32), buf(ROWS // 8, 128, 8, dtype=F32), buf(2, 104, 256, dtype=F32), buf(2, 208, 256),
        buf(8 * 168, 128, dtype=F32), buf(6, 192, 128, dtype=F32), buf(6, 192, 128, dtype=F32),
        buf(2, 8 * ROWS, 128, dtype=F32), buf(2, 4 * ROWS, 128), buf(2, 4 * ROWS, 128), buf(208, 256, dtype=F32),
        buf(3 * TOK, 768), buf(3 * TOK, 384), buf(768, 384, dtype=F32), buf(256, 768, dtype=F32),
        buf(4, 4, 48, C), buf(4, 4, 48, C),
        buf(2, 2, ny, 4, nz, rows, 128), buf(2, ny, 4, nz, rows, 128), buf(2, ny, 4, nz, rows, 128),
        buf(2, 4 * ny - 1, nz, rows, 128),
        buf(2, nz, rows, 128), buf(2, nz - 1, rows, 128), buf(2, rows, 128), buf(2, n_lat, rows, 128),
        buf(2, 2, 8, 16, 128), buf(3, 8, 16, 128), buf(8, 16, 128), buf(7, 16, 128), buf(16, 128),
        buf(8, 16, 128), buf(2, 2, 8, 16, 128),
        pltpu.SemaphoreType.DMA((N_SEMS,)), pltpu.SemaphoreType.DMA((N_SEMS,)),
    ]
    results = pl.pallas_call(
        functools.partial(kernel, n_lat, n_lon),
        out_shape=(
            jax.ShapeDtypeStruct((72, 2, C), BF),
            jax.ShapeDtypeStruct((72, 2, C), BF),
            jax.ShapeDtypeStruct((2, n_lat, rows, 128), BF),
            jax.ShapeDtypeStruct((2, 2, 8, 16, 128), BF),
        ),
        in_specs=[pl.BlockSpec(memory_space=pltpu.HBM)] * 13 + [smem],
        out_specs=[vmem] * 4,
        scratch_shapes=scratch,
        compiler_params=pltpu.CompilerParams(
            collective_id=0, has_side_effects=True, vmem_limit_bytes=60 * 1024 * 1024
        ),
    )(
        rel_index,
        bias_table.reshape(12, 1, POS),
        jnp.asarray(index_rows()),
        tokens.transpose(1, 2, 0, 3).reshape(72, 2, C),
        grad_mixed.transpose(1, 2, 0, 3).reshape(72, 2, C),
        w_qkv, w_proj, gains, w_up, w_down.transpose(0, 2, 1),
        *permutations(),
        mask_ids,
    )
    mixed, grad_tokens, qkv, proj, up, down, table = pl.pallas_call(
        finish,
        out_shape=(
            jax.ShapeDtypeStruct((72, 2, C), BF),
            jax.ShapeDtypeStruct((72, 2, C), BF),
            jax.ShapeDtypeStruct((18, 2, C), F32),
            jax.ShapeDtypeStruct((6, 2, C), F32),
            jax.ShapeDtypeStruct((2, 24, C), F32),
            jax.ShapeDtypeStruct((6, 2, 768), F32),
            jax.ShapeDtypeStruct((12, 1, POS), F32),
        ),
        in_specs=[vmem] * 4,
        out_specs=[vmem] * 7,
        compiler_params=pltpu.CompilerParams(vmem_limit_bytes=60 * 1024 * 1024),
    )(*results)

    def field(value):
        return value.reshape(6, 12, 2, C).transpose(2, 0, 1, 3)

    return (
        field(mixed),
        field(grad_tokens),
        qkv.transpose(1, 2, 0),
        proj.transpose(1, 2, 0),
        up.transpose(0, 2, 1),
        down.transpose(1, 2, 0),
        table.reshape(2, 1, 1, 6, POS),
    )


def solution(mesh):
    field = P(None, "lat", "lon", None)
    table = P(None, None, "lat", None, None)
    in_specs = (field, field, P(), P(), P(), P(), P(), table, P(), P("lat"))
    columns = P(None, None, "lon")
    out_specs = (field, field, columns, columns, columns, columns, table)
    return jax.shard_map(per_device, mesh=mesh, in_specs=in_specs, out_specs=out_specs, check_vma=False)
```

```python
import functools

import jax
import jax.numpy as jnp
import numpy as np
from jax import lax
from jax.experimental import pallas as pl
from jax.experimental.pallas import tpu as pltpu
from jax.sharding import PartitionSpec as P

HEADS = 6
C = 192
TOK = 144
POS = 3312
EPS = 1e-05
NEGATIVE = -1e30
SCALE = 32 ** -0.5
BF = jnp.bfloat16
F32 = jnp.float32
MESH = pl.DeviceIdType.MESH
ROWS = 192
TAIL = 144
N_SEMS = 132


def index_rows():
    rows = np.full((16, 768), -1, np.int32)
    tok = np.arange(TOK)
    level, row, col = tok // 72, tok // 12 % 6, tok % 12
    place = 24 * row + 2 * col + level
    own = 18 * level + row % 3 * 6 + col % 6
    other = 18 * (1 - level) + row % 3 * 6 + col % 6
    low = 48 * (2 * (row // 3) + col // 6)
    high = 48 * (2 * (1 - row // 3) + 1 - col // 6)
    rows[0, place] = tok
    rows[1, tok] = place
    rows[2, tok] = high + own
    rows[3, low + other] = tok
    rows[4, tok] = low + own
    rows[5, high + other] = tok
    rows[6, high + other] = place
    rows[10, place] = high + own
    return rows


def permutations():
    qkv = np.zeros((3 * C, 768), np.float32)
    proj = np.zeros((C, 768), np.float32)
    down = np.zeros((C, 256), np.float32)
    for piece in range(32):
        for i in range(18):
            qkv[18 * piece + i, 24 * piece + i] = 1
        for i in range(6):
            proj[6 * piece + i, 24 * piece + 18 + i] = 1
            down[6 * piece + i, 8 * piece + i] = 1
    return tuple(jnp.asarray(matrix, BF) for matrix in (qkv, proj, down))


def dot(a, b):
    return jnp.dot(a, b, preferred_element_type=F32)


def dot_nt(a, b):
    return lax.dot_general(a, b, (((1,), (1,)), ((), ())), preferred_element_type=F32)


def dot_tn(a, b):
    return lax.dot_general(a, b, (((0,), (0,)), ((), ())), preferred_element_type=F32)


def norm_parts(v):
    center = v - jnp.mean(v, axis=-1, keepdims=True)
    spread = jnp.mean(center * center, axis=-1, keepdims=True)
    inverse = lax.rsqrt(spread + EPS)
    return center * inverse, inverse


def norm_back(grad, unit, inverse):
    along = jnp.mean(grad * unit, axis=-1, keepdims=True)
    return inverse * (grad - jnp.mean(grad, axis=-1, keepdims=True) - unit * along)


def kernel(
    n_lat, n_lon,
    rel_hbm, table_hbm, const_hbm, tok_hbm, gmix_hbm, wqkv_hbm, wproj_hbm, gains_hbm, wup_hbm, wdown_hbm, pq_hbm, pp_hbm, pd_hbm, ids_ref,
    mixed_ref, gtok_ref, wg_ref, tgrad_ref,
    rel_ref, table_ref, const_ref, tok_ref, gmix_ref, wqkv_ref, wproj_ref, gains_ref, wup_ref, wdown_ref, pq_ref, pp_ref, pd_ref, load_sem,
    x_ref, qkv_ref, km_ref, vm_ref, s_ref, p_ref, att_ref, u1_ref, i1_ref, mid_ref, gp_ref, hid_ref, u2_ref, i2_ref,
    gup_ref, ds_ref, idx_ref, low_ref, tabf_ref, tab_ref, bias_ref, btail_ref, pk_ref, gall_ref, gsend_ref, grecv_ref, acc_ref,
    l_ref, r_ref, o1_ref, o2_ref, o3_ref,
    hs_ref, hr_ref,
    second_refs, early_refs, late_refs,
    tb_ref, tr1_ref, t1_ref, tr2_ref, t2_ref, t3_ref, t4_ref,
    ssem, rsem,
):
    loads = [
        pltpu.make_async_copy(src, dst, load_sem.at[k])
        for k, (src, dst) in enumerate([
            (rel_hbm, rel_ref), (table_hbm, table_ref), (const_hbm, const_ref), (tok_hbm, tok_ref), (gmix_hbm, gmix_ref),
            (wqkv_hbm, wqkv_ref), (wproj_hbm, wproj_ref), (gains_hbm, gains_ref), (wup_hbm, wup_ref), (wdown_hbm, wdown_ref),
            (pq_hbm, pq_ref), (pp_hbm, pp_ref), (pd_hbm, pd_ref),
        ])
    ]
    for load in loads:
        load.start()
    ny, nz = n_lat // 2, n_lon // 4
    lat, lon = lax.axis_index("lat"), lax.axis_index("lon")
    y, xh = lat // 2, lat % 2
    z, xl, co = lon // 4, lon // 2 % 2, lon % 2
    x = xh * 2 + xl
    lon_pair = [
        (z * 4 + ((xl + (k >> 1)) % 2) * 2 + (co + (k & 1)) % 2, (xl + (k >> 1)) % 2, (co + (k & 1)) % 2)
        for k in range(4)
    ]
    ahead = [((lat + n_lat - a) % n_lat, (lon + n_lon - b) % n_lon) for a in (0, 1) for b in (0, 1)]
    back = [((lat + a) % n_lat, (lon + b) % n_lon) for a in (0, 1) for b in (0, 1)]
    z_lons = [(z + k) % nz * 4 + xl * 2 + co for k in range(nz)]

    greeted = [((lat + k) % n_lat, lon) for k in range(1, n_lat)]
    greeted += [(lat, z_lons[k]) for k in range(1, nz)]
    greeted += [(lat, lon_pair[k][0]) for k in (1, 3)]
    greeted += [((lat + k) % n_lat, lon_pair[2][0]) for k in range(n_lat)]
    greeted += [ahead[1], ahead[3], back[1], back[3]]
    barrier = pltpu.get_barrier_semaphore()
    for device in greeted:
        pl.semaphore_signal(barrier, inc=1, device_id=device, device_id_type=MESH)

    sems = iter(range(N_SEMS))
    sent = []

    def push(src, dst, device):
        k = next(sems)
        copy = pltpu.make_async_remote_copy(
            src_ref=src, dst_ref=dst, send_sem=ssem.at[k], recv_sem=rsem.at[k], device_id=device, device_id_type=MESH
        )
        copy.start()
        sent.append(copy)
        return copy

    def arrive(copies):
        for copy in copies:
            copy.wait_recv()

    def onehot(n_rows, n_lanes, which):
        place = lax.broadcasted_iota(jnp.int32, (n_rows, n_lanes), 0)
        return jnp.where(place == const_ref[which : which + 1, :n_lanes], 1.0, 0.0).astype(BF)

    def moved(matrix, value):
        return dot(matrix, value).astype(BF)

    lane = lax.broadcasted_iota(jnp.int32, (1, C), 1)
    head_lanes = [(lane >= 32 * h) & (lane < 32 * h + 32) for h in range(HEADS)]

    def of_head(value, h):
        return jnp.where(head_lanes[h], value, jnp.zeros_like(value))

    def pack_tail(value, h):
        pk_ref[h, 0:TOK, 0:16] = value
        total = pk_ref[h, pl.ds(0, 24, stride=8), :]
        for j in range(1, 8):
            total = total + pltpu.roll(pk_ref[h, pl.ds(j, 24, stride=8), :], 16 * j, 1)
        return total

    def unpack_tail(value, k):
        for j in range(8):
            rolled = pltpu.roll(value, (128 - 16 * j) % 128, 1)
            btail_ref[k, pl.ds(j, 24, stride=8), :] = rolled

    def gather_bias(b):
        place = lax.broadcasted_iota(jnp.int32, (256, 128), 0).astype(BF)
        one, zero = jnp.ones((256, 128), BF), jnp.zeros((256, 128), BF)

        def step(i, carry):
            for m in range(3):
                group = i * 3 + m
                index = idx_ref[pl.ds(pl.multiple_of(group * 8, 8), 8), :]
                low, high = (index & 255).astype(F32), index >> 8
                picks = []
                for r in range(8):
                    row = jnp.broadcast_to(low[r : r + 1, :], (16, 128)).astype(BF)
                    picks.append(jnp.where(place == jnp.concatenate([row] * 16, axis=0), one, zero))
                rows = dot(tab_ref[b], jnp.concatenate(picks, axis=1))
                for r in range(8):
                    high_row = jnp.broadcast_to(high[r : r + 1, :], (8, 128))
                    found = jnp.zeros((8, 128), F32)
                    for part in range(13):
                        coarse = rows[8 * part : 8 * part + 8, 128 * r : 128 * r + 128]
                        fine = rows[104 + 8 * part : 112 + 8 * part, 128 * r : 128 * r + 128]
                        found = jnp.where(high_row == part, coarse + fine, found)
                    bias_ref[pl.ds(pl.multiple_of(group * 64 + r * 8, 8), 8), :] = found
            return carry

        lax.fori_loop(0, 7, step, 0)
        for h in range(HEADS):
            unpack_tail(bias_ref[pl.ds(8 * TAIL + h, 24, stride=8), :], h)

    half = ROWS // 2

    def share_scores(b):
        gsend_ref[b] = gall_ref[b, pl.ds((1 - co) * 8 * half, 8 * half), :].astype(BF)
        return [push(gsend_ref.at[b], grecv_ref.at[b], (lat, lon + 1 - 2 * co))]

    def add_scores(b, copies):
        arrive(copies)
        mine = pl.ds(co * 8 * half, 8 * half)
        gall_ref[b, mine, :] = gall_ref[b, mine, :] + grecv_ref[b].astype(F32)

    def fold_tables(start, stop):
        place = lax.broadcasted_iota(jnp.int32, (128, 256), 1).astype(BF)
        one, zero = jnp.ones((128, 256), BF), jnp.zeros((128, 256), BF)

        def step(i, carry):
            total = acc_ref[...]
            for m in range(3):
                group = co * (half // 8) + i * 3 + m
                high = idx_ref[pl.ds(pl.multiple_of(group * 8, 8), 8), :] >> 8
                block = low_ref[group]
                left, right = [[] for _ in range(26)], []
                for r in range(8):
                    high_row = jnp.broadcast_to(high[r : r + 1, :], (8, 128))
                    hits = [high_row == part for part in range(13)]
                    for b in range(2):
                        grads = gall_ref[b, pl.ds(pl.multiple_of(group * 64 + r * 8, 8), 8), :]
                        for part in range(13):
                            left[13 * b + part].append(jnp.where(hits[part], grads, 0.0))
                    column = jnp.broadcast_to(block[:, r : r + 1], (128, 128)).astype(BF)
                    right.append(jnp.where(place == jnp.concatenate([column] * 2, axis=1), one, zero))
                left = jnp.concatenate([jnp.concatenate(rows, axis=1) for rows in left], axis=0).astype(BF)
                total = total + dot(left, jnp.concatenate(right, axis=0))
            acc_ref[...] = total
            return carry

        lax.fori_loop(start, stop, step, 0)

    def region_codes(place):
        code = jnp.zeros_like(place)
        for part in range(12):
            value = ids_ref[part % 6] + 64 * (part // 6)
            code = jnp.where(place >= 12 * part, value, code)
        return code

    def forward(b):
        tokens = x_ref[b]
        qkv_ref[b] = dot(tokens, wqkv_ref[b]).astype(BF)
        q, k, v = (qkv_ref[b, :, C * i : C * i + C] for i in range(3))
        for h in range(HEADS):
            km_ref[b, TOK * h : TOK * h + TOK, :] = of_head(k, h)
            vm_ref[b, TOK * h : TOK * h + TOK, :] = of_head(v, h)
        s_ref[...] = dot_nt(km_ref[b], q)
        if b == 1:
            codes_t = region_codes(lax.broadcasted_iota(jnp.int32, (TOK, 1), 0))
            codes_s = region_codes(lax.broadcasted_iota(jnp.int32, (1, TOK), 1))
            allowed = codes_s == codes_t
        for h in range(HEADS):
            span = pl.ds(TOK * h, TOK)
            bias = jnp.concatenate([bias_ref[pl.ds(h, TOK, stride=8), :], btail_ref[h, 0:TOK, 0:16]], axis=1)
            scores = s_ref[span, :] * SCALE + bias
            if b == 1:
                scores = jnp.where(allowed, scores, NEGATIVE)
            powers = jnp.exp(scores - jnp.max(scores, axis=0, keepdims=True))
            probs = powers * (1.0 / jnp.sum(powers, axis=0, keepdims=True))
            p_ref[b, span, :] = probs.astype(BF)
        attended = dot_tn(p_ref[b], vm_ref[b]).astype(BF)
        att_ref[b] = attended
        unit, inverse = norm_parts(dot(attended, wproj_ref[b]))
        u1_ref[b], i1_ref[b] = unit, inverse
        middle = (tokens.astype(F32) + unit * gains_ref[b, 0:1, :]).astype(BF)
        mid_ref[b] = middle
        for part in range(3):
            cols = pl.ds(256 * part, 256)
            up = dot(middle, wup_ref[b, :, cols])
            phi = 0.5 + 0.5 * lax.erf(up * (0.5**0.5))
            hid_ref[b, :, cols] = (up * phi).astype(BF)
            gp_ref[b, :, cols] = phi + up * (0.3989422804014327 * jnp.exp(-0.5 * up * up))
        unit, inverse = norm_parts(dot_nt(hid_ref[b], wdown_ref[b]))
        u2_ref[b], i2_ref[b] = unit, inverse
        return (middle.astype(F32) + unit * gains_ref[b, 1:2, :]).astype(BF)

    def backward(b, grad, after_up=lambda grad_down: None, after_scores=lambda: None):
        grad = grad.astype(F32)
        grad_down = norm_back(grad * gains_ref[b, 1:2, :], u2_ref[b], i2_ref[b]).astype(BF)
        for part in range(3):
            cols = pl.ds(256 * part, 256)
            grad_hidden = dot(grad_down, wdown_ref[b, :, cols])
            gup_ref[b, :, cols] = (grad_hidden * gp_ref[b, :, cols]).astype(BF)
        grad_middle = grad + dot_nt(gup_ref[b], wup_ref[b])
        after_up(grad_down)
        grad_pre = norm_back(grad_middle * gains_ref[b, 0:1, :], u1_ref[b], i1_ref[b]).astype(BF)
        grad_att = dot_nt(grad_pre, wproj_ref[b]).astype(BF)
        q = qkv_ref[b, :, 0:C]
        s_ref[...] = dot_nt(vm_ref[b], grad_att)
        for h in range(HEADS):
            span = pl.ds(TOK * h, TOK)
            probs = p_ref[b, span, :].astype(F32)
            grad_probs = s_ref[span, :]
            grad_scores = probs * (grad_probs - jnp.sum(grad_probs * probs, axis=0, keepdims=True))
            ds_ref[span, :] = grad_scores.astype(BF)
            gall_ref[b, pl.ds(h, TOK, stride=8), :] = grad_scores[:, 0:128]
            gall_ref[b, pl.ds(8 * TAIL + h, 24, stride=8), :] = pack_tail(grad_scores[:, 128:TOK], h)
        after_scores()
        grad_q = dot_tn(ds_ref[...], km_ref[b])
        grad_k, grad_v = jnp.zeros((TOK, C), F32), jnp.zeros((TOK, C), F32)
        for h in range(HEADS):
            span = pl.ds(TOK * h, TOK)
            grad_k = jnp.where(head_lanes[h], dot(ds_ref[span, :], q), grad_k)
            grad_v = jnp.where(head_lanes[h], dot(p_ref[b, span, :], grad_att), grad_v)
        grad_qkv = jnp.concatenate([grad_q * SCALE, grad_k * SCALE, grad_v], axis=1).astype(BF)
        grad_in = (grad_middle + dot_nt(grad_qkv, wqkv_ref[b])).astype(BF)
        return grad_in, grad_down, grad_pre, grad_qkv

    def pack(buffer, piece, first_row, units):
        z_of = piece // 4
        for tile in range(len(units) // 2):
            pair = jnp.concatenate([units[2 * tile], units[2 * tile + 1]], axis=0).astype(BF)
            row = first_row + 16 * tile
            buffer[piece % 2, z_of // 2, z_of % 2 * 2 + piece // 2 % 2, row : row + 16, :] = pair

    def early_grads(b, grad_down, buffer):
        o2_ref[...] = dot_tn(gup_ref[b], mid_ref[b, :, 0:128])
        o3_ref[...] = dot_tn(moved(grad_down, pd_ref[...]), hid_ref[b])
        for piece in range(32):
            units = [o2_ref[24 * piece + 8 * i : 24 * piece + 8 * i + 8, :] for i in range(3)]
            units += [o3_ref[8 * piece : 8 * piece + 8, 128 * i : 128 * i + 128] for i in range(6)]
            pack(buffer, piece, 0, units + [jnp.zeros((8, 128), F32)])

    def late_grads(b, grad_pre, grad_qkv, buffer, first_row):
        l_ref[0:TOK, :] = moved(grad_qkv, pq_ref[...])
        l_ref[TOK : 2 * TOK, :] = moved(grad_pre, pp_ref[...])
        l_ref[2 * TOK : 3 * TOK, :] = gup_ref[b]
        r_ref[0:TOK, 0:192] = x_ref[b]
        r_ref[TOK : 2 * TOK, 0:192] = att_ref[b]
        r_ref[2 * TOK : 3 * TOK, 192:256] = mid_ref[b, :, 128:C]
        o1_ref[...] = dot_tn(l_ref[...], r_ref[...])
        for piece in range(32):
            units = [o1_ref[24 * piece + 8 * i : 24 * piece + 8 * i + 8, 128 * m : 128 * m + 128] for m in range(2) for i in range(3)]
            pack(buffer, piece, first_row, units)

    class Sum:
        def __init__(self, refs, out):
            self.sb, self.rc, self.wa, self.rx, self.wc, self.rz, self.wl = refs
            self.out = out
            self.copies = []
            self.steps = [self.core, self.along_xy, self.along_z, self.share, self.done]
            self.z_sems = [next(sems) for _ in range(nz - 1)]
            self.lat_sems = [next(sems) for _ in range(n_lat - 1)]

        def next(self):
            if self.steps:
                self.steps.pop(0)()

        def core(self):
            self.copies = [push(self.sb.at[1 - co], self.rc, (lat, lon + 1 - 2 * co))]

        def along_xy(self):
            arrive(self.copies)
            self.wa[...] = (self.sb[co].astype(F32) + self.rc[...].astype(F32)).astype(BF)
            self.copies = []
            for k in range(1, 4 * ny):
                its_y, its_x = (y + k // 4) % ny, (x + k % 4) % 4
                device = (its_y * 2 + its_x // 2, z * 4 + its_x % 2 * 2 + co)
                self.copies.append(push(self.wa.at[its_y, its_x], self.rx.at[k - 1], device))

        def to_owner(self):
            slot = (z + nz - lat) % nz - 1
            return pltpu.make_async_remote_copy(
                src_ref=self.wc, dst_ref=self.rz.at[slot], send_sem=ssem.at[self.z_sems[0]],
                recv_sem=rsem.at[self.z_sems[0] + slot], device_id=(lat, lat * 4 + xl * 2 + co), device_id_type=MESH,
            )

        def from_z(self, k):
            return pltpu.make_async_remote_copy(
                src_ref=self.wc, dst_ref=self.rz.at[k - 1], send_sem=ssem.at[self.z_sems[0]],
                recv_sem=rsem.at[self.z_sems[k - 1]], device_id=(lat, z_lons[k]), device_id_type=MESH,
            )

        def to_lat(self, k):
            return pltpu.make_async_remote_copy(
                src_ref=self.wl, dst_ref=self.wl, send_sem=ssem.at[self.lat_sems[k - 1]],
                recv_sem=rsem.at[self.lat_sems[0]], device_id=((lat + k) % n_lat, lon), device_id_type=MESH,
            )

        def along_z(self):
            arrive(self.copies)
            total = self.wa[y, x].astype(F32)
            for k in range(4 * ny - 1):
                total = total + self.rx[k].astype(F32)
            self.wc[...] = total.astype(BF)

            @pl.when(z != lat)
            def _():
                self.to_owner().start()

        def share(self):
            @pl.when(z == lat)
            def _():
                total = self.wc[...].astype(F32)
                for k in range(1, nz):
                    self.from_z(k).wait_recv()
                    total = total + self.rz[k - 1].astype(F32)
                self.wl[...] = total.astype(BF)
                for k in range(1, n_lat):
                    self.to_lat(k).start()

        def done(self):
            @pl.when(z != lat)
            def _():
                self.to_lat(1).wait_recv()
                self.to_owner().wait_send()

            self.out[...] = self.wl[...]

            @pl.when(z == lat)
            def _():
                for k in range(1, n_lat):
                    self.to_lat(k).wait_send()

    class TableSum:
        def __init__(self):
            self.copies = []
            self.steps = [self.pair, self.along_z, self.share_z, self.share_pair, self.done]

        def next(self):
            if self.steps:
                self.steps.pop(0)()

        def pair(self):
            for part in range(26):
                row, lanes = 8 * (part // 2), slice(128 * (part % 2), 128 * (part % 2) + 128)
                both = jnp.concatenate([acc_ref[row : row + 8, lanes], acc_ref[104 + row : 112 + row, lanes]], axis=0)
                tb_ref[part // 16, part // 8 % 2, part % 8] = both.astype(BF)
            for part in range(26, 32):
                tb_ref[part // 16, part // 8 % 2, part % 8] = jnp.zeros((16, 128), BF)
            for k in range(1, 4):
                device, its_xl, its_co = lon_pair[k]
                self.copies.append(push(tb_ref.at[its_co, its_xl], tr1_ref.at[k - 1], (lat, device)))

        def along_z(self):
            arrive(self.copies)
            total = tb_ref[co, xl].astype(F32)
            for k in range(3):
                total = total + tr1_ref[k].astype(F32)
            t1_ref[...] = total.astype(BF)
            self.copies = []
            for k in range(1, nz):
                self.copies.append(push(t1_ref.at[(z + k) % nz], tr2_ref.at[k - 1], (lat, z_lons[k])))

        def share_z(self):
            arrive(self.copies)
            total = t1_ref[z].astype(F32)
            for k in range(nz - 1):
                total = total + tr2_ref[k].astype(F32)
            t2_ref[...] = total.astype(BF)
            self.copies = []
            for k in range(1, nz):
                self.copies.append(push(t2_ref, t3_ref.at[z], (lat, z_lons[k])))
            t3_ref[z] = t2_ref[...]

        def share_pair(self):
            arrive(self.copies)
            self.copies = []
            for k in range(1, 4):
                self.copies.append(push(t3_ref, t4_ref.at[co, xl], (lat, lon_pair[k][0])))
            t4_ref[co, xl] = t3_ref[...]

        def done(self):
            arrive(self.copies)
            tgrad_ref[...] = t4_ref[...]

    def send_quarters(which, devices):
        copies = []
        for quarter in range(1, 4):
            copies.append(push(hs_ref.at[which, quarter], hr_ref.at[which, quarter], devices[quarter]))
        hr_ref[which, 0] = hs_ref[which, 0]
        return copies

    pk_ref[...] = jnp.zeros_like(pk_ref)
    gall_ref[...] = jnp.zeros_like(gall_ref)
    r_ref[...] = jnp.zeros_like(r_ref)
    loads[0].wait()
    relative = rel_ref[...].astype(F32).T
    idx_ref[0:TOK, :] = relative[:, 0:128].astype(jnp.int32)
    idx_ref[TAIL : TAIL + 24, :] = pack_tail(relative[:, 128:TOK], 0).astype(jnp.int32)
    idx_ref[TAIL + 18 : ROWS, :] = jnp.full((ROWS - TAIL - 18, 128), -1, jnp.int32)
    low = (idx_ref[...] & 255).astype(F32).T
    for i in range(ROWS // 8):
        low_ref[i] = low[:, 8 * i : 8 * i + 8]
    loads[1].wait()
    tabf_ref[...] = jnp.zeros_like(tabf_ref)
    for b in range(2):
        for part in range(13):
            width = min(256, POS - 256 * part)
            tabf_ref[b, 8 * part : 8 * part + 6, 0:width] = table_ref[6 * b : 6 * b + 6, 0, 256 * part : 256 * part + width]
        table = tabf_ref[b]
        coarse = table.astype(BF)
        tab_ref[b, 0:104, :] = coarse
        tab_ref[b, 104:208, :] = (table - coarse.astype(F32)).astype(BF)
    gather_bias(0)
    for load in loads[2:]:
        load.wait()
    x_ref[0] = moved(onehot(TOK, TOK, 0), tok_ref[...].reshape(TOK, C))
    hs_ref[0] = moved(onehot(192, TOK, 10), gmix_ref[...].reshape(TOK, C)).reshape(4, 48, C)

    first = forward(0)
    hs_ref[1] = moved(onehot(192, TOK, 2), first).reshape(4, 48, C)
    pl.semaphore_wait(barrier, len(greeted))
    copies_x = send_quarters(1, ahead)
    copies_g = send_quarters(0, ahead)
    gather_bias(1)
    acc_ref[...] = jnp.zeros_like(acc_ref)
    arrive(copies_x)
    arrive(copies_g)
    come = onehot(TOK, 192, 3)
    x_ref[1] = moved(come, hr_ref[1].reshape(192, C))
    grad_shifted = moved(come, hr_ref[0].reshape(192, C))

    second = forward(1)
    hs_ref[2] = moved(onehot(192, TOK, 4), second).reshape(4, 48, C)
    grad_second, *rest = backward(1, grad_shifted)
    hs_ref[3] = moved(onehot(192, TOK, 4), grad_second).reshape(4, 48, C)
    copies_s = send_quarters(3, back)
    copies_m = send_quarters(2, back)
    copies_two = share_scores(1)
    grad_down, grad_pre, grad_qkv = rest
    early_grads(1, grad_down, second_refs[0])
    late_grads(1, grad_pre, grad_qkv, second_refs[0], 80)
    sum_two = Sum(second_refs, wg_ref.at[1])
    sum_early = Sum(early_refs, wg_ref.at[0, 0:80])
    sum_late = Sum(late_refs, wg_ref.at[0, 80:128])
    sum_two.next()

    arrive(copies_s)
    grad_first = moved(onehot(TOK, 192, 5), hr_ref[3].reshape(192, C))
    def after_up(grad_down):
        sum_two.next()
        early_grads(0, grad_down, early_refs[0])
        sum_early.next()

    copies_one = []

    def after_scores():
        copies_one.extend(share_scores(0))
        sum_early.next()

    grad_in, _, grad_pre, grad_qkv = backward(0, grad_first, after_up, after_scores)
    add_scores(1, copies_two)
    add_scores(0, copies_one)
    fold_tables(0, 4)
    sum_table = TableSum()
    sum_table.next()
    late_grads(0, grad_pre, grad_qkv, late_refs[0], 0)
    sum_late.next()
    sum_two.next()
    sum_table.next()
    sum_late.next()
    arrive(copies_m)
    mixed_ref[...] = moved(onehot(TOK, 192, 6), hr_ref[2].reshape(192, C)).reshape(72, 2, C)
    gtok_ref[...] = moved(onehot(TOK, TOK, 1), grad_in).reshape(72, 2, C)
    sum_early.next()
    sum_table.next()
    sum_two.next()
    sum_late.next()
    sum_table.next()
    sum_early.next()
    sum_late.next()
    sum_table.next()
    sum_two.next()
    sum_early.next()
    sum_late.next()
    for copy in sent:
        copy.wait_send()


def finish(mixed_in, gtok_in, wg_in, table_in, mixed_ref, gtok_ref, qkv_ref, proj_ref, up_ref, down_ref, table_ref):
    mixed_ref[...] = mixed_in[...]
    gtok_ref[...] = gtok_in[...]
    for b in range(2):
        rows = wg_in[b].astype(F32)
        up_ref[b, :, 0:128] = rows[0:24, :]
        up_ref[b, :, 128:C] = rows[104:128, 64:128]
        qkv_ref[:, b, 0:128] = rows[80:98, :]
        qkv_ref[:, b, 128:C] = rows[104:122, 0:64]
        proj_ref[:, b, 0:128] = rows[98:104, :]
        proj_ref[:, b, 128:C] = rows[122:128, 0:64]
        for i in range(6):
            down_ref[:, b, 128 * i : 128 * i + 128] = rows[24 + 8 * i : 30 + 8 * i, :]
    for part in range(26):
        tile = table_in[part // 16, part // 8 % 2, part % 8].astype(F32)
        width = min(128, POS - 128 * part)
        for b in range(2):
            table_ref[6 * b : 6 * b + 6, 0, 128 * part : 128 * part + width] = tile[8 * b : 8 * b + 6, 0:width]


def per_device(tokens, grad_mixed, w_qkv, w_proj, w_up, w_down, gains, bias_table, rel_index, mask_ids):
    n_lat, n_lon = lax.axis_size("lat"), lax.axis_size("lon")
    ny, nz = n_lat // 2, n_lon // 4
    vmem = pl.BlockSpec(memory_space=pltpu.VMEM)
    smem = pl.BlockSpec(memory_space=pltpu.SMEM)

    def buf(*shape, dtype=BF):
        return pltpu.VMEM(shape, dtype)

    def stream(rows):
        return (
            buf(2, ny, 4, rows, 128), buf(ny, 4, rows, 128), buf(ny, 4, rows, 128), buf(4 * ny - 1, rows, 128),
            buf(rows, 128), buf(nz - 1, rows, 128), buf(rows, 128),
        )

    scratch = [
        buf(TOK, TOK, dtype=jnp.int32), buf(12, 1, POS, dtype=F32), buf(16, 768, dtype=jnp.int32),
        buf(72, 2, C), buf(72, 2, C), buf(2, C, 3 * C), buf(2, C, C), buf(2, 2, C, dtype=F32), buf(2, C, 768), buf(2, C, 768),
        buf(3 * C, 768), buf(C, 768), buf(C, 256),
        pltpu.SemaphoreType.DMA((13,)),
        buf(2, TOK, C), buf(2, TOK, 3 * C), buf(2, 6 * TOK, C), buf(2, 6 * TOK, C), buf(6 * TOK, TOK, dtype=F32),
        buf(2, 6 * TOK, TOK), buf(2, TOK, C), buf(2, TOK, C, dtype=F32), buf(2, TOK, 1, dtype=F32), buf(2, TOK, C),
        buf(2, TOK, 768, dtype=F32), buf(2, TOK, 768), buf(2, TOK, C, dtype=F32), buf(2, TOK, 1, dtype=F32),
        buf(2, TOK, 768), buf(6 * TOK, TOK),
        buf(ROWS, 128, dtype=jnp.int32), buf(ROWS // 8, 128, 8, dtype=F32), buf(2, 104, 256, dtype=F32), buf(2, 208, 256),
        buf(8 * 168, 128, dtype=F32), buf(6, 192, 128, dtype=F32), buf(6, 192, 128, dtype=F32),
        buf(2, 8 * ROWS, 128, dtype=F32), buf(2, 4 * ROWS, 128), buf(2, 4 * ROWS, 128), buf(208, 256, dtype=F32),
        buf(3 * TOK, 768), buf(3 * TOK, 256), buf(768, 256, dtype=F32), buf(768, 128, dtype=F32), buf(256, 768, dtype=F32),
        buf(4, 4, 48, C), buf(4, 4, 48, C),
        stream(128), stream(80), stream(48),
        buf(2, 2, 8, 16, 128), buf(3, 8, 16, 128), buf(8, 16, 128), buf(7, 16, 128), buf(16, 128),
        buf(8, 16, 128), buf(2, 2, 8, 16, 128),
        pltpu.SemaphoreType.DMA((N_SEMS,)), pltpu.SemaphoreType.DMA((N_SEMS,)),
    ]
    results = pl.pallas_call(
        functools.partial(kernel, n_lat, n_lon),
        out_shape=(
            jax.ShapeDtypeStruct((72, 2, C), BF),
            jax.ShapeDtypeStruct((72, 2, C), BF),
            jax.ShapeDtypeStruct((2, 128, 128), BF),
            jax.ShapeDtypeStruct((2, 2, 8, 16, 128), BF),
        ),
        in_specs=[pl.BlockSpec(memory_space=pltpu.HBM)] * 13 + [smem],
        out_specs=[vmem] * 4,
        scratch_shapes=scratch,
        compiler_params=pltpu.CompilerParams(
            collective_id=0, has_side_effects=True, vmem_limit_bytes=60 * 1024 * 1024
        ),
    )(
        rel_index,
        bias_table.reshape(12, 1, POS),
        jnp.asarray(index_rows()),
        tokens.transpose(1, 2, 0, 3).reshape(72, 2, C),
        grad_mixed.transpose(1, 2, 0, 3).reshape(72, 2, C),
        w_qkv, w_proj, gains, w_up, w_down.transpose(0, 2, 1),
        *permutations(),
        mask_ids,
    )
    mixed, grad_tokens, qkv, proj, up, down, table = pl.pallas_call(
        finish,
        out_shape=(
            jax.ShapeDtypeStruct((72, 2, C), BF),
            jax.ShapeDtypeStruct((72, 2, C), BF),
            jax.ShapeDtypeStruct((18, 2, C), F32),
            jax.ShapeDtypeStruct((6, 2, C), F32),
            jax.ShapeDtypeStruct((2, 24, C), F32),
            jax.ShapeDtypeStruct((6, 2, 768), F32),
            jax.ShapeDtypeStruct((12, 1, POS), F32),
        ),
        in_specs=[vmem] * 4,
        out_specs=[vmem] * 7,
        compiler_params=pltpu.CompilerParams(vmem_limit_bytes=60 * 1024 * 1024),
    )(*results)

    def field(value):
        return value.reshape(6, 12, 2, C).transpose(2, 0, 1, 3)

    return (
        field(mixed),
        field(grad_tokens),
        qkv.transpose(1, 2, 0),
        proj.transpose(1, 2, 0),
        up.transpose(0, 2, 1),
        down.transpose(1, 2, 0),
        table.reshape(2, 1, 1, 6, POS),
    )


def solution(mesh):
    field = P(None, "lat", "lon", None)
    table = P(None, None, "lat", None, None)
    in_specs = (field, field, P(), P(), P(), P(), P(), table, P(), P("lat"))
    columns = P(None, None, "lon")
    out_specs = (field, field, columns, columns, columns, columns, table)
    return jax.shard_map(per_device, mesh=mesh, in_specs=in_specs, out_specs=out_specs, check_vma=False)
```

```python
import functools

import jax
import jax.numpy as jnp
import numpy as np
from jax import lax
from jax.experimental import pallas as pl
from jax.experimental.pallas import tpu as pltpu
from jax.sharding import PartitionSpec as P

HEADS = 6
C = 192
TOK = 144
POS = 3312
EPS = 1e-05
NEGATIVE = -1e30
SCALE = 32 ** -0.5
BF = jnp.bfloat16
F32 = jnp.float32
MESH = pl.DeviceIdType.MESH
ROWS = 192
TAIL = 144
N_SEMS = 132


def index_rows():
    rows = np.full((16, 768), -1, np.int32)
    tok = np.arange(TOK)
    level, row, col = tok // 72, tok // 12 % 6, tok % 12
    place = 24 * row + 2 * col + level
    own = 18 * level + row % 3 * 6 + col % 6
    other = 18 * (1 - level) + row % 3 * 6 + col % 6
    low = 48 * (2 * (row // 3) + col // 6)
    high = 48 * (2 * (1 - row // 3) + 1 - col // 6)
    rows[0, place] = tok
    rows[1, tok] = place
    rows[2, tok] = high + own
    rows[3, low + other] = tok
    rows[4, tok] = low + own
    rows[5, high + other] = tok
    rows[6, high + other] = place
    rows[10, place] = high + own
    return rows


def permutations():
    qkv = np.zeros((3 * C, 768), np.float32)
    proj = np.zeros((C, 768), np.float32)
    down = np.zeros((C, 256), np.float32)
    for piece in range(32):
        for i in range(18):
            qkv[18 * piece + i, 24 * piece + i] = 1
        for i in range(6):
            proj[6 * piece + i, 24 * piece + 18 + i] = 1
            down[6 * piece + i, 8 * piece + i] = 1
    return tuple(jnp.asarray(matrix, BF) for matrix in (qkv, proj, down))


def dot(a, b):
    return jnp.dot(a, b, preferred_element_type=F32)


def dot_nt(a, b):
    return lax.dot_general(a, b, (((1,), (1,)), ((), ())), preferred_element_type=F32)


def dot_tn(a, b):
    return lax.dot_general(a, b, (((0,), (0,)), ((), ())), preferred_element_type=F32)


def normal(u):
    power = jnp.exp(u * u * -0.5)
    place = 1.0 / (1.0 + jnp.abs(u) * (0.3275911 * 0.5**0.5))
    upper = 0.5 * 1.061405429
    for term in (-1.453152027, 1.421413741, -0.284496736, 0.254829592):
        upper = upper * place + 0.5 * term
    upper = upper * place * power
    return jnp.where(u < 0.0, upper, 1.0 - upper), power * 0.3989422804014327


def norm_parts(v):
    center = v - jnp.mean(v, axis=-1, keepdims=True)
    spread = jnp.mean(center * center, axis=-1, keepdims=True)
    inverse = lax.rsqrt(spread + EPS)
    return center * inverse, inverse


def norm_back(grad, unit, inverse):
    along = jnp.mean(grad * unit, axis=-1, keepdims=True)
    return inverse * (grad - jnp.mean(grad, axis=-1, keepdims=True) - unit * along)


def kernel(
    n_lat, n_lon,
    rel_hbm, table_hbm, const_hbm, tok_hbm, gmix_hbm, wqkv_hbm, wproj_hbm, gains_hbm, wup_hbm, wdown_hbm, pq_hbm, pp_hbm, pd_hbm, ids_ref,
    mixed_ref, gtok_ref, wg_ref, tgrad_ref,
    rel_ref, table_ref, const_ref, tok_ref, gmix_ref, wqkv_ref, wproj_ref, gains_ref, wup_ref, wdown_ref, pq_ref, pp_ref, pd_ref, load_sem,
    x_ref, qkv_ref, km_ref, vm_ref, s_ref, p_ref, att_ref, u1_ref, i1_ref, mid_ref, gp_ref, hid_ref, u2_ref, i2_ref,
    gup_ref, ds_ref, idx_ref, low_ref, tabf_ref, tab_ref, bias_ref, btail_ref, pk_ref, gall_ref, gsend_ref, grecv_ref, gx_ref, acc_ref,
    l_ref, r_ref, o1_ref, o2_ref, o3_ref,
    hs_ref, hr_ref,
    second_refs, early_refs, late_refs,
    tb_ref, tr1_ref, t1_ref, tr2_ref, t2_ref, t3_ref, t4_ref,
    ssem, rsem,
):
    loads = [
        pltpu.make_async_copy(src, dst, load_sem.at[k])
        for k, (src, dst) in enumerate([
            (rel_hbm, rel_ref), (table_hbm, table_ref), (const_hbm, const_ref), (tok_hbm, tok_ref), (gmix_hbm, gmix_ref),
            (wqkv_hbm, wqkv_ref), (wproj_hbm, wproj_ref), (gains_hbm, gains_ref), (wup_hbm, wup_ref), (wdown_hbm, wdown_ref),
            (pq_hbm, pq_ref), (pp_hbm, pp_ref), (pd_hbm, pd_ref),
        ])
    ]
    for load in loads:
        load.start()
    ny, nz = n_lat // 2, n_lon // 4
    lat, lon = lax.axis_index("lat"), lax.axis_index("lon")
    y, xh = lat >> 1, lat & 1
    z, xl, co = lon >> 2, (lon >> 1) & 1, lon & 1
    x = xh * 2 + xl
    lon_pair = [(lon ^ k, xl ^ (k >> 1), co ^ (k & 1)) for k in range(4)]
    lats = [(lat + k) & (n_lat - 1) for k in range(n_lat)]
    ahead = [((lat - a) & (n_lat - 1), (lon - b) & (n_lon - 1)) for a in (0, 1) for b in (0, 1)]
    back = [((lat + a) & (n_lat - 1), (lon + b) & (n_lon - 1)) for a in (0, 1) for b in (0, 1)]
    z_lons = [(lon + 4 * k) & (n_lon - 1) for k in range(nz)]
    ys, xs = [(y + k) & (ny - 1) for k in range(ny)], [(x + k) & 3 for k in range(4)]
    xy_lons = [lon - xl * 2 + (its_x & 1) * 2 for its_x in xs]
    xy_lats = [[its_y * 2 + (its_x >> 1) for its_x in xs] for its_y in ys]

    greeted = [(lats[k], lon) for k in range(1, n_lat)]
    greeted += [(lat, z_lons[k]) for k in range(1, nz)]
    greeted += [(lat, lon_pair[k][0]) for k in (1, 3)]
    greeted += [(lats[k], lon_pair[2][0]) for k in range(n_lat)]
    greeted += [ahead[1], ahead[3], back[1], back[3]]
    barrier = pltpu.get_barrier_semaphore()
    for device in greeted:
        pl.semaphore_signal(barrier, inc=1, device_id=device, device_id_type=MESH)

    sems = iter(range(N_SEMS))
    sent = []

    def push(src, dst, device):
        k = next(sems)
        copy = pltpu.make_async_remote_copy(
            src_ref=src, dst_ref=dst, send_sem=ssem.at[k], recv_sem=rsem.at[k], device_id=device, device_id_type=MESH
        )
        copy.start()
        sent.append(copy)
        return copy

    def arrive(copies):
        for copy in copies:
            copy.wait_recv()

    def onehot(n_rows, n_lanes, which):
        place = lax.broadcasted_iota(jnp.int32, (n_rows, n_lanes), 0)
        return jnp.where(place == const_ref[which : which + 1, :n_lanes], 1.0, 0.0).astype(BF)

    def moved(matrix, value):
        return dot(matrix, value).astype(BF)

    lane = lax.broadcasted_iota(jnp.int32, (1, C), 1)
    head_lanes = [(lane >= 32 * h) & (lane < 32 * h + 32) for h in range(HEADS)]

    def of_head(value, h):
        return jnp.where(head_lanes[h], value, jnp.zeros_like(value))

    def pack_tail(value, h):
        pk_ref[h, 0:TOK, 0:16] = value
        total = pk_ref[h, pl.ds(0, 24, stride=8), :]
        for j in range(1, 8):
            total = total + pltpu.roll(pk_ref[h, pl.ds(j, 24, stride=8), :], 16 * j, 1)
        return total

    def unpack_tail(value, k):
        for j in range(8):
            rolled = pltpu.roll(value, (128 - 16 * j) % 128, 1)
            btail_ref[k, pl.ds(j, 24, stride=8), :] = rolled

    def gather_bias(b):
        place = lax.broadcasted_iota(jnp.int32, (256, 128), 0).astype(BF)
        one, zero = jnp.ones((256, 128), BF), jnp.zeros((256, 128), BF)

        def step(i, carry):
            for m in range(7):
                group = i * 7 + m
                index = idx_ref[pl.ds(pl.multiple_of(group * 8, 8), 8), :]
                low, high = (index & 255).astype(F32), index >> 8
                picks = []
                for r in range(8):
                    row = jnp.broadcast_to(low[r : r + 1, :], (16, 128)).astype(BF)
                    picks.append(jnp.where(place == jnp.concatenate([row] * 16, axis=0), one, zero))
                rows = dot(tab_ref[b], jnp.concatenate(picks, axis=1))
                for r in range(8):
                    high_row = jnp.broadcast_to(high[r : r + 1, :], (8, 128))
                    found = jnp.zeros((8, 128), F32)
                    for part in range(13):
                        coarse = rows[8 * part : 8 * part + 8, 128 * r : 128 * r + 128]
                        fine = rows[104 + 8 * part : 112 + 8 * part, 128 * r : 128 * r + 128]
                        found = jnp.where(high_row == part, coarse + fine, found)
                    bias_ref[pl.ds(pl.multiple_of(group * 64 + r * 8, 8), 8), :] = found
            return carry

        lax.fori_loop(0, 3, step, 0)
        for h in range(HEADS):
            unpack_tail(bias_ref[pl.ds(8 * TAIL + h, 24, stride=8), :], h)

    half = ROWS // 2

    def share_scores(b):
        gsend_ref[b] = gall_ref[b, pl.ds((1 - co) * 8 * half, 8 * half), :].astype(BF)
        return [push(gsend_ref.at[b], grecv_ref.at[b], (lat, lon_pair[1][0]))]

    def add_scores(copies):
        both = []
        for b in range(2):
            arrive(copies[b])
            total = gall_ref[b, pl.ds(co * 8 * half, 8 * half), :] + grecv_ref[b].astype(F32)
            both.append(total.reshape(half, 8, 128))
        gx_ref[...] = jnp.concatenate(both, axis=1).astype(BF)

    def fold_tables():
        place = lax.broadcasted_iota(jnp.int32, (128, 256), 1).astype(BF)
        one, zero = jnp.ones((128, 256), BF), jnp.zeros((128, 256), BF)
        nothing = jnp.zeros((16, 128), BF)

        def step(i, carry):
            total = acc_ref[...]
            for m in range(6):
                group = i * 6 + m
                start = pl.multiple_of(co * half + group * 8, 8)
                high = (idx_ref[pl.ds(start, 8), :] >> 8).astype(F32)
                block = low_ref[group]
                left, right = [[] for _ in range(13)], []
                for r in range(8):
                    high_row = jnp.broadcast_to(high[r : r + 1, :], (16, 128)).astype(BF)
                    grads = gx_ref[group * 8 + r]
                    for part in range(13):
                        left[part].append(jnp.where(high_row == jnp.full((16, 128), part, BF), grads, nothing))
                    column = jnp.broadcast_to(block[:, r : r + 1], (128, 128)).astype(BF)
                    right.append(jnp.where(place == jnp.concatenate([column] * 2, axis=1), one, zero))
                left = jnp.concatenate([jnp.concatenate(rows, axis=1) for rows in left], axis=0)
                total = total + dot(left, jnp.concatenate(right, axis=0))
            acc_ref[...] = total
            return carry

        lax.fori_loop(0, 2, step, 0)

    def region_codes(place):
        code = jnp.zeros_like(place)
        for part in range(12):
            value = ids_ref[part % 6] + 64 * (part // 6)
            code = jnp.where(place >= 12 * part, value, code)
        return code

    def forward(b):
        tokens = x_ref[b]
        qkv_ref[b] = dot(tokens, wqkv_ref[b]).astype(BF)
        q, k, v = (qkv_ref[b, :, C * i : C * i + C] for i in range(3))
        for h in range(HEADS):
            km_ref[b, TOK * h : TOK * h + TOK, :] = of_head(k, h)
            vm_ref[b, TOK * h : TOK * h + TOK, :] = of_head(v, h)
        s_ref[...] = dot_nt(km_ref[b], q)
        if b == 1:
            codes_t = region_codes(lax.broadcasted_iota(jnp.int32, (TOK, 1), 0))
            codes_s = region_codes(lax.broadcasted_iota(jnp.int32, (1, TOK), 1))
            allowed = codes_s == codes_t
        for h in range(HEADS):
            span = pl.ds(TOK * h, TOK)
            bias = jnp.concatenate([bias_ref[pl.ds(h, TOK, stride=8), :], btail_ref[h, 0:TOK, 0:16]], axis=1)
            scores = s_ref[span, :] * SCALE + bias
            if b == 1:
                scores = jnp.where(allowed, scores, NEGATIVE)
            powers = jnp.exp(scores - jnp.max(scores, axis=0, keepdims=True))
            probs = powers * (1.0 / jnp.sum(powers, axis=0, keepdims=True))
            p_ref[b, span, :] = probs.astype(BF)
        attended = dot_tn(p_ref[b], vm_ref[b]).astype(BF)
        att_ref[b] = attended
        unit, inverse = norm_parts(dot(attended, wproj_ref[b]))
        u1_ref[b], i1_ref[b] = unit, inverse
        middle = (tokens.astype(F32) + unit * gains_ref[b, 0:1, :]).astype(BF)
        mid_ref[b] = middle
        for part in range(3):
            cols = pl.ds(256 * part, 256)
            up = dot(middle, wup_ref[b, :, cols])
            phi, density = normal(up)
            hid_ref[b, :, cols] = (up * phi).astype(BF)
            gp_ref[b, :, cols] = phi + up * density
        unit, inverse = norm_parts(dot_nt(hid_ref[b], wdown_ref[b]))
        u2_ref[b], i2_ref[b] = unit, inverse
        return (middle.astype(F32) + unit * gains_ref[b, 1:2, :]).astype(BF)

    def backward(b, grad, after_up=lambda grad_down: None, after_scores=lambda: None):
        grad = grad.astype(F32)
        grad_down = norm_back(grad * gains_ref[b, 1:2, :], u2_ref[b], i2_ref[b]).astype(BF)
        for part in range(3):
            cols = pl.ds(256 * part, 256)
            grad_hidden = dot(grad_down, wdown_ref[b, :, cols])
            gup_ref[b, :, cols] = (grad_hidden * gp_ref[b, :, cols]).astype(BF)
        grad_middle = grad + dot_nt(gup_ref[b], wup_ref[b])
        after_up(grad_down)
        grad_pre = norm_back(grad_middle * gains_ref[b, 0:1, :], u1_ref[b], i1_ref[b]).astype(BF)
        grad_att = dot_nt(grad_pre, wproj_ref[b]).astype(BF)
        q = qkv_ref[b, :, 0:C]
        s_ref[...] = dot_nt(vm_ref[b], grad_att)
        for h in range(HEADS):
            span = pl.ds(TOK * h, TOK)
            probs = p_ref[b, span, :].astype(F32)
            grad_probs = s_ref[span, :]
            grad_scores = probs * (grad_probs - jnp.sum(grad_probs * probs, axis=0, keepdims=True))
            ds_ref[span, :] = grad_scores.astype(BF)
            gall_ref[b, pl.ds(h, TOK, stride=8), :] = grad_scores[:, 0:128]
            gall_ref[b, pl.ds(8 * TAIL + h, 24, stride=8), :] = pack_tail(grad_scores[:, 128:TOK], h)
        after_scores()
        grad_q = dot_tn(ds_ref[...], km_ref[b])
        grad_k, grad_v = jnp.zeros((TOK, C), F32), jnp.zeros((TOK, C), F32)
        for h in range(HEADS):
            span = pl.ds(TOK * h, TOK)
            grad_k = jnp.where(head_lanes[h], dot(ds_ref[span, :], q), grad_k)
            grad_v = jnp.where(head_lanes[h], dot(p_ref[b, span, :], grad_att), grad_v)
        grad_qkv = jnp.concatenate([grad_q * SCALE, grad_k * SCALE, grad_v], axis=1).astype(BF)
        grad_in = (grad_middle + dot_nt(grad_qkv, wqkv_ref[b])).astype(BF)
        return grad_in, grad_down, grad_pre, grad_qkv

    def pack(buffer, piece, first_row, units):
        z_of = piece // 4
        for tile in range(len(units) // 2):
            pair = jnp.concatenate([units[2 * tile], units[2 * tile + 1]], axis=0).astype(BF)
            row = first_row + 16 * tile
            buffer[piece % 2, z_of // 2, z_of % 2 * 2 + piece // 2 % 2, row : row + 16, :] = pair

    def early_grads(b, grad_down, buffer):
        o2_ref[...] = dot_tn(gup_ref[b], mid_ref[b, :, 0:128])
        o3_ref[...] = dot_tn(moved(grad_down, pd_ref[...]), hid_ref[b])
        for piece in range(32):
            units = [o2_ref[24 * piece + 8 * i : 24 * piece + 8 * i + 8, :] for i in range(3)]
            units += [o3_ref[8 * piece : 8 * piece + 8, 128 * i : 128 * i + 128] for i in range(6)]
            pack(buffer, piece, 0, units + [jnp.zeros((8, 128), F32)])

    def late_grads(b, grad_pre, grad_qkv, buffer, first_row):
        l_ref[0:TOK, :] = moved(grad_qkv, pq_ref[...])
        l_ref[TOK : 2 * TOK, :] = moved(grad_pre, pp_ref[...])
        l_ref[2 * TOK : 3 * TOK, :] = gup_ref[b]
        r_ref[0:TOK, 0:192] = x_ref[b]
        r_ref[TOK : 2 * TOK, 0:192] = att_ref[b]
        r_ref[2 * TOK : 3 * TOK, 192:256] = mid_ref[b, :, 128:C]
        o1_ref[...] = dot_tn(l_ref[...], r_ref[...])
        for piece in range(32):
            units = [o1_ref[24 * piece + 8 * i : 24 * piece + 8 * i + 8, 128 * m : 128 * m + 128] for m in range(2) for i in range(3)]
            pack(buffer, piece, first_row, units)

    class Sum:
        def __init__(self, refs, out):
            self.sb, self.rc, self.wa, self.rx, self.wc, self.rz, self.wl = refs
            self.out = out
            self.copies = []
            self.steps = [self.core, self.along_xy, self.along_z, self.share, self.done]
            self.z_sems = [next(sems) for _ in range(nz - 1)]
            self.lat_sems = [next(sems) for _ in range(n_lat - 1)]

        def next(self):
            if self.steps:
                self.steps.pop(0)()

        def core(self):
            self.copies = [push(self.sb.at[1 - co], self.rc, (lat, lon_pair[1][0]))]

        def along_xy(self):
            arrive(self.copies)
            self.wa[...] = (self.sb[co].astype(F32) + self.rc[...].astype(F32)).astype(BF)
            self.copies = []
            for k in range(1, 4 * ny):
                device = (xy_lats[k // 4][k % 4], xy_lons[k % 4])
                self.copies.append(push(self.wa.at[ys[k // 4], xs[k % 4]], self.rx.at[k - 1], device))

        def to_owner(self):
            slot = ((z - lat) & (nz - 1)) - 1
            return pltpu.make_async_remote_copy(
                src_ref=self.wc, dst_ref=self.rz.at[slot], send_sem=ssem.at[self.z_sems[0]],
                recv_sem=rsem.at[self.z_sems[0] + slot], device_id=(lat, lat * 4 + xl * 2 + co), device_id_type=MESH,
            )

        def from_z(self, k):
            return pltpu.make_async_remote_copy(
                src_ref=self.wc, dst_ref=self.rz.at[k - 1], send_sem=ssem.at[self.z_sems[0]],
                recv_sem=rsem.at[self.z_sems[k - 1]], device_id=(lat, z_lons[k]), device_id_type=MESH,
            )

        def to_lat(self, k):
            return pltpu.make_async_remote_copy(
                src_ref=self.wl, dst_ref=self.wl, send_sem=ssem.at[self.lat_sems[k - 1]],
                recv_sem=rsem.at[self.lat_sems[0]], device_id=(lats[k], lon), device_id_type=MESH,
            )

        def along_z(self):
            arrive(self.copies)
            total = self.wa[y, x].astype(F32)
            for k in range(4 * ny - 1):
                total = total + self.rx[k].astype(F32)
            self.wc[...] = total.astype(BF)

            @pl.when(z != lat)
            def _():
                self.to_owner().start()

        def share(self):
            @pl.when(z == lat)
            def _():
                total = self.wc[...].astype(F32)
                for k in range(1, nz):
                    self.from_z(k).wait_recv()
                    total = total + self.rz[k - 1].astype(F32)
                self.wl[...] = total.astype(BF)
                for k in range(1, n_lat):
                    self.to_lat(k).start()

        def done(self):
            @pl.when(z != lat)
            def _():
                self.to_lat(1).wait_recv()
                self.to_owner().wait_send()

            self.out[...] = self.wl[...]

            @pl.when(z == lat)
            def _():
                for k in range(1, n_lat):
                    self.to_lat(k).wait_send()

    class TableSum:
        def __init__(self):
            self.copies = []
            self.steps = [self.pair, self.along_z, self.share_z, self.share_pair, self.done]

        def next(self):
            if self.steps:
                self.steps.pop(0)()

        def pair(self):
            for part in range(26):
                row, lanes = 16 * (part // 2), slice(128 * (part % 2), 128 * (part % 2) + 128)
                both = acc_ref[row : row + 16, lanes]
                tb_ref[part // 16, part // 8 % 2, part % 8] = both.astype(BF)
            for part in range(26, 32):
                tb_ref[part // 16, part // 8 % 2, part % 8] = jnp.zeros((16, 128), BF)
            for k in range(1, 4):
                device, its_xl, its_co = lon_pair[k]
                self.copies.append(push(tb_ref.at[its_co, its_xl], tr1_ref.at[k - 1], (lat, device)))

        def along_z(self):
            arrive(self.copies)
            total = tb_ref[co, xl].astype(F32)
            for k in range(3):
                total = total + tr1_ref[k].astype(F32)
            t1_ref[...] = total.astype(BF)
            self.copies = []
            for k in range(1, nz):
                self.copies.append(push(t1_ref.at[(z + k) & (nz - 1)], tr2_ref.at[k - 1], (lat, z_lons[k])))

        def share_z(self):
            arrive(self.copies)
            total = t1_ref[z].astype(F32)
            for k in range(nz - 1):
                total = total + tr2_ref[k].astype(F32)
            t2_ref[...] = total.astype(BF)
            self.copies = []
            for k in range(1, nz):
                self.copies.append(push(t2_ref, t3_ref.at[z], (lat, z_lons[k])))
            t3_ref[z] = t2_ref[...]

        def share_pair(self):
            arrive(self.copies)
            self.copies = []
            for k in range(1, 4):
                self.copies.append(push(t3_ref, t4_ref.at[co, xl], (lat, lon_pair[k][0])))
            t4_ref[co, xl] = t3_ref[...]

        def done(self):
            arrive(self.copies)
            tgrad_ref[...] = t4_ref[...]

    def send_quarters(which, devices):
        copies = []
        for quarter in range(1, 4):
            copies.append(push(hs_ref.at[which, quarter], hr_ref.at[which, quarter], devices[quarter]))
        hr_ref[which, 0] = hs_ref[which, 0]
        return copies

    pk_ref[...] = jnp.zeros_like(pk_ref)
    gall_ref[...] = jnp.zeros_like(gall_ref)
    r_ref[...] = jnp.zeros_like(r_ref)
    loads[0].wait()
    relative = rel_ref[...].astype(F32).T
    idx_ref[0:TOK, :] = relative[:, 0:128].astype(jnp.int32)
    idx_ref[TAIL : TAIL + 24, :] = pack_tail(relative[:, 128:TOK], 0).astype(jnp.int32)
    idx_ref[TAIL + 18 : ROWS, :] = jnp.full((ROWS - TAIL - 18, 128), -1, jnp.int32)
    low = (idx_ref[pl.ds(pl.multiple_of(co * half, 8), half), :] & 255).astype(F32).T
    for i in range(half // 8):
        low_ref[i] = low[:, 8 * i : 8 * i + 8]
    loads[1].wait()
    tabf_ref[...] = jnp.zeros_like(tabf_ref)
    for b in range(2):
        for part in range(13):
            width = min(256, POS - 256 * part)
            tabf_ref[b, 8 * part : 8 * part + 6, 0:width] = table_ref[6 * b : 6 * b + 6, 0, 256 * part : 256 * part + width]
        table = tabf_ref[b]
        coarse = table.astype(BF)
        tab_ref[b, 0:104, :] = coarse
        tab_ref[b, 104:208, :] = (table - coarse.astype(F32)).astype(BF)
    gather_bias(0)
    for load in loads[2:]:
        load.wait()
    x_ref[0] = moved(onehot(TOK, TOK, 0), tok_ref[...].reshape(TOK, C))
    hs_ref[0] = moved(onehot(192, TOK, 10), gmix_ref[...].reshape(TOK, C)).reshape(4, 48, C)

    first = forward(0)
    hs_ref[1] = moved(onehot(192, TOK, 2), first).reshape(4, 48, C)
    pl.semaphore_wait(barrier, len(greeted))
    copies_x = send_quarters(1, ahead)
    copies_g = send_quarters(0, ahead)
    gather_bias(1)
    acc_ref[...] = jnp.zeros_like(acc_ref)
    arrive(copies_x)
    arrive(copies_g)
    come = onehot(TOK, 192, 3)
    x_ref[1] = moved(come, hr_ref[1].reshape(192, C))
    grad_shifted = moved(come, hr_ref[0].reshape(192, C))

    second = forward(1)
    hs_ref[2] = moved(onehot(192, TOK, 4), second).reshape(4, 48, C)
    grad_second, *rest = backward(1, grad_shifted)
    hs_ref[3] = moved(onehot(192, TOK, 4), grad_second).reshape(4, 48, C)
    copies_s = send_quarters(3, back)
    copies_m = send_quarters(2, back)
    copies_two = share_scores(1)
    grad_down, grad_pre, grad_qkv = rest
    early_grads(1, grad_down, second_refs[0])
    late_grads(1, grad_pre, grad_qkv, second_refs[0], 80)
    sum_two = Sum(second_refs, wg_ref.at[1])
    sum_early = Sum(early_refs, wg_ref.at[0, 0:80])
    sum_late = Sum(late_refs, wg_ref.at[0, 80:128])
    sum_two.next()

    arrive(copies_s)
    grad_first = moved(onehot(TOK, 192, 5), hr_ref[3].reshape(192, C))
    def after_up(grad_down):
        sum_two.next()
        early_grads(0, grad_down, early_refs[0])
        sum_early.next()

    copies_one = []

    def after_scores():
        copies_one.extend(share_scores(0))
        sum_early.next()

    grad_in, _, grad_pre, grad_qkv = backward(0, grad_first, after_up, after_scores)
    add_scores([copies_one, copies_two])
    fold_tables()
    sum_table = TableSum()
    sum_table.next()
    late_grads(0, grad_pre, grad_qkv, late_refs[0], 0)
    sum_late.next()
    sum_two.next()
    sum_table.next()
    sum_late.next()
    arrive(copies_m)
    mixed_ref[...] = moved(onehot(TOK, 192, 6), hr_ref[2].reshape(192, C)).reshape(72, 2, C)
    gtok_ref[...] = moved(onehot(TOK, TOK, 1), grad_in).reshape(72, 2, C)
    sum_early.next()
    sum_table.next()
    sum_two.next()
    sum_late.next()
    sum_table.next()
    sum_early.next()
    sum_late.next()
    sum_table.next()
    sum_two.next()
    sum_early.next()
    sum_late.next()
    for copy in sent:
        copy.wait_send()


def finish(mixed_in, gtok_in, wg_in, table_in, mixed_ref, gtok_ref, qkv_ref, proj_ref, up_ref, down_ref, table_ref):
    mixed_ref[...] = mixed_in[...]
    gtok_ref[...] = gtok_in[...]
    for b in range(2):
        rows = wg_in[b].astype(F32)
        up_ref[b, :, 0:128] = rows[0:24, :]
        up_ref[b, :, 128:C] = rows[104:128, 64:128]
        qkv_ref[:, b, 0:128] = rows[80:98, :]
        qkv_ref[:, b, 128:C] = rows[104:122, 0:64]
        proj_ref[:, b, 0:128] = rows[98:104, :]
        proj_ref[:, b, 128:C] = rows[122:128, 0:64]
        for i in range(6):
            down_ref[:, b, 128 * i : 128 * i + 128] = rows[24 + 8 * i : 30 + 8 * i, :]
    for part in range(26):
        tile = table_in[part // 16, part // 8 % 2, part % 8].astype(F32)
        width = min(128, POS - 128 * part)
        for b in range(2):
            table_ref[6 * b : 6 * b + 6, 0, 128 * part : 128 * part + width] = tile[8 * b : 8 * b + 6, 0:width]


def per_device(tokens, grad_mixed, w_qkv, w_proj, w_up, w_down, gains, bias_table, rel_index, mask_ids):
    n_lat, n_lon = lax.axis_size("lat"), lax.axis_size("lon")
    ny, nz = n_lat // 2, n_lon // 4
    vmem = pl.BlockSpec(memory_space=pltpu.VMEM)
    smem = pl.BlockSpec(memory_space=pltpu.SMEM)

    def buf(*shape, dtype=BF):
        return pltpu.VMEM(shape, dtype)

    def stream(rows):
        return (
            buf(2, ny, 4, rows, 128), buf(ny, 4, rows, 128), buf(ny, 4, rows, 128), buf(4 * ny - 1, rows, 128),
            buf(rows, 128), buf(nz - 1, rows, 128), buf(rows, 128),
        )

    scratch = [
        buf(TOK, TOK, dtype=jnp.int32), buf(12, 1, POS, dtype=F32), buf(16, 768, dtype=jnp.int32),
        buf(72, 2, C), buf(72, 2, C), buf(2, C, 3 * C), buf(2, C, C), buf(2, 2, C, dtype=F32), buf(2, C, 768), buf(2, C, 768),
        buf(3 * C, 768), buf(C, 768), buf(C, 256),
        pltpu.SemaphoreType.DMA((13,)),
        buf(2, TOK, C), buf(2, TOK, 3 * C), buf(2, 6 * TOK, C), buf(2, 6 * TOK, C), buf(6 * TOK, TOK, dtype=F32),
        buf(2, 6 * TOK, TOK), buf(2, TOK, C), buf(2, TOK, C, dtype=F32), buf(2, TOK, 1, dtype=F32), buf(2, TOK, C),
        buf(2, TOK, 768, dtype=F32), buf(2, TOK, 768), buf(2, TOK, C, dtype=F32), buf(2, TOK, 1, dtype=F32),
        buf(2, TOK, 768), buf(6 * TOK, TOK),
        buf(ROWS, 128, dtype=jnp.int32), buf(ROWS // 16, 128, 8, dtype=F32), buf(2, 104, 256, dtype=F32), buf(2, 208, 256),
        buf(8 * 168, 128, dtype=F32), buf(6, 192, 128, dtype=F32), buf(6, 192, 128, dtype=F32),
        buf(2, 8 * ROWS, 128, dtype=F32), buf(2, 4 * ROWS, 128), buf(2, 4 * ROWS, 128),
        buf(ROWS // 2, 16, 128), buf(208, 256, dtype=F32),
        buf(3 * TOK, 768), buf(3 * TOK, 256), buf(768, 256, dtype=F32), buf(768, 128, dtype=F32), buf(256, 768, dtype=F32),
        buf(4, 4, 48, C), buf(4, 4, 48, C),
        stream(128), stream(80), stream(48),
        buf(2, 2, 8, 16, 128), buf(3, 8, 16, 128), buf(8, 16, 128), buf(7, 16, 128), buf(16, 128),
        buf(8, 16, 128), buf(2, 2, 8, 16, 128),
        pltpu.SemaphoreType.DMA((N_SEMS,)), pltpu.SemaphoreType.DMA((N_SEMS,)),
    ]
    results = pl.pallas_call(
        functools.partial(kernel, n_lat, n_lon),
        out_shape=(
            jax.ShapeDtypeStruct((72, 2, C), BF),
            jax.ShapeDtypeStruct((72, 2, C), BF),
            jax.ShapeDtypeStruct((2, 128, 128), BF),
            jax.ShapeDtypeStruct((2, 2, 8, 16, 128), BF),
        ),
        in_specs=[pl.BlockSpec(memory_space=pltpu.HBM)] * 13 + [smem],
        out_specs=[vmem] * 4,
        scratch_shapes=scratch,
        compiler_params=pltpu.CompilerParams(
            collective_id=0, has_side_effects=True, vmem_limit_bytes=60 * 1024 * 1024
        ),
    )(
        rel_index,
        bias_table.reshape(12, 1, POS),
        jnp.asarray(index_rows()),
        tokens.transpose(1, 2, 0, 3).reshape(72, 2, C),
        grad_mixed.transpose(1, 2, 0, 3).reshape(72, 2, C),
        w_qkv, w_proj, gains, w_up, w_down.transpose(0, 2, 1),
        *permutations(),
        mask_ids,
    )
    mixed, grad_tokens, qkv, proj, up, down, table = pl.pallas_call(
        finish,
        out_shape=(
            jax.ShapeDtypeStruct((72, 2, C), BF),
            jax.ShapeDtypeStruct((72, 2, C), BF),
            jax.ShapeDtypeStruct((18, 2, C), F32),
            jax.ShapeDtypeStruct((6, 2, C), F32),
            jax.ShapeDtypeStruct((2, 24, C), F32),
            jax.ShapeDtypeStruct((6, 2, 768), F32),
            jax.ShapeDtypeStruct((12, 1, POS), F32),
        ),
        in_specs=[vmem] * 4,
        out_specs=[vmem] * 7,
        compiler_params=pltpu.CompilerParams(vmem_limit_bytes=60 * 1024 * 1024),
    )(*results)

    def field(value):
        return value.reshape(6, 12, 2, C).transpose(2, 0, 1, 3)

    return (
        field(mixed),
        field(grad_tokens),
        qkv.transpose(1, 2, 0),
        proj.transpose(1, 2, 0),
        up.transpose(0, 2, 1),
        down.transpose(1, 2, 0),
        table.reshape(2, 1, 1, 6, POS),
    )


def solution(mesh):
    field = P(None, "lat", "lon", None)
    table = P(None, None, "lat", None, None)
    in_specs = (field, field, P(), P(), P(), P(), P(), table, P(), P("lat"))
    columns = P(None, None, "lon")
    out_specs = (field, field, columns, columns, columns, columns, table)
    return jax.shard_map(per_device, mesh=mesh, in_specs=in_specs, out_specs=out_specs, check_vma=False)
```

```python
import functools

import jax
import jax.numpy as jnp
import numpy as np
from jax import lax
from jax.experimental import pallas as pl
from jax.experimental.pallas import tpu as pltpu
from jax.sharding import PartitionSpec as P

HEADS = 6
C = 192
TOK = 144
POS = 3312
EPS = 1e-05
NEGATIVE = -1e30
SCALE = 32 ** -0.5
BF = jnp.bfloat16
F32 = jnp.float32
MESH = pl.DeviceIdType.MESH
ROWS = 192
TAIL = 144
N_SEMS = 132


def index_rows():
    rows = np.full((16, 768), -1, np.int32)
    tok = np.arange(TOK)
    level, row, col = tok // 72, tok // 12 % 6, tok % 12
    place = 24 * row + 2 * col + level
    own = 18 * level + row % 3 * 6 + col % 6
    other = 18 * (1 - level) + row % 3 * 6 + col % 6
    low = 48 * (2 * (row // 3) + col // 6)
    high = 48 * (2 * (1 - row // 3) + 1 - col // 6)
    rows[0, place] = tok
    rows[1, tok] = place
    rows[2, tok] = high + own
    rows[3, low + other] = tok
    rows[4, tok] = low + own
    rows[5, high + other] = tok
    rows[6, high + other] = place
    rows[10, place] = high + own
    return rows


def permutations():
    qkv = np.zeros((3 * C, 768), np.float32)
    proj = np.zeros((C, 768), np.float32)
    down = np.zeros((C, 256), np.float32)
    for piece in range(32):
        for i in range(18):
            qkv[18 * piece + i, 24 * piece + i] = 1
        for i in range(6):
            proj[6 * piece + i, 24 * piece + 18 + i] = 1
            down[6 * piece + i, 8 * piece + i] = 1
    return tuple(jnp.asarray(matrix, BF) for matrix in (qkv.T, proj.T, down.T, np.eye(256, dtype=np.float32)))


def dot(a, b):
    return jnp.dot(a, b, preferred_element_type=F32)


def dot_nt(a, b):
    return lax.dot_general(a, b, (((1,), (1,)), ((), ())), preferred_element_type=F32)


def dot_tn(a, b):
    return lax.dot_general(a, b, (((0,), (0,)), ((), ())), preferred_element_type=F32)


def normal(u):
    power = jnp.exp(u * u * -0.5)
    place = 1.0 / (1.0 + jnp.abs(u) * (0.3275911 * 0.5**0.5))
    upper = 0.5 * 1.061405429
    for term in (-1.453152027, 1.421413741, -0.284496736, 0.254829592):
        upper = upper * place + 0.5 * term
    upper = upper * place * power
    return jnp.where(u < 0.0, upper, 1.0 - upper), power * 0.3989422804014327


def norm_parts(v):
    center = v - jnp.mean(v, axis=-1, keepdims=True)
    spread = jnp.mean(center * center, axis=-1, keepdims=True)
    inverse = lax.rsqrt(spread + EPS)
    return center * inverse, inverse


def norm_back(grad, unit, inverse):
    along = jnp.mean(grad * unit, axis=-1, keepdims=True)
    return inverse * (grad - jnp.mean(grad, axis=-1, keepdims=True) - unit * along)


def kernel(
    n_lat, n_lon,
    rel_hbm, table_hbm, const_hbm, tok_hbm, gmix_hbm, wqkv_hbm, wproj_hbm, gains_hbm, wup_hbm, wdown_hbm, pq_hbm, pp_hbm, pd_hbm, eye_hbm, ids_ref,
    mixed_ref, gtok_ref, wg_ref, tgrad_ref,
    rel_ref, table_ref, const_ref, tok_ref, gmix_ref, wqkv_ref, wproj_ref, gains_ref, wup_ref, wdown_ref, pq_ref, pp_ref, pd_ref, eye_ref, load_sem,
    x_ref, qkv_ref, km_ref, vm_ref, s_ref, p_ref, att_ref, u1_ref, i1_ref, mid_ref, gp_ref, hid_ref, u2_ref, i2_ref,
    gup_ref, ds_ref, idx_ref, low_ref, tabf_ref, tab_ref, bias_ref, btail_ref, pk_ref, gall_ref, gsend_ref, grecv_ref, gx_ref, acc_ref,
    r_ref, o1_ref, o2_ref, o3_ref,
    hs_ref, hr_ref,
    second_refs, early_refs, late_refs,
    tb_ref, tr1_ref, t1_ref, tr2_ref, t2_ref, t3_ref, t4_ref,
    ssem, rsem,
):
    loads = [
        pltpu.make_async_copy(src, dst, load_sem.at[k])
        for k, (src, dst) in enumerate([
            (rel_hbm, rel_ref), (table_hbm, table_ref), (const_hbm, const_ref), (tok_hbm, tok_ref), (gmix_hbm, gmix_ref),
            (wqkv_hbm, wqkv_ref), (wproj_hbm, wproj_ref), (gains_hbm, gains_ref), (wup_hbm, wup_ref), (wdown_hbm, wdown_ref),
            (pq_hbm, pq_ref), (pp_hbm, pp_ref), (pd_hbm, pd_ref), (eye_hbm, eye_ref),
        ])
    ]
    for load in loads:
        load.start()
    ny, nz = n_lat // 2, n_lon // 4
    lat, lon = lax.axis_index("lat"), lax.axis_index("lon")
    y, xh = lat >> 1, lat & 1
    z, xl, co = lon >> 2, (lon >> 1) & 1, lon & 1
    x = xh * 2 + xl
    lon_pair = [(lon ^ k, xl ^ (k >> 1), co ^ (k & 1)) for k in range(4)]
    lats = [(lat + k) & (n_lat - 1) for k in range(n_lat)]
    ahead = [((lat - a) & (n_lat - 1), (lon - b) & (n_lon - 1)) for a in (0, 1) for b in (0, 1)]
    back = [((lat + a) & (n_lat - 1), (lon + b) & (n_lon - 1)) for a in (0, 1) for b in (0, 1)]
    z_lons = [(lon + 4 * k) & (n_lon - 1) for k in range(nz)]
    ys, xs = [(y + k) & (ny - 1) for k in range(ny)], [(x + k) & 3 for k in range(4)]
    xy_lons = [lon - xl * 2 + (its_x & 1) * 2 for its_x in xs]
    xy_lats = [[its_y * 2 + (its_x >> 1) for its_x in xs] for its_y in ys]

    greeted = [(lats[k], lon) for k in range(1, n_lat)]
    greeted += [(lat, z_lons[k] ^ flip) for k in range(1, nz) for flip in (0, 2)]
    greeted += [(lat, lon_pair[k][0]) for k in (1, 3)]
    greeted += [(lats[k], lon_pair[2][0]) for k in range(n_lat)]
    greeted += [ahead[1], ahead[3], back[1], back[3]]
    barrier = pltpu.get_barrier_semaphore()
    for device in greeted:
        pl.semaphore_signal(barrier, inc=1, device_id=device, device_id_type=MESH)

    sems = iter(range(N_SEMS))
    sent = []

    def push(src, dst, device):
        k = next(sems)
        copy = pltpu.make_async_remote_copy(
            src_ref=src, dst_ref=dst, send_sem=ssem.at[k], recv_sem=rsem.at[k], device_id=device, device_id_type=MESH
        )
        copy.start()
        sent.append(copy)
        return copy

    def arrive(copies):
        for copy in copies:
            copy.wait_recv()

    def onehot(n_rows, n_lanes, which):
        place = lax.broadcasted_iota(jnp.int32, (n_rows, n_lanes), 0)
        return jnp.where(place == const_ref[which : which + 1, :n_lanes], 1.0, 0.0).astype(BF)

    def moved(matrix, value):
        return dot(matrix, value).astype(BF)

    lane = lax.broadcasted_iota(jnp.int32, (1, C), 1)
    head_lanes = [(lane >= 32 * h) & (lane < 32 * h + 32) for h in range(HEADS)]

    def of_head(value, h):
        return jnp.where(head_lanes[h], value, jnp.zeros_like(value))

    def pack_tail(value, h):
        pk_ref[h, 0:TOK, 0:16] = value
        total = pk_ref[h, pl.ds(0, 24, stride=8), :]
        for j in range(1, 8):
            total = total + pltpu.roll(pk_ref[h, pl.ds(j, 24, stride=8), :], 16 * j, 1)
        return total

    def unpack_tail(value, k):
        for j in range(8):
            rolled = pltpu.roll(value, (128 - 16 * j) % 128, 1)
            btail_ref[k, pl.ds(j, 24, stride=8), :] = rolled

    def gather_bias(b):
        place = lax.broadcasted_iota(jnp.int32, (256, 128), 0).astype(BF)
        one, zero = jnp.ones((256, 128), BF), jnp.zeros((256, 128), BF)

        def step(i, carry):
            for m in range(7):
                group = i * 7 + m
                index = idx_ref[pl.ds(pl.multiple_of(group * 8, 8), 8), :]
                low, high = (index & 255).astype(F32), index >> 8
                picks = []
                for r in range(8):
                    row = jnp.broadcast_to(low[r : r + 1, :], (16, 128)).astype(BF)
                    picks.append(jnp.where(place == jnp.concatenate([row] * 16, axis=0), one, zero))
                rows = dot(tab_ref[b], jnp.concatenate(picks, axis=1))
                for r in range(8):
                    high_row = jnp.broadcast_to(high[r : r + 1, :], (8, 128))
                    found = jnp.zeros((8, 128), F32)
                    for part in range(13):
                        coarse = rows[8 * part : 8 * part + 8, 128 * r : 128 * r + 128]
                        fine = rows[104 + 8 * part : 112 + 8 * part, 128 * r : 128 * r + 128]
                        found = jnp.where(high_row == part, coarse + fine, found)
                    bias_ref[pl.ds(pl.multiple_of(group * 64 + r * 8, 8), 8), :] = found
            return carry

        lax.fori_loop(0, 3, step, 0)
        for h in range(HEADS):
            unpack_tail(bias_ref[pl.ds(8 * TAIL + h, 24, stride=8), :], h)

    half = ROWS // 2

    def share_scores(b):
        gsend_ref[b] = gall_ref[b, pl.ds((1 - co) * 8 * half, 8 * half), :].astype(BF)
        return [push(gsend_ref.at[b], grecv_ref.at[b], (lat, lon_pair[1][0]))]

    def add_scores(copies):
        both = []
        for b in range(2):
            arrive(copies[b])
            total = gall_ref[b, pl.ds(co * 8 * half, 8 * half), :] + grecv_ref[b].astype(F32)
            both.append(total.reshape(half, 8, 128))
        gx_ref[...] = jnp.concatenate(both, axis=1).astype(BF)

    def fold_tables():
        place = lax.broadcasted_iota(jnp.int32, (128, 256), 1).astype(BF)
        one, zero = jnp.ones((128, 256), BF), jnp.zeros((128, 256), BF)
        nothing = jnp.zeros((16, 128), BF)

        def step(i, carry):
            total = acc_ref[...]
            for m in range(6):
                group = i * 6 + m
                start = pl.multiple_of(co * half + group * 8, 8)
                high = (idx_ref[pl.ds(start, 8), :] >> 8).astype(F32)
                block = low_ref[group]
                left, right = [[] for _ in range(13)], []
                for r in range(8):
                    high_row = jnp.broadcast_to(high[r : r + 1, :], (16, 128)).astype(BF)
                    grads = gx_ref[group * 8 + r]
                    for part in range(13):
                        left[part].append(jnp.where(high_row == jnp.full((16, 128), part, BF), grads, nothing))
                    column = jnp.broadcast_to(block[:, r : r + 1], (128, 128)).astype(BF)
                    right.append(jnp.where(place == jnp.concatenate([column] * 2, axis=1), one, zero))
                left = jnp.concatenate([jnp.concatenate(rows, axis=1) for rows in left], axis=0)
                total = total + dot(left, jnp.concatenate(right, axis=0))
            acc_ref[...] = total
            return carry

        lax.fori_loop(0, 2, step, 0)

    def region_codes(place):
        code = jnp.zeros_like(place)
        for part in range(12):
            value = ids_ref[part % 6] + 64 * (part // 6)
            code = jnp.where(place >= 12 * part, value, code)
        return code

    def forward(b):
        tokens = x_ref[b]
        qkv_ref[b] = dot(tokens, wqkv_ref[b]).astype(BF)
        q, k, v = (qkv_ref[b, :, C * i : C * i + C] for i in range(3))
        for h in range(HEADS):
            km_ref[b, TOK * h : TOK * h + TOK, :] = of_head(k, h)
            vm_ref[b, TOK * h : TOK * h + TOK, :] = of_head(v, h)
        s_ref[...] = dot_nt(km_ref[b], q)
        if b == 1:
            codes_t = region_codes(lax.broadcasted_iota(jnp.int32, (TOK, 1), 0))
            codes_s = region_codes(lax.broadcasted_iota(jnp.int32, (1, TOK), 1))
            allowed = codes_s == codes_t
        for h in range(HEADS):
            span = pl.ds(TOK * h, TOK)
            bias = jnp.concatenate([bias_ref[pl.ds(h, TOK, stride=8), :], btail_ref[h, 0:TOK, 0:16]], axis=1)
            scores = s_ref[span, :] * SCALE + bias
            if b == 1:
                scores = jnp.where(allowed, scores, NEGATIVE)
            powers = jnp.exp(scores - jnp.max(scores, axis=0, keepdims=True))
            probs = powers * (1.0 / jnp.sum(powers, axis=0, keepdims=True))
            p_ref[b, span, :] = probs.astype(BF)
        attended = dot_tn(p_ref[b], vm_ref[b]).astype(BF)
        att_ref[b] = attended
        unit, inverse = norm_parts(dot(attended, wproj_ref[b]))
        u1_ref[b], i1_ref[b] = unit, inverse
        middle = (tokens.astype(F32) + unit * gains_ref[b, 0:1, :]).astype(BF)
        mid_ref[b] = middle
        for part in range(3):
            cols = pl.ds(256 * part, 256)
            up = dot(middle, wup_ref[b, :, cols])
            phi, density = normal(up)
            hid_ref[b, :, cols] = (up * phi).astype(BF)
            gp_ref[b, :, cols] = phi + up * density
        unit, inverse = norm_parts(dot_nt(hid_ref[b], wdown_ref[b]))
        u2_ref[b], i2_ref[b] = unit, inverse
        return (middle.astype(F32) + unit * gains_ref[b, 1:2, :]).astype(BF)

    def backward(b, grad, after_up=lambda grad_down: None, after_scores=lambda: None):
        grad = grad.astype(F32)
        grad_down = norm_back(grad * gains_ref[b, 1:2, :], u2_ref[b], i2_ref[b]).astype(BF)
        for part in range(3):
            cols = pl.ds(256 * part, 256)
            grad_hidden = dot(grad_down, wdown_ref[b, :, cols])
            gup_ref[b, :, cols] = (grad_hidden * gp_ref[b, :, cols]).astype(BF)
        grad_middle = grad + dot_nt(gup_ref[b], wup_ref[b])
        after_up(grad_down)
        grad_pre = norm_back(grad_middle * gains_ref[b, 0:1, :], u1_ref[b], i1_ref[b]).astype(BF)
        grad_att = dot_nt(grad_pre, wproj_ref[b]).astype(BF)
        q = qkv_ref[b, :, 0:C]
        s_ref[...] = dot_nt(vm_ref[b], grad_att)
        for h in range(HEADS):
            span = pl.ds(TOK * h, TOK)
            probs = p_ref[b, span, :].astype(F32)
            grad_probs = s_ref[span, :]
            grad_scores = probs * (grad_probs - jnp.sum(grad_probs * probs, axis=0, keepdims=True))
            ds_ref[span, :] = grad_scores.astype(BF)
            gall_ref[b, pl.ds(h, TOK, stride=8), :] = grad_scores[:, 0:128]
            gall_ref[b, pl.ds(8 * TAIL + h, 24, stride=8), :] = pack_tail(grad_scores[:, 128:TOK], h)
        after_scores()
        grad_q = dot_tn(ds_ref[...], km_ref[b])
        grad_k, grad_v = jnp.zeros((TOK, C), F32), jnp.zeros((TOK, C), F32)
        for h in range(HEADS):
            span = pl.ds(TOK * h, TOK)
            grad_k = jnp.where(head_lanes[h], dot(ds_ref[span, :], q), grad_k)
            grad_v = jnp.where(head_lanes[h], dot(p_ref[b, span, :], grad_att), grad_v)
        grad_qkv = jnp.concatenate([grad_q * SCALE, grad_k * SCALE, grad_v], axis=1).astype(BF)
        grad_in = (grad_middle + dot_nt(grad_qkv, wqkv_ref[b])).astype(BF)
        return grad_in, grad_down, grad_pre, grad_qkv

    def by_owner(buffer, piece):
        return buffer.at[piece % 2, piece // 8, piece // 4 % 2 * 2 + piece // 2 % 2]

    def by_lon(buffer, piece):
        return buffer.at[piece % 2, piece // 4, piece // 2 % 2]

    def pack(place, first_row, units):
        for tile in range(len(units) // 2):
            pair = jnp.concatenate([units[2 * tile], units[2 * tile + 1]], axis=0).astype(BF)
            row = first_row + 16 * tile
            place[row : row + 16, :] = pair

    def early_grads(b, grad_down, buffer):
        r_ref[:, 0:128] = mid_ref[b, :, 0:128]
        r_ref[:, C:256] = mid_ref[b, :, 128:C]
        for part in range(3):
            span = slice(256 * part, 256 * part + 256)
            turned = dot_nt(eye_ref[...], gup_ref[b, :, span]).astype(BF)
            grads = dot(turned, r_ref[...])
            o2_ref[span, :] = grads[:, 0:128]
            o1_ref[span, C:256] = grads[:, C:256]
        o3_ref[...] = dot(dot_nt(pd_ref[...], grad_down).astype(BF), hid_ref[b])
        for piece in range(32):
            units = [o2_ref[24 * piece + 8 * i : 24 * piece + 8 * i + 8, :] for i in range(3)]
            units += [o3_ref[8 * piece : 8 * piece + 8, 128 * i : 128 * i + 128] for i in range(6)]
            pack(by_owner(buffer, piece), 0, units + [jnp.zeros((8, 128), F32)])

    def late_grads(b, grad_pre, grad_qkv, buffer, layout, first_row):
        turned = dot_nt(pp_ref[...], grad_pre).astype(BF)
        grads = dot(turned, att_ref[b])
        turned = dot_nt(pq_ref[...], grad_qkv).astype(BF)
        o1_ref[:, 0:C] = grads + dot(turned, x_ref[b])
        for piece in range(32):
            units = [o1_ref[24 * piece + 8 * i : 24 * piece + 8 * i + 8, 128 * m : 128 * m + 128] for m in range(2) for i in range(3)]
            pack(layout(buffer, piece), first_row, units)

    class Sum:
        def __init__(self, refs, out):
            self.sb, self.rc, self.wa, self.rx, self.wc, self.rz, self.wl = refs
            self.out = out
            self.copies = []
            self.steps = [self.core, self.along_xy, self.along_z, self.share, self.done]
            self.z_sems = [next(sems) for _ in range(nz - 1)]
            self.lat_sems = [next(sems) for _ in range(n_lat - 1)]

        def next(self):
            if self.steps:
                self.steps.pop(0)()

        def core(self):
            self.copies = [push(self.sb.at[1 - co], self.rc, (lat, lon_pair[1][0]))]

        def along_xy(self):
            arrive(self.copies)
            self.wa[...] = (self.sb[co].astype(F32) + self.rc[...].astype(F32)).astype(BF)
            self.copies = []
            for k in range(1, 4 * ny):
                device = (xy_lats[k // 4][k % 4], xy_lons[k % 4])
                self.copies.append(push(self.wa.at[ys[k // 4], xs[k % 4]], self.rx.at[k - 1], device))

        def to_owner(self):
            slot = ((z - lat) & (nz - 1)) - 1
            return pltpu.make_async_remote_copy(
                src_ref=self.wc, dst_ref=self.rz.at[slot], send_sem=ssem.at[self.z_sems[0]],
                recv_sem=rsem.at[self.z_sems[0] + slot], device_id=(lat, lat * 4 + xl * 2 + co), device_id_type=MESH,
            )

        def from_z(self, k):
            return pltpu.make_async_remote_copy(
                src_ref=self.wc, dst_ref=self.rz.at[k - 1], send_sem=ssem.at[self.z_sems[0]],
                recv_sem=rsem.at[self.z_sems[k - 1]], device_id=(lat, z_lons[k]), device_id_type=MESH,
            )

        def to_lat(self, k):
            return pltpu.make_async_remote_copy(
                src_ref=self.wl, dst_ref=self.wl, send_sem=ssem.at[self.lat_sems[k - 1]],
                recv_sem=rsem.at[self.lat_sems[0]], device_id=(lats[k], lon), device_id_type=MESH,
            )

        def along_z(self):
            arrive(self.copies)
            total = self.wa[y, x].astype(F32)
            for k in range(4 * ny - 1):
                total = total + self.rx[k].astype(F32)
            self.wc[...] = total.astype(BF)

            @pl.when(z != lat)
            def _():
                self.to_owner().start()

        def share(self):
            @pl.when(z == lat)
            def _():
                total = self.wc[...].astype(F32)
                for k in range(1, nz):
                    self.from_z(k).wait_recv()
                    total = total + self.rz[k - 1].astype(F32)
                self.wl[...] = total.astype(BF)
                for k in range(1, n_lat):
                    self.to_lat(k).start()

        def done(self):
            @pl.when(z != lat)
            def _():
                self.to_lat(1).wait_recv()
                self.to_owner().wait_send()

            self.out[...] = self.wl[...]

            @pl.when(z == lat)
            def _():
                for k in range(1, n_lat):
                    self.to_lat(k).wait_send()

    class LateSum(Sum):
        def __init__(self, refs, out):
            self.sb, self.rc, self.wa, self.rx, self.wc, self.wl = refs
            self.out = out
            self.copies = []
            self.steps = [self.core, self.along_zx, self.share, self.done]

        def along_zx(self):
            arrive(self.copies)
            self.wa[...] = (self.sb[co].astype(F32) + self.rc[...].astype(F32)).astype(BF)
            self.copies = []
            for k in range(1, 2 * nz):
                device = (lat, z_lons[k >> 1] ^ (2 * (k & 1)))
                target = self.wa.at[(z + (k >> 1)) & (nz - 1), xl ^ (k & 1)]
                self.copies.append(push(target, self.rx.at[k - 1], device))

        def share(self):
            arrive(self.copies)
            total = self.wa[z, xl].astype(F32)
            for k in range(2 * nz - 1):
                total = total + self.rx[k].astype(F32)
            self.wc[...] = total.astype(BF)
            self.copies = [push(self.wc, self.wl.at[lat], (lats[k], lon)) for k in range(1, n_lat)]
            self.wl[lat] = self.wc[...]

        def done(self):
            arrive(self.copies)
            total = self.wl[0].astype(F32)
            for k in range(1, n_lat):
                total = total + self.wl[k].astype(F32)
            self.out[...] = total.astype(BF)

    class TableSum:
        def __init__(self):
            self.copies = []
            self.steps = [self.pair, self.along_z, self.share_z, self.share_pair, self.done]

        def next(self):
            if self.steps:
                self.steps.pop(0)()

        def pair(self):
            for part in range(26):
                row, lanes = 16 * (part // 2), slice(128 * (part % 2), 128 * (part % 2) + 128)
                both = acc_ref[row : row + 16, lanes]
                tb_ref[part // 16, part // 8 % 2, part % 8] = both.astype(BF)
            for part in range(26, 32):
                tb_ref[part // 16, part // 8 % 2, part % 8] = jnp.zeros((16, 128), BF)
            for k in range(1, 4):
                device, its_xl, its_co = lon_pair[k]
                self.copies.append(push(tb_ref.at[its_co, its_xl], tr1_ref.at[k - 1], (lat, device)))

        def along_z(self):
            arrive(self.copies)
            total = tb_ref[co, xl].astype(F32)
            for k in range(3):
                total = total + tr1_ref[k].astype(F32)
            t1_ref[...] = total.astype(BF)
            self.copies = []
            for k in range(1, nz):
                self.copies.append(push(t1_ref.at[(z + k) & (nz - 1)], tr2_ref.at[k - 1], (lat, z_lons[k])))

        def share_z(self):
            arrive(self.copies)
            total = t1_ref[z].astype(F32)
            for k in range(nz - 1):
                total = total + tr2_ref[k].astype(F32)
            t2_ref[...] = total.astype(BF)
            self.copies = []
            for k in range(1, nz):
                self.copies.append(push(t2_ref, t3_ref.at[z], (lat, z_lons[k])))
            t3_ref[z] = t2_ref[...]

        def share_pair(self):
            arrive(self.copies)
            self.copies = []
            for k in range(1, 4):
                self.copies.append(push(t3_ref, t4_ref.at[co, xl], (lat, lon_pair[k][0])))
            t4_ref[co, xl] = t3_ref[...]

        def done(self):
            arrive(self.copies)
            tgrad_ref[...] = t4_ref[...]

    def send_quarters(which, devices):
        copies = []
        for quarter in range(1, 4):
            copies.append(push(hs_ref.at[which, quarter], hr_ref.at[which, quarter], devices[quarter]))
        hr_ref[which, 0] = hs_ref[which, 0]
        return copies

    pk_ref[...] = jnp.zeros_like(pk_ref)
    gall_ref[...] = jnp.zeros_like(gall_ref)
    r_ref[...] = jnp.zeros_like(r_ref)
    loads[0].wait()
    relative = rel_ref[...].astype(F32).T
    idx_ref[0:TOK, :] = relative[:, 0:128].astype(jnp.int32)
    idx_ref[TAIL : TAIL + 24, :] = pack_tail(relative[:, 128:TOK], 0).astype(jnp.int32)
    idx_ref[TAIL + 18 : ROWS, :] = jnp.full((ROWS - TAIL - 18, 128), -1, jnp.int32)
    low = (idx_ref[pl.ds(pl.multiple_of(co * half, 8), half), :] & 255).astype(F32).T
    for i in range(half // 8):
        low_ref[i] = low[:, 8 * i : 8 * i + 8]
    loads[1].wait()
    tabf_ref[...] = jnp.zeros_like(tabf_ref)
    for b in range(2):
        for part in range(13):
            width = min(256, POS - 256 * part)
            tabf_ref[b, 8 * part : 8 * part + 6, 0:width] = table_ref[6 * b : 6 * b + 6, 0, 256 * part : 256 * part + width]
        table = tabf_ref[b]
        coarse = table.astype(BF)
        tab_ref[b, 0:104, :] = coarse
        tab_ref[b, 104:208, :] = (table - coarse.astype(F32)).astype(BF)
    gather_bias(0)
    for load in loads[2:]:
        load.wait()
    x_ref[0] = moved(onehot(TOK, TOK, 0), tok_ref[...].reshape(TOK, C))
    hs_ref[0] = moved(onehot(192, TOK, 10), gmix_ref[...].reshape(TOK, C)).reshape(4, 48, C)

    first = forward(0)
    hs_ref[1] = moved(onehot(192, TOK, 2), first).reshape(4, 48, C)
    pl.semaphore_wait(barrier, len(greeted))
    copies_x = send_quarters(1, ahead)
    copies_g = send_quarters(0, ahead)
    gather_bias(1)
    acc_ref[...] = jnp.zeros_like(acc_ref)
    arrive(copies_x)
    arrive(copies_g)
    come = onehot(TOK, 192, 3)
    x_ref[1] = moved(come, hr_ref[1].reshape(192, C))
    grad_shifted = moved(come, hr_ref[0].reshape(192, C))

    second = forward(1)
    hs_ref[2] = moved(onehot(192, TOK, 4), second).reshape(4, 48, C)
    grad_second, *rest = backward(1, grad_shifted)
    hs_ref[3] = moved(onehot(192, TOK, 4), grad_second).reshape(4, 48, C)
    copies_s = send_quarters(3, back)
    copies_m = send_quarters(2, back)
    copies_two = share_scores(1)
    grad_down, grad_pre, grad_qkv = rest
    early_grads(1, grad_down, second_refs[0])
    late_grads(1, grad_pre, grad_qkv, second_refs[0], by_owner, 80)
    sum_two = Sum(second_refs, wg_ref.at[1])
    sum_early = Sum(early_refs, wg_ref.at[0, 0:80])
    sum_late = LateSum(late_refs, wg_ref.at[0, 80:128])
    sum_two.next()

    arrive(copies_s)
    grad_first = moved(onehot(TOK, 192, 5), hr_ref[3].reshape(192, C))
    def after_up(grad_down):
        sum_two.next()
        early_grads(0, grad_down, early_refs[0])
        sum_early.next()

    copies_one = []

    def after_scores():
        copies_one.extend(share_scores(0))
        sum_early.next()

    grad_in, _, grad_pre, grad_qkv = backward(0, grad_first, after_up, after_scores)
    add_scores([copies_one, copies_two])
    fold_tables()
    sum_table = TableSum()
    sum_table.next()
    late_grads(0, grad_pre, grad_qkv, late_refs[0], by_lon, 0)
    sum_late.next()
    sum_two.next()
    sum_table.next()
    sum_late.next()
    arrive(copies_m)
    mixed_ref[...] = moved(onehot(TOK, 192, 6), hr_ref[2].reshape(192, C)).reshape(72, 2, C)
    gtok_ref[...] = moved(onehot(TOK, TOK, 1), grad_in).reshape(72, 2, C)
    sum_early.next()
    sum_table.next()
    sum_two.next()
    sum_late.next()
    sum_early.next()
    sum_table.next()
    sum_two.next()
    sum_late.next()
    sum_early.next()
    sum_table.next()
    for copy in sent:
        copy.wait_send()


def finish(mixed_in, gtok_in, wg_in, table_in, mixed_ref, gtok_ref, qkv_ref, proj_ref, up_ref, down_ref, table_ref):
    mixed_ref[...] = mixed_in[...]
    gtok_ref[...] = gtok_in[...]
    for b in range(2):
        rows = wg_in[b].astype(F32)
        up_ref[b, :, 0:128] = rows[0:24, :]
        up_ref[b, :, 128:C] = rows[104:128, 64:128]
        qkv_ref[:, b, 0:128] = rows[80:98, :]
        qkv_ref[:, b, 128:C] = rows[104:122, 0:64]
        proj_ref[:, b, 0:128] = rows[98:104, :]
        proj_ref[:, b, 128:C] = rows[122:128, 0:64]
        for i in range(6):
            down_ref[:, b, 128 * i : 128 * i + 128] = rows[24 + 8 * i : 30 + 8 * i, :]
    for part in range(26):
        tile = table_in[part // 16, part // 8 % 2, part % 8].astype(F32)
        width = min(128, POS - 128 * part)
        for b in range(2):
            table_ref[6 * b : 6 * b + 6, 0, 128 * part : 128 * part + width] = tile[8 * b : 8 * b + 6, 0:width]


def per_device(tokens, grad_mixed, w_qkv, w_proj, w_up, w_down, gains, bias_table, rel_index, mask_ids):
    n_lat, n_lon = lax.axis_size("lat"), lax.axis_size("lon")
    ny, nz = n_lat // 2, n_lon // 4
    vmem = pl.BlockSpec(memory_space=pltpu.VMEM)
    smem = pl.BlockSpec(memory_space=pltpu.SMEM)

    def buf(*shape, dtype=BF):
        return pltpu.VMEM(shape, dtype)

    def stream(rows):
        return (
            buf(2, ny, 4, rows, 128), buf(ny, 4, rows, 128), buf(ny, 4, rows, 128), buf(4 * ny - 1, rows, 128),
            buf(rows, 128), buf(nz - 1, rows, 128), buf(rows, 128),
        )

    scratch = [
        buf(TOK, TOK, dtype=jnp.int32), buf(12, 1, POS, dtype=F32), buf(16, 768, dtype=jnp.int32),
        buf(72, 2, C), buf(72, 2, C), buf(2, C, 3 * C), buf(2, C, C), buf(2, 2, C, dtype=F32), buf(2, C, 768), buf(2, C, 768),
        buf(768, 3 * C), buf(768, C), buf(256, C), buf(256, 256),
        pltpu.SemaphoreType.DMA((14,)),
        buf(2, TOK, C), buf(2, TOK, 3 * C), buf(2, 6 * TOK, C), buf(2, 6 * TOK, C), buf(6 * TOK, TOK, dtype=F32),
        buf(2, 6 * TOK, TOK), buf(2, TOK, C), buf(2, TOK, C, dtype=F32), buf(2, TOK, 1, dtype=F32), buf(2, TOK, C),
        buf(2, TOK, 768, dtype=F32), buf(2, TOK, 768), buf(2, TOK, C, dtype=F32), buf(2, TOK, 1, dtype=F32),
        buf(2, TOK, 768), buf(6 * TOK, TOK),
        buf(ROWS, 128, dtype=jnp.int32), buf(ROWS // 16, 128, 8, dtype=F32), buf(2, 104, 256, dtype=F32), buf(2, 208, 256),
        buf(8 * 168, 128, dtype=F32), buf(6, 192, 128, dtype=F32), buf(6, 192, 128, dtype=F32),
        buf(2, 8 * ROWS, 128, dtype=F32), buf(2, 4 * ROWS, 128), buf(2, 4 * ROWS, 128),
        buf(ROWS // 2, 16, 128), buf(208, 256, dtype=F32),
        buf(TOK, 256), buf(768, 256, dtype=F32), buf(768, 128, dtype=F32), buf(256, 768, dtype=F32),
        buf(4, 4, 48, C), buf(4, 4, 48, C),
        stream(128), stream(80),
        (
            buf(2, nz, 2, 48, 128), buf(nz, 2, 48, 128), buf(nz, 2, 48, 128), buf(2 * nz - 1, 48, 128),
            buf(48, 128), buf(n_lat, 48, 128),
        ),
        buf(2, 2, 8, 16, 128), buf(3, 8, 16, 128), buf(8, 16, 128), buf(7, 16, 128), buf(16, 128),
        buf(8, 16, 128), buf(2, 2, 8, 16, 128),
        pltpu.SemaphoreType.DMA((N_SEMS,)), pltpu.SemaphoreType.DMA((N_SEMS,)),
    ]
    results = pl.pallas_call(
        functools.partial(kernel, n_lat, n_lon),
        out_shape=(
            jax.ShapeDtypeStruct((72, 2, C), BF),
            jax.ShapeDtypeStruct((72, 2, C), BF),
            jax.ShapeDtypeStruct((2, 128, 128), BF),
            jax.ShapeDtypeStruct((2, 2, 8, 16, 128), BF),
        ),
        in_specs=[pl.BlockSpec(memory_space=pltpu.HBM)] * 14 + [smem],
        out_specs=[vmem] * 4,
        scratch_shapes=scratch,
        compiler_params=pltpu.CompilerParams(
            collective_id=0, has_side_effects=True, vmem_limit_bytes=60 * 1024 * 1024
        ),
    )(
        rel_index,
        bias_table.reshape(12, 1, POS),
        jnp.asarray(index_rows()),
        tokens.transpose(1, 2, 0, 3).reshape(72, 2, C),
        grad_mixed.transpose(1, 2, 0, 3).reshape(72, 2, C),
        w_qkv, w_proj, gains, w_up, w_down.transpose(0, 2, 1),
        *permutations(),
        mask_ids,
    )
    mixed, grad_tokens, qkv, proj, up, down, table = pl.pallas_call(
        finish,
        out_shape=(
            jax.ShapeDtypeStruct((72, 2, C), BF),
            jax.ShapeDtypeStruct((72, 2, C), BF),
            jax.ShapeDtypeStruct((18, 2, C), F32),
            jax.ShapeDtypeStruct((6, 2, C), F32),
            jax.ShapeDtypeStruct((2, 24, C), F32),
            jax.ShapeDtypeStruct((6, 2, 768), F32),
            jax.ShapeDtypeStruct((12, 1, POS), F32),
        ),
        in_specs=[vmem] * 4,
        out_specs=[vmem] * 7,
        compiler_params=pltpu.CompilerParams(vmem_limit_bytes=60 * 1024 * 1024),
    )(*results)

    def field(value):
        return value.reshape(6, 12, 2, C).transpose(2, 0, 1, 3)

    return (
        field(mixed),
        field(grad_tokens),
        qkv.transpose(1, 2, 0),
        proj.transpose(1, 2, 0),
        up.transpose(0, 2, 1),
        down.transpose(1, 2, 0),
        table.reshape(2, 1, 1, 6, POS),
    )


def solution(mesh):
    field = P(None, "lat", "lon", None)
    table = P(None, None, "lat", None, None)
    in_specs = (field, field, P(), P(), P(), P(), P(), table, P(), P("lat"))
    columns = P(None, None, "lon")
    out_specs = (field, field, columns, columns, columns, columns, table)
    return jax.shard_map(per_device, mesh=mesh, in_specs=in_specs, out_specs=out_specs, check_vma=False)
```

```python
import functools

import jax
import jax.numpy as jnp
import numpy as np
from jax import lax
from jax.experimental import pallas as pl
from jax.experimental.pallas import tpu as pltpu
from jax.sharding import PartitionSpec as P

HEADS = 6
C = 192
TOK = 144
POS = 3312
EPS = 1e-05
NEGATIVE = -1e30
SCALE = 32 ** -0.5
BF = jnp.bfloat16
F32 = jnp.float32
MESH = pl.DeviceIdType.MESH
ROWS = 192
TAIL = 144
N_SEMS = 132


def index_rows():
    rows = np.full((16, 768), -1, np.int32)
    tok = np.arange(TOK)
    level, row, col = tok // 72, tok // 12 % 6, tok % 12
    place = 24 * row + 2 * col + level
    own = 18 * level + row % 3 * 6 + col % 6
    other = 18 * (1 - level) + row % 3 * 6 + col % 6
    low = 48 * (2 * (row // 3) + col // 6)
    high = 48 * (2 * (1 - row // 3) + 1 - col // 6)
    rows[0, place] = tok
    rows[1, tok] = place
    rows[2, tok] = high + own
    rows[3, low + other] = tok
    rows[4, tok] = low + own
    rows[5, high + other] = tok
    rows[6, high + other] = place
    rows[10, place] = high + own
    return rows


def permutations():
    qkv = np.zeros((3 * C, 768), np.float32)
    proj = np.zeros((C, 768), np.float32)
    down = np.zeros((C, 256), np.float32)
    for piece in range(32):
        for i in range(18):
            qkv[18 * piece + i, 24 * piece + i] = 1
        for i in range(6):
            proj[6 * piece + i, 24 * piece + 18 + i] = 1
            down[6 * piece + i, 8 * piece + i] = 1
    return tuple(jnp.asarray(matrix, BF) for matrix in (qkv.T, proj.T, down.T, np.eye(256, dtype=np.float32)))


def dot(a, b):
    return jnp.dot(a, b, preferred_element_type=F32)


def dot_nt(a, b):
    return lax.dot_general(a, b, (((1,), (1,)), ((), ())), preferred_element_type=F32)


def dot_tn(a, b):
    return lax.dot_general(a, b, (((0,), (0,)), ((), ())), preferred_element_type=F32)


def normal(u):
    power = jnp.exp(u * u * -0.5)
    place = 1.0 / (1.0 + jnp.abs(u) * (0.3275911 * 0.5**0.5))
    upper = 0.5 * 1.061405429
    for term in (-1.453152027, 1.421413741, -0.284496736, 0.254829592):
        upper = upper * place + 0.5 * term
    upper = upper * place * power
    return jnp.where(u < 0.0, upper, 1.0 - upper), power * 0.3989422804014327


def norm_parts(v):
    center = v - jnp.mean(v, axis=-1, keepdims=True)
    spread = jnp.mean(center * center, axis=-1, keepdims=True)
    inverse = lax.rsqrt(spread + EPS)
    return center * inverse, inverse


def norm_back(grad, unit, inverse):
    along = jnp.mean(grad * unit, axis=-1, keepdims=True)
    return inverse * (grad - jnp.mean(grad, axis=-1, keepdims=True) - unit * along)


def kernel(
    n_lat, n_lon,
    rel_hbm, table_hbm, const_hbm, tok_hbm, gmix_hbm, wqkv_hbm, wproj_hbm, gains_hbm, wup_hbm, wdown_hbm, pq_hbm, pp_hbm, pd_hbm, eye_hbm, ids_ref,
    mixed_ref, gtok_ref, gqkv_out, gproj_out, gup_out, gdown_out, tgrad_ref,
    rel_ref, table_ref, const_ref, tok_ref, gmix_ref, wqkv_ref, wproj_ref, gains_ref, wup_ref, wdown_ref, pq_ref, pp_ref, pd_ref, eye_ref, load_sem,
    x_ref, qkv_ref, km_ref, vm_ref, s_ref, p_ref, att_ref, u1_ref, i1_ref, mid_ref, gp_ref, hid_ref, u2_ref, i2_ref,
    gup_ref, ds_ref, idx_ref, low_ref, tabf_ref, tab_ref, bias_ref, btail_ref, pk_ref, gall_ref, gsend_ref, grecv_ref, gx_ref, acc_ref,
    r_ref, o1_ref, o2_ref, o3_ref,
    hs_ref, hr_ref,
    second_refs, early_refs, late_refs,
    tb_ref, tr1_ref, t1_ref, tr2_ref, t2_ref, t3_ref, t4_ref,
    ssem, rsem,
):
    loads = [
        pltpu.make_async_copy(src, dst, load_sem.at[k])
        for k, (src, dst) in enumerate([
            (rel_hbm, rel_ref), (table_hbm, table_ref), (const_hbm, const_ref), (tok_hbm, tok_ref), (gmix_hbm, gmix_ref),
            (wqkv_hbm, wqkv_ref), (wproj_hbm, wproj_ref), (gains_hbm, gains_ref), (wup_hbm, wup_ref), (wdown_hbm, wdown_ref),
            (pq_hbm, pq_ref), (pp_hbm, pp_ref), (pd_hbm, pd_ref), (eye_hbm, eye_ref),
        ])
    ]
    for load in loads:
        load.start()
    ny, nz = n_lat // 2, n_lon // 4
    lat, lon = lax.axis_index("lat"), lax.axis_index("lon")
    y, xh = lat >> 1, lat & 1
    z, xl, co = lon >> 2, (lon >> 1) & 1, lon & 1
    x = xh * 2 + xl
    lon_pair = [(lon ^ k, xl ^ (k >> 1), co ^ (k & 1)) for k in range(4)]
    lats = [(lat + k) & (n_lat - 1) for k in range(n_lat)]
    ahead = [((lat - a) & (n_lat - 1), (lon - b) & (n_lon - 1)) for a in (0, 1) for b in (0, 1)]
    back = [((lat + a) & (n_lat - 1), (lon + b) & (n_lon - 1)) for a in (0, 1) for b in (0, 1)]
    z_lons = [(lon + 4 * k) & (n_lon - 1) for k in range(nz)]
    ys, xs = [(y + k) & (ny - 1) for k in range(ny)], [(x + k) & 3 for k in range(4)]
    xy_lons = [lon - xl * 2 + (its_x & 1) * 2 for its_x in xs]
    xy_lats = [[its_y * 2 + (its_x >> 1) for its_x in xs] for its_y in ys]

    greeted = [(lats[k], lon) for k in range(1, n_lat)]
    greeted += [(lat, z_lons[k]) for k in range(1, nz)]
    greeted += [(lat, lon_pair[k][0]) for k in (1, 3)]
    greeted += [(lats[k], lon_pair[2][0]) for k in range(n_lat)]
    greeted += [ahead[1], ahead[3], back[1], back[3]]
    barrier = pltpu.get_barrier_semaphore()
    for device in greeted:
        pl.semaphore_signal(barrier, inc=1, device_id=device, device_id_type=MESH)

    sems = iter(range(N_SEMS))
    sent = []

    def push(src, dst, device):
        k = next(sems)
        copy = pltpu.make_async_remote_copy(
            src_ref=src, dst_ref=dst, send_sem=ssem.at[k], recv_sem=rsem.at[k], device_id=device, device_id_type=MESH
        )
        copy.start()
        sent.append(copy)
        return copy

    def arrive(copies):
        for copy in copies:
            copy.wait_recv()

    def onehot(n_rows, n_lanes, which):
        place = lax.broadcasted_iota(jnp.int32, (n_rows, n_lanes), 0)
        return jnp.where(place == const_ref[which : which + 1, :n_lanes], 1.0, 0.0).astype(BF)

    def moved(matrix, value):
        return dot(matrix, value).astype(BF)

    lane = lax.broadcasted_iota(jnp.int32, (1, C), 1)
    head_lanes = [(lane >= 32 * h) & (lane < 32 * h + 32) for h in range(HEADS)]

    def of_head(value, h):
        return jnp.where(head_lanes[h], value, jnp.zeros_like(value))

    def pack_tail(value, h):
        pk_ref[h, 0:TOK, 0:16] = value
        total = pk_ref[h, pl.ds(0, 24, stride=8), :]
        for j in range(1, 8):
            total = total + pltpu.roll(pk_ref[h, pl.ds(j, 24, stride=8), :], 16 * j, 1)
        return total

    def unpack_tail(value, k):
        for j in range(8):
            rolled = pltpu.roll(value, (128 - 16 * j) % 128, 1)
            btail_ref[k, pl.ds(j, 24, stride=8), :] = rolled

    def gather_bias(b):
        place = lax.broadcasted_iota(jnp.int32, (256, 128), 0).astype(BF)
        one, zero = jnp.ones((256, 128), BF), jnp.zeros((256, 128), BF)

        def step(i, carry):
            for m in range(7):
                group = i * 7 + m
                index = idx_ref[pl.ds(pl.multiple_of(group * 8, 8), 8), :]
                low, high = (index & 255).astype(F32), index >> 8
                picks = []
                for r in range(8):
                    row = jnp.broadcast_to(low[r : r + 1, :], (16, 128)).astype(BF)
                    picks.append(jnp.where(place == jnp.concatenate([row] * 16, axis=0), one, zero))
                rows = dot(tab_ref[b], jnp.concatenate(picks, axis=1))
                for r in range(8):
                    high_row = jnp.broadcast_to(high[r : r + 1, :], (8, 128))
                    found = jnp.zeros((8, 128), F32)
                    for part in range(13):
                        coarse = rows[8 * part : 8 * part + 8, 128 * r : 128 * r + 128]
                        fine = rows[104 + 8 * part : 112 + 8 * part, 128 * r : 128 * r + 128]
                        found = jnp.where(high_row == part, coarse + fine, found)
                    bias_ref[pl.ds(pl.multiple_of(group * 64 + r * 8, 8), 8), :] = found
            return carry

        lax.fori_loop(0, 3, step, 0)
        for h in range(HEADS):
            unpack_tail(bias_ref[pl.ds(8 * TAIL + h, 24, stride=8), :], h)

    half = ROWS // 2

    def share_scores(b):
        gsend_ref[b] = gall_ref[b, pl.ds((1 - co) * 8 * half, 8 * half), :].astype(BF)
        return [push(gsend_ref.at[b], grecv_ref.at[b], (lat, lon_pair[1][0]))]

    def add_scores(copies):
        both = []
        for b in range(2):
            arrive(copies[b])
            total = gall_ref[b, pl.ds(co * 8 * half, 8 * half), :] + grecv_ref[b].astype(F32)
            both.append(total.reshape(half, 8, 128))
        gx_ref[...] = jnp.concatenate(both, axis=1).astype(BF)

    def fold_tables():
        place = lax.broadcasted_iota(jnp.int32, (128, 256), 1).astype(BF)
        one, zero = jnp.ones((128, 256), BF), jnp.zeros((128, 256), BF)
        nothing = jnp.zeros((16, 128), BF)

        def step(i, carry):
            total = acc_ref[...]
            for m in range(6):
                group = i * 6 + m
                start = pl.multiple_of(co * half + group * 8, 8)
                high = (idx_ref[pl.ds(start, 8), :] >> 8).astype(F32)
                block = low_ref[group]
                left, right = [[] for _ in range(13)], []
                for r in range(8):
                    high_row = jnp.broadcast_to(high[r : r + 1, :], (16, 128)).astype(BF)
                    grads = gx_ref[group * 8 + r]
                    for part in range(13):
                        left[part].append(jnp.where(high_row == jnp.full((16, 128), part, BF), grads, nothing))
                    column = jnp.broadcast_to(block[:, r : r + 1], (128, 128)).astype(BF)
                    right.append(jnp.where(place == jnp.concatenate([column] * 2, axis=1), one, zero))
                left = jnp.concatenate([jnp.concatenate(rows, axis=1) for rows in left], axis=0)
                total = total + dot(left, jnp.concatenate(right, axis=0))
            acc_ref[...] = total
            return carry

        lax.fori_loop(0, 2, step, 0)

    def region_codes(place):
        code = jnp.zeros_like(place)
        for part in range(12):
            value = ids_ref[part % 6] + 64 * (part // 6)
            code = jnp.where(place >= 12 * part, value, code)
        return code

    def forward(b):
        tokens = x_ref[b]
        qkv_ref[b] = dot(tokens, wqkv_ref[b]).astype(BF)
        q, k, v = (qkv_ref[b, :, C * i : C * i + C] for i in range(3))
        for h in range(HEADS):
            km_ref[b, TOK * h : TOK * h + TOK, :] = of_head(k, h)
            vm_ref[b, TOK * h : TOK * h + TOK, :] = of_head(v, h)
        s_ref[...] = dot_nt(km_ref[b], q)
        if b == 1:
            codes_t = region_codes(lax.broadcasted_iota(jnp.int32, (TOK, 1), 0))
            codes_s = region_codes(lax.broadcasted_iota(jnp.int32, (1, TOK), 1))
            allowed = codes_s == codes_t
        for h in range(HEADS):
            span = pl.ds(TOK * h, TOK)
            bias = jnp.concatenate([bias_ref[pl.ds(h, TOK, stride=8), :], btail_ref[h, 0:TOK, 0:16]], axis=1)
            scores = s_ref[span, :] * SCALE + bias
            if b == 1:
                scores = jnp.where(allowed, scores, NEGATIVE)
            powers = jnp.exp(scores - jnp.max(scores, axis=0, keepdims=True))
            probs = powers * (1.0 / jnp.sum(powers, axis=0, keepdims=True))
            p_ref[b, span, :] = probs.astype(BF)
        attended = dot_tn(p_ref[b], vm_ref[b]).astype(BF)
        att_ref[b] = attended
        unit, inverse = norm_parts(dot(attended, wproj_ref[b]))
        u1_ref[b], i1_ref[b] = unit, inverse
        middle = (tokens.astype(F32) + unit * gains_ref[b, 0:1, :]).astype(BF)
        mid_ref[b] = middle
        for part in range(3):
            cols = pl.ds(256 * part, 256)
            up = dot(middle, wup_ref[b, :, cols])
            phi, density = normal(up)
            hid_ref[b, :, cols] = (up * phi).astype(BF)
            gp_ref[b, :, cols] = phi + up * density
        unit, inverse = norm_parts(dot_nt(hid_ref[b], wdown_ref[b]))
        u2_ref[b], i2_ref[b] = unit, inverse
        return (middle.astype(F32) + unit * gains_ref[b, 1:2, :]).astype(BF)

    def backward(b, grad, after_up=lambda grad_down: None, after_scores=lambda: None):
        grad = grad.astype(F32)
        grad_down = norm_back(grad * gains_ref[b, 1:2, :], u2_ref[b], i2_ref[b]).astype(BF)
        for part in range(3):
            cols = pl.ds(256 * part, 256)
            grad_hidden = dot(grad_down, wdown_ref[b, :, cols])
            gup_ref[b, :, cols] = (grad_hidden * gp_ref[b, :, cols]).astype(BF)
        grad_middle = grad + dot_nt(gup_ref[b], wup_ref[b])
        after_up(grad_down)
        grad_pre = norm_back(grad_middle * gains_ref[b, 0:1, :], u1_ref[b], i1_ref[b]).astype(BF)
        grad_att = dot_nt(grad_pre, wproj_ref[b]).astype(BF)
        q = qkv_ref[b, :, 0:C]
        s_ref[...] = dot_nt(vm_ref[b], grad_att)
        for h in range(HEADS):
            span = pl.ds(TOK * h, TOK)
            probs = p_ref[b, span, :].astype(F32)
            grad_probs = s_ref[span, :]
            grad_scores = probs * (grad_probs - jnp.sum(grad_probs * probs, axis=0, keepdims=True))
            ds_ref[span, :] = grad_scores.astype(BF)
            gall_ref[b, pl.ds(h, TOK, stride=8), :] = grad_scores[:, 0:128]
            gall_ref[b, pl.ds(8 * TAIL + h, 24, stride=8), :] = pack_tail(grad_scores[:, 128:TOK], h)
        after_scores()
        grad_q = dot_tn(ds_ref[...], km_ref[b])
        grad_k, grad_v = jnp.zeros((TOK, C), F32), jnp.zeros((TOK, C), F32)
        for h in range(HEADS):
            span = pl.ds(TOK * h, TOK)
            grad_k = jnp.where(head_lanes[h], dot(ds_ref[span, :], q), grad_k)
            grad_v = jnp.where(head_lanes[h], dot(p_ref[b, span, :], grad_att), grad_v)
        grad_qkv = jnp.concatenate([grad_q * SCALE, grad_k * SCALE, grad_v], axis=1).astype(BF)

        def grad_in():
            return (grad_middle + dot_nt(grad_qkv, wqkv_ref[b])).astype(BF)

        return grad_in, grad_down, grad_pre, grad_qkv

    def by_owner(buffer, piece):
        return buffer.at[piece % 2, piece // 8, piece // 4 % 2 * 2 + piece // 2 % 2]

    def pack(place, first_row, units):
        for tile in range(len(units) // 2):
            pair = jnp.concatenate([units[2 * tile], units[2 * tile + 1]], axis=0).astype(BF)
            row = first_row + 16 * tile
            place[row : row + 16, :] = pair

    def early_grads(b, grad_down, buffer):
        r_ref[:, 0:128] = mid_ref[b, :, 0:128]
        r_ref[:, C:256] = mid_ref[b, :, 128:C]
        for part in range(3):
            span = slice(256 * part, 256 * part + 256)
            turned = dot_nt(eye_ref[...], gup_ref[b, :, span]).astype(BF)
            grads = dot(turned, r_ref[...])
            o2_ref[span, :] = grads[:, 0:128]
            o1_ref[span, C:256] = grads[:, C:256]
        o3_ref[...] = dot(dot_nt(pd_ref[...], grad_down).astype(BF), hid_ref[b])
        for piece in range(32):
            units = [o2_ref[24 * piece + 8 * i : 24 * piece + 8 * i + 8, :] for i in range(3)]
            units += [o3_ref[8 * piece : 8 * piece + 8, 128 * i : 128 * i + 128] for i in range(6)]
            pack(by_owner(buffer, piece), 0, units + [jnp.zeros((8, 128), F32)])

    def late_grads(b, grad_pre, grad_qkv, buffer, first_row):
        turned = dot_nt(pp_ref[...], grad_pre).astype(BF)
        grads = dot(turned, att_ref[b])
        turned = dot_nt(pq_ref[...], grad_qkv).astype(BF)
        o1_ref[:, 0:C] = grads + dot(turned, x_ref[b])
        for piece in range(32):
            units = [o1_ref[24 * piece + 8 * i : 24 * piece + 8 * i + 8, 128 * m : 128 * m + 128] for m in range(2) for i in range(3)]
            pack(by_owner(buffer, piece), first_row, units)

    class Sum:
        def __init__(self, refs):
            self.sb, self.rc, self.wa, self.rx, self.wc, self.rz, self.wl = refs
            self.copies = []
            self.steps = [self.core, self.along_xy, self.along_z, self.share, self.done]
            self.z_sems = [next(sems) for _ in range(nz - 1)]
            self.lat_sems = [next(sems) for _ in range(n_lat - 1)]

        def next(self):
            if self.steps:
                self.steps.pop(0)()

        def core(self):
            self.copies = [push(self.sb.at[1 - co], self.rc, (lat, lon_pair[1][0]))]

        def along_xy(self):
            arrive(self.copies)
            self.wa[...] = (self.sb[co].astype(F32) + self.rc[...].astype(F32)).astype(BF)
            self.copies = []
            for k in range(1, 4 * ny):
                device = (xy_lats[k // 4][k % 4], xy_lons[k % 4])
                self.copies.append(push(self.wa.at[ys[k // 4], xs[k % 4]], self.rx.at[k - 1], device))

        def to_owner(self):
            slot = ((z - lat) & (nz - 1)) - 1
            return pltpu.make_async_remote_copy(
                src_ref=self.wc, dst_ref=self.rz.at[slot], send_sem=ssem.at[self.z_sems[0]],
                recv_sem=rsem.at[self.z_sems[0] + slot], device_id=(lat, lat * 4 + xl * 2 + co), device_id_type=MESH,
            )

        def from_z(self, k):
            return pltpu.make_async_remote_copy(
                src_ref=self.wc, dst_ref=self.rz.at[k - 1], send_sem=ssem.at[self.z_sems[0]],
                recv_sem=rsem.at[self.z_sems[k - 1]], device_id=(lat, z_lons[k]), device_id_type=MESH,
            )

        def to_lat(self, k):
            return pltpu.make_async_remote_copy(
                src_ref=self.wl, dst_ref=self.wl, send_sem=ssem.at[self.lat_sems[k - 1]],
                recv_sem=rsem.at[self.lat_sems[0]], device_id=(lats[k], lon), device_id_type=MESH,
            )

        def along_z(self):
            arrive(self.copies)
            total = self.wa[y, x].astype(F32)
            for k in range(4 * ny - 1):
                total = total + self.rx[k].astype(F32)
            self.wc[...] = total.astype(BF)

            @pl.when(z != lat)
            def _():
                self.to_owner().start()

        def share(self):
            @pl.when(z == lat)
            def _():
                total = self.wc[...].astype(F32)
                for k in range(1, nz):
                    self.from_z(k).wait_recv()
                    total = total + self.rz[k - 1].astype(F32)
                self.wl[...] = total.astype(BF)
                for k in range(1, n_lat):
                    self.to_lat(k).start()

        def done(self):
            @pl.when(z != lat)
            def _():
                self.to_lat(1).wait_recv()
                self.to_owner().wait_send()

            @pl.when(z == lat)
            def _():
                for k in range(1, n_lat):
                    self.to_lat(k).wait_send()

    class TableSum:
        def __init__(self):
            self.copies = []
            self.steps = [self.pair, self.along_z, self.share_z, self.share_pair, self.done]

        def next(self):
            if self.steps:
                self.steps.pop(0)()

        def pair(self):
            for part in range(26):
                row, lanes = 16 * (part // 2), slice(128 * (part % 2), 128 * (part % 2) + 128)
                both = acc_ref[row : row + 16, lanes]
                tb_ref[part // 16, part // 8 % 2, part % 8] = both.astype(BF)
            for part in range(26, 32):
                tb_ref[part // 16, part // 8 % 2, part % 8] = jnp.zeros((16, 128), BF)
            for k in range(1, 4):
                device, its_xl, its_co = lon_pair[k]
                self.copies.append(push(tb_ref.at[its_co, its_xl], tr1_ref.at[k - 1], (lat, device)))

        def along_z(self):
            arrive(self.copies)
            total = tb_ref[co, xl].astype(F32)
            for k in range(3):
                total = total + tr1_ref[k].astype(F32)
            t1_ref[...] = total.astype(BF)
            self.copies = []
            for k in range(1, nz):
                self.copies.append(push(t1_ref.at[(z + k) & (nz - 1)], tr2_ref.at[k - 1], (lat, z_lons[k])))

        def share_z(self):
            arrive(self.copies)
            total = t1_ref[z].astype(F32)
            for k in range(nz - 1):
                total = total + tr2_ref[k].astype(F32)
            t2_ref[...] = total.astype(BF)
            self.copies = []
            for k in range(1, nz):
                self.copies.append(push(t2_ref, t3_ref.at[z], (lat, z_lons[k])))
            t3_ref[z] = t2_ref[...]

        def share_pair(self):
            arrive(self.copies)
            self.copies = []
            for k in range(1, 4):
                self.copies.append(push(t3_ref, t4_ref.at[co, xl], (lat, lon_pair[k][0])))
            t4_ref[co, xl] = t3_ref[...]

        def done(self):
            arrive(self.copies)

    def write_grads(b, rows):
        gup_out[b, :, 0:128] = rows[0:24, :]
        for i in range(6):
            gdown_out[:, b, 128 * i : 128 * i + 128] = rows[24 + 8 * i : 30 + 8 * i, :]
        main, tail = rows[80:104, :], rows[104:128, :]
        gqkv_out[:, b, 0:128], gproj_out[:, b, 0:128] = main[0:18, :], main[18:24, :]
        gqkv_out[:, b, 128:C], gproj_out[:, b, 128:C] = tail[0:18, 0:64], tail[18:24, 0:64]
        gup_out[b, :, 128:C] = tail[:, 64:128]

    def send_quarters(which, devices):
        copies = []
        for quarter in range(1, 4):
            copies.append(push(hs_ref.at[which, quarter], hr_ref.at[which, quarter], devices[quarter]))
        hr_ref[which, 0] = hs_ref[which, 0]
        return copies

    pk_ref[...] = jnp.zeros_like(pk_ref)
    gall_ref[...] = jnp.zeros_like(gall_ref)
    r_ref[...] = jnp.zeros_like(r_ref)
    loads[0].wait()
    relative = rel_ref[...].astype(F32).T
    idx_ref[0:TOK, :] = relative[:, 0:128].astype(jnp.int32)
    idx_ref[TAIL : TAIL + 24, :] = pack_tail(relative[:, 128:TOK], 0).astype(jnp.int32)
    idx_ref[TAIL + 18 : ROWS, :] = jnp.full((ROWS - TAIL - 18, 128), -1, jnp.int32)
    low = (idx_ref[pl.ds(pl.multiple_of(co * half, 8), half), :] & 255).astype(F32).T
    for i in range(half // 8):
        low_ref[i] = low[:, 8 * i : 8 * i + 8]
    loads[1].wait()
    tabf_ref[...] = jnp.zeros_like(tabf_ref)
    for b in range(2):
        for part in range(13):
            width = min(256, POS - 256 * part)
            tabf_ref[b, 8 * part : 8 * part + 6, 0:width] = table_ref[6 * b : 6 * b + 6, 0, 256 * part : 256 * part + width]
        table = tabf_ref[b]
        coarse = table.astype(BF)
        tab_ref[b, 0:104, :] = coarse
        tab_ref[b, 104:208, :] = (table - coarse.astype(F32)).astype(BF)
    gather_bias(0)
    for load in loads[2:]:
        load.wait()
    x_ref[0] = moved(onehot(TOK, TOK, 0), tok_ref[...].reshape(TOK, C))
    hs_ref[0] = moved(onehot(192, TOK, 10), gmix_ref[...].reshape(TOK, C)).reshape(4, 48, C)

    first = forward(0)
    hs_ref[1] = moved(onehot(192, TOK, 2), first).reshape(4, 48, C)
    pl.semaphore_wait(barrier, len(greeted))
    copies_x = send_quarters(1, ahead)
    copies_g = send_quarters(0, ahead)
    gather_bias(1)
    acc_ref[...] = jnp.zeros_like(acc_ref)
    arrive(copies_x)
    arrive(copies_g)
    come = onehot(TOK, 192, 3)
    x_ref[1] = moved(come, hr_ref[1].reshape(192, C))
    grad_shifted = moved(come, hr_ref[0].reshape(192, C))

    second = forward(1)
    hs_ref[2] = moved(onehot(192, TOK, 4), second).reshape(4, 48, C)
    grad_second, *rest = backward(1, grad_shifted)
    hs_ref[3] = moved(onehot(192, TOK, 4), grad_second()).reshape(4, 48, C)
    copies_s = send_quarters(3, back)
    copies_m = send_quarters(2, back)
    copies_two = share_scores(1)
    grad_down, grad_pre, grad_qkv = rest
    early_grads(1, grad_down, second_refs[0])
    late_grads(1, grad_pre, grad_qkv, second_refs[0], 80)
    sum_two, sum_early, sum_late = Sum(second_refs), Sum(early_refs), Sum(late_refs)
    sum_two.next()

    arrive(copies_s)
    grad_first = moved(onehot(TOK, 192, 5), hr_ref[3].reshape(192, C))
    def after_up(grad_down):
        sum_two.next()
        early_grads(0, grad_down, early_refs[0])
        sum_early.next()

    copies_one = []

    def after_scores():
        copies_one.extend(share_scores(0))
        sum_early.next()

    grad_in, _, grad_pre, grad_qkv = backward(0, grad_first, after_up, after_scores)
    add_scores([copies_one, copies_two])
    fold_tables()
    sum_table = TableSum()
    sum_table.next()
    sum_two.next()
    late_grads(0, grad_pre, grad_qkv, late_refs[0], 0)
    sum_late.next()
    sum_table.next()
    sum_late.next()
    gtok_ref[...] = moved(onehot(TOK, TOK, 1), grad_in()).reshape(72, 2, C)
    sum_table.next()
    sum_early.next()
    arrive(copies_m)
    mixed_ref[...] = moved(onehot(TOK, 192, 6), hr_ref[2].reshape(192, C)).reshape(72, 2, C)
    sum_table.next()
    sum_two.next()
    sum_late.next()
    sum_early.next()
    sum_late.next()
    sum_two.next()
    write_grads(1, second_refs[-1][...].astype(F32))
    sum_table.next()
    for part in range(26):
        tile = t4_ref[part // 16, part // 8 % 2, part % 8].astype(F32)
        width = min(128, POS - 128 * part)
        for b in range(2):
            tgrad_ref[6 * b : 6 * b + 6, 0, 128 * part : 128 * part + width] = tile[8 * b : 8 * b + 6, 0:width]
    sum_early.next()
    sum_late.next()
    write_grads(0, jnp.concatenate([early_refs[-1][...].astype(F32), late_refs[-1][...].astype(F32)], axis=0))
    for copy in sent:
        copy.wait_send()


def hand_over(*refs):
    sources, targets, sems = refs[:7], refs[7:14], refs[14]
    copies = [pltpu.make_async_copy(source, target, sems.at[k]) for k, (source, target) in enumerate(zip(sources, targets))]
    for copy in copies:
        copy.start()
    for copy in copies:
        copy.wait()


def per_device(tokens, grad_mixed, w_qkv, w_proj, w_up, w_down, gains, bias_table, rel_index, mask_ids):
    n_lat, n_lon = lax.axis_size("lat"), lax.axis_size("lon")
    ny, nz = n_lat // 2, n_lon // 4
    vmem = pl.BlockSpec(memory_space=pltpu.VMEM)
    smem = pl.BlockSpec(memory_space=pltpu.SMEM)

    def buf(*shape, dtype=BF):
        return pltpu.VMEM(shape, dtype)

    def stream(rows):
        return (
            buf(2, ny, 4, rows, 128), buf(ny, 4, rows, 128), buf(ny, 4, rows, 128), buf(4 * ny - 1, rows, 128),
            buf(rows, 128), buf(nz - 1, rows, 128), buf(rows, 128),
        )

    scratch = [
        buf(TOK, TOK, dtype=jnp.int32), buf(12, 1, POS, dtype=F32), buf(16, 768, dtype=jnp.int32),
        buf(72, 2, C), buf(72, 2, C), buf(2, C, 3 * C), buf(2, C, C), buf(2, 2, C, dtype=F32), buf(2, C, 768), buf(2, C, 768),
        buf(768, 3 * C), buf(768, C), buf(256, C), buf(256, 256),
        pltpu.SemaphoreType.DMA((14,)),
        buf(2, TOK, C), buf(2, TOK, 3 * C), buf(2, 6 * TOK, C), buf(2, 6 * TOK, C), buf(6 * TOK, TOK, dtype=F32),
        buf(2, 6 * TOK, TOK), buf(2, TOK, C), buf(2, TOK, C, dtype=F32), buf(2, TOK, 1, dtype=F32), buf(2, TOK, C),
        buf(2, TOK, 768, dtype=F32), buf(2, TOK, 768), buf(2, TOK, C, dtype=F32), buf(2, TOK, 1, dtype=F32),
        buf(2, TOK, 768), buf(6 * TOK, TOK),
        buf(ROWS, 128, dtype=jnp.int32), buf(ROWS // 16, 128, 8, dtype=F32), buf(2, 104, 256, dtype=F32), buf(2, 208, 256),
        buf(8 * 168, 128, dtype=F32), buf(6, 192, 128, dtype=F32), buf(6, 192, 128, dtype=F32),
        buf(2, 8 * ROWS, 128, dtype=F32), buf(2, 4 * ROWS, 128), buf(2, 4 * ROWS, 128),
        buf(ROWS // 2, 16, 128), buf(208, 256, dtype=F32),
        buf(TOK, 256), buf(768, 256, dtype=F32), buf(768, 128, dtype=F32), buf(256, 768, dtype=F32),
        buf(4, 4, 48, C), buf(4, 4, 48, C),
        stream(128), stream(80), stream(48),
        buf(2, 2, 8, 16, 128), buf(3, 8, 16, 128), buf(8, 16, 128), buf(7, 16, 128), buf(16, 128),
        buf(8, 16, 128), buf(2, 2, 8, 16, 128),
        pltpu.SemaphoreType.DMA((N_SEMS,)), pltpu.SemaphoreType.DMA((N_SEMS,)),
    ]
    shapes = (
        jax.ShapeDtypeStruct((72, 2, C), BF),
        jax.ShapeDtypeStruct((72, 2, C), BF),
        jax.ShapeDtypeStruct((18, 2, C), F32),
        jax.ShapeDtypeStruct((6, 2, C), F32),
        jax.ShapeDtypeStruct((2, 24, C), F32),
        jax.ShapeDtypeStruct((6, 2, 768), F32),
        jax.ShapeDtypeStruct((12, 1, POS), F32),
    )
    results = pl.pallas_call(
        functools.partial(kernel, n_lat, n_lon),
        out_shape=shapes,
        in_specs=[pl.BlockSpec(memory_space=pltpu.HBM)] * 14 + [smem],
        out_specs=[vmem] * 7,
        scratch_shapes=scratch,
        compiler_params=pltpu.CompilerParams(
            collective_id=0, has_side_effects=True, vmem_limit_bytes=60 * 1024 * 1024
        ),
    )(
        rel_index,
        bias_table.reshape(12, 1, POS),
        jnp.asarray(index_rows()),
        tokens.transpose(1, 2, 0, 3).reshape(72, 2, C),
        grad_mixed.transpose(1, 2, 0, 3).reshape(72, 2, C),
        w_qkv, w_proj, gains, w_up, w_down.transpose(0, 2, 1),
        *permutations(),
        mask_ids,
    )
    mixed, grad_tokens, qkv, proj, up, down, table = pl.pallas_call(
        hand_over,
        out_shape=shapes,
        in_specs=[pl.BlockSpec(memory_space=pltpu.HBM)] * 7,
        out_specs=[pl.BlockSpec(memory_space=pltpu.HBM)] * 7,
        scratch_shapes=[pltpu.SemaphoreType.DMA((7,))],
        compiler_params=pltpu.CompilerParams(vmem_limit_bytes=60 * 1024 * 1024),
    )(*results)

    def field(value):
        return value.reshape(6, 12, 2, C).transpose(2, 0, 1, 3)

    return (
        field(mixed),
        field(grad_tokens),
        qkv.transpose(1, 2, 0),
        proj.transpose(1, 2, 0),
        up.transpose(0, 2, 1),
        down.transpose(1, 2, 0),
        table.reshape(2, 1, 1, 6, POS),
    )


def solution(mesh):
    field = P(None, "lat", "lon", None)
    table = P(None, None, "lat", None, None)
    in_specs = (field, field, P(), P(), P(), P(), P(), table, P(), P("lat"))
    columns = P(None, None, "lon")
    out_specs = (field, field, columns, columns, columns, columns, table)
    return jax.shard_map(per_device, mesh=mesh, in_specs=in_specs, out_specs=out_specs, check_vma=False)
```

```python
import functools

import jax
import jax.numpy as jnp
import numpy as np
from jax import lax
from jax.experimental import pallas as pl
from jax.experimental.pallas import tpu as pltpu
from jax.sharding import PartitionSpec as P

HEADS = 6
C = 192
TOK = 144
POS = 3312
EPS = 1e-05
NEGATIVE = -1e30
SCALE = 32 ** -0.5
BF = jnp.bfloat16
F32 = jnp.float32
MESH = pl.DeviceIdType.MESH
ROWS = 192
TAIL = 144
N_SEMS = 132


def index_rows():
    rows = np.full((16, 768), -1, np.int32)
    tok = np.arange(TOK)
    level, row, col = tok // 72, tok // 12 % 6, tok % 12
    place = 24 * row + 2 * col + level
    own = 18 * level + row % 3 * 6 + col % 6
    other = 18 * (1 - level) + row % 3 * 6 + col % 6
    low = 48 * (2 * (row // 3) + col // 6)
    high = 48 * (2 * (1 - row // 3) + 1 - col // 6)
    rows[0, place] = tok
    rows[1, tok] = place
    rows[2, tok] = high + own
    rows[3, low + other] = tok
    rows[4, tok] = low + own
    rows[5, high + other] = tok
    rows[6, high + other] = place
    rows[10, place] = high + own
    return rows


def permutations():
    qkv = np.zeros((3 * C, 768), np.float32)
    proj = np.zeros((C, 768), np.float32)
    down = np.zeros((C, 256), np.float32)
    for piece in range(32):
        for i in range(18):
            qkv[18 * piece + i, 24 * piece + i] = 1
        for i in range(6):
            proj[6 * piece + i, 24 * piece + 18 + i] = 1
            down[6 * piece + i, 8 * piece + i] = 1
    return tuple(jnp.asarray(matrix, BF) for matrix in (qkv.T, proj.T, down.T, np.eye(256, dtype=np.float32)))


def dot(a, b):
    return jnp.dot(a, b, preferred_element_type=F32)


def dot_nt(a, b):
    return lax.dot_general(a, b, (((1,), (1,)), ((), ())), preferred_element_type=F32)


def dot_tn(a, b):
    return lax.dot_general(a, b, (((0,), (0,)), ((), ())), preferred_element_type=F32)


def normal(u):
    power = jnp.exp(u * u * -0.5)
    place = 1.0 / (1.0 + jnp.abs(u) * (0.3275911 * 0.5**0.5))
    upper = 0.5 * 1.061405429
    for term in (-1.453152027, 1.421413741, -0.284496736, 0.254829592):
        upper = upper * place + 0.5 * term
    upper = upper * place * power
    return jnp.where(u < 0.0, upper, 1.0 - upper), power * 0.3989422804014327


def norm_parts(v):
    center = v - jnp.mean(v, axis=-1, keepdims=True)
    spread = jnp.mean(center * center, axis=-1, keepdims=True)
    inverse = lax.rsqrt(spread + EPS)
    return center * inverse, inverse


def norm_back(grad, unit, inverse):
    along = jnp.mean(grad * unit, axis=-1, keepdims=True)
    return inverse * (grad - jnp.mean(grad, axis=-1, keepdims=True) - unit * along)


def kernel(
    n_lat, n_lon,
    rel_hbm, table_hbm, const_hbm, tok_hbm, gmix_hbm, wqkv_hbm, wproj_hbm, gains_hbm, wup_hbm, wdown_hbm, pq_hbm, pp_hbm, pd_hbm, eye_hbm, ids_ref,
    mixed_ref, gtok_ref, wg_ref, tgrad_ref,
    rel_ref, table_ref, const_ref, tok_ref, gmix_ref, wqkv_ref, wproj_ref, gains_ref, wup_ref, wdown_ref, pq_ref, pp_ref, pd_ref, eye_ref, load_sem,
    x_ref, qkv_ref, km_ref, vm_ref, s_ref, p_ref, att_ref, u1_ref, i1_ref, mid_ref, gp_ref, hid_ref, u2_ref, i2_ref,
    gup_ref, ds_ref, idx_ref, low_ref, tabf_ref, tab_ref, bias_ref, btail_ref, pk_ref, gall_ref, gsend_ref, grecv_ref, gx_ref, oht_ref, acc_ref,
    r_ref, o1_ref, o2_ref, o3_ref,
    hs_ref, hr_ref,
    second_refs, early_refs, late_refs,
    tb_ref, tr1_ref, t1_ref, tr2_ref, t2_ref, t3_ref, t4_ref,
    ssem, rsem,
):
    loads = [
        pltpu.make_async_copy(src, dst, load_sem.at[k])
        for k, (src, dst) in enumerate([
            (rel_hbm, rel_ref), (table_hbm, table_ref), (const_hbm, const_ref), (tok_hbm, tok_ref), (gmix_hbm, gmix_ref),
            (wqkv_hbm, wqkv_ref), (wproj_hbm, wproj_ref), (gains_hbm, gains_ref), (wup_hbm, wup_ref), (wdown_hbm, wdown_ref),
            (pq_hbm, pq_ref), (pp_hbm, pp_ref), (pd_hbm, pd_ref), (eye_hbm, eye_ref),
        ])
    ]
    for load in loads:
        load.start()
    ny, nz = n_lat // 2, n_lon // 4
    lat, lon = lax.axis_index("lat"), lax.axis_index("lon")
    y, xh = lat >> 1, lat & 1
    z, xl, co = lon >> 2, (lon >> 1) & 1, lon & 1
    x = xh * 2 + xl
    lon_pair = [(lon ^ k, xl ^ (k >> 1), co ^ (k & 1)) for k in range(4)]
    lats = [(lat + k) & (n_lat - 1) for k in range(n_lat)]
    ahead = [((lat - a) & (n_lat - 1), (lon - b) & (n_lon - 1)) for a in (0, 1) for b in (0, 1)]
    back = [((lat + a) & (n_lat - 1), (lon + b) & (n_lon - 1)) for a in (0, 1) for b in (0, 1)]
    z_lons = [(lon + 4 * k) & (n_lon - 1) for k in range(nz)]
    ys, xs = [(y + k) & (ny - 1) for k in range(ny)], [(x + k) & 3 for k in range(4)]
    xy_lons = [lon - xl * 2 + (its_x & 1) * 2 for its_x in xs]
    xy_lats = [[its_y * 2 + (its_x >> 1) for its_x in xs] for its_y in ys]

    greeted = [(lats[k], lon) for k in range(1, n_lat)]
    greeted += [(lat, z_lons[k]) for k in range(1, nz)]
    greeted += [(lat, lon_pair[k][0]) for k in (1, 3)]
    greeted += [(lats[k], lon_pair[2][0]) for k in range(n_lat)]
    greeted += [ahead[1], ahead[3], back[1], back[3]]
    barrier = pltpu.get_barrier_semaphore()
    for device in greeted:
        pl.semaphore_signal(barrier, inc=1, device_id=device, device_id_type=MESH)

    sems = iter(range(N_SEMS))
    sent = []

    def push(src, dst, device):
        k = next(sems)
        copy = pltpu.make_async_remote_copy(
            src_ref=src, dst_ref=dst, send_sem=ssem.at[k], recv_sem=rsem.at[k], device_id=device, device_id_type=MESH
        )
        copy.start()
        sent.append(copy)
        return copy

    def arrive(copies):
        for copy in copies:
            copy.wait_recv()

    def onehot(n_rows, n_lanes, which):
        place = lax.broadcasted_iota(jnp.int32, (n_rows, n_lanes), 0)
        return jnp.where(place == const_ref[which : which + 1, :n_lanes], 1.0, 0.0).astype(BF)

    def moved(matrix, value):
        return dot(matrix, value).astype(BF)

    lane = lax.broadcasted_iota(jnp.int32, (1, C), 1)
    head_lanes = [(lane >= 32 * h) & (lane < 32 * h + 32) for h in range(HEADS)]

    def of_head(value, h):
        return jnp.where(head_lanes[h], value, jnp.zeros_like(value))

    def pack_tail(value, h):
        pk_ref[h, 0:TOK, 0:16] = value
        total = pk_ref[h, pl.ds(0, 24, stride=8), :]
        for j in range(1, 8):
            total = total + pltpu.roll(pk_ref[h, pl.ds(j, 24, stride=8), :], 16 * j, 1)
        return total

    def unpack_tail(value, k):
        for j in range(8):
            rolled = pltpu.roll(value, (128 - 16 * j) % 128, 1)
            btail_ref[k, pl.ds(j, 24, stride=8), :] = rolled

    def gather_bias(b):
        place = lax.broadcasted_iota(jnp.int32, (256, 128), 0).astype(BF)
        one, zero = jnp.ones((256, 128), BF), jnp.zeros((256, 128), BF)

        def step(i, carry):
            for m in range(7):
                group = i * 7 + m
                index = idx_ref[pl.ds(pl.multiple_of(group * 8, 8), 8), :]
                low, high = (index & 255).astype(F32), index >> 8
                picks = []
                for r in range(8):
                    row = jnp.broadcast_to(low[r : r + 1, :], (16, 128)).astype(BF)
                    picks.append(jnp.where(place == jnp.concatenate([row] * 16, axis=0), one, zero))
                rows = dot(tab_ref[b], jnp.concatenate(picks, axis=1))
                for r in range(8):
                    high_row = jnp.broadcast_to(high[r : r + 1, :], (8, 128))
                    found = jnp.zeros((8, 128), F32)
                    for part in range(13):
                        coarse = rows[8 * part : 8 * part + 8, 128 * r : 128 * r + 128]
                        fine = rows[104 + 8 * part : 112 + 8 * part, 128 * r : 128 * r + 128]
                        found = jnp.where(high_row == part, coarse + fine, found)
                    bias_ref[pl.ds(pl.multiple_of(group * 64 + r * 8, 8), 8), :] = found
            return carry

        lax.fori_loop(0, 3, step, 0)
        for h in range(HEADS):
            unpack_tail(bias_ref[pl.ds(8 * TAIL + h, 24, stride=8), :], h)

    half = ROWS // 2

    def share_scores(b):
        gsend_ref[b] = gall_ref[b, pl.ds((1 - co) * 8 * half, 8 * half), :].astype(BF)
        return [push(gsend_ref.at[b], grecv_ref.at[b], (lat, lon_pair[1][0]))]

    def fold_table(b, copies):
        arrive(copies)
        gx_ref[...] = gall_ref[b, pl.ds(co * 8 * half, 8 * half), :] + grecv_ref[b].astype(F32)
        place = lax.broadcasted_iota(jnp.int32, (128, 256), 1).astype(BF)
        one, zero = jnp.ones((128, 256), BF), jnp.zeros((128, 256), BF)

        def step(i, carry):
            total = acc_ref[b]
            for m in range(6):
                group = i * 6 + m
                start = pl.multiple_of(co * half + group * 8, 8)
                high = idx_ref[pl.ds(start, 8), :] >> 8
                left = [[] for _ in range(13)]
                for r in range(8):
                    high_row = jnp.broadcast_to(high[r : r + 1, :], (8, 128))
                    grads = gx_ref[pl.ds(pl.multiple_of(group * 64 + r * 8, 8), 8), :]
                    for part in range(13):
                        left[part].append(jnp.where(high_row == part, grads, 0.0))
                left = jnp.concatenate([jnp.concatenate(rows, axis=1) for rows in left], axis=0).astype(BF)
                span = pl.ds(pl.multiple_of(group * 1024, 1024), 1024)
                if b == 1:
                    block, right = low_ref[group], []
                    for r in range(8):
                        column = jnp.broadcast_to(block[:, r : r + 1], (128, 128)).astype(BF)
                        right.append(jnp.where(place == jnp.concatenate([column] * 2, axis=1), one, zero))
                    right = jnp.concatenate(right, axis=0)
                    oht_ref[span, :] = right
                else:
                    right = oht_ref[span, :]
                total = total + dot(left, right)
            acc_ref[b] = total
            return carry

        lax.fori_loop(0, 2, step, 0)

    def region_codes(place):
        code = jnp.zeros_like(place)
        for part in range(12):
            value = ids_ref[part % 6] + 64 * (part // 6)
            code = jnp.where(place >= 12 * part, value, code)
        return code

    def forward(b):
        tokens = x_ref[b]
        qkv_ref[b] = dot(tokens, wqkv_ref[b]).astype(BF)
        q, k, v = (qkv_ref[b, :, C * i : C * i + C] for i in range(3))
        for h in range(HEADS):
            km_ref[b, TOK * h : TOK * h + TOK, :] = of_head(k, h)
            vm_ref[b, TOK * h : TOK * h + TOK, :] = of_head(v, h)
        s_ref[...] = dot_nt(km_ref[b], q)
        if b == 1:
            codes_t = region_codes(lax.broadcasted_iota(jnp.int32, (TOK, 1), 0))
            codes_s = region_codes(lax.broadcasted_iota(jnp.int32, (1, TOK), 1))
            allowed = codes_s == codes_t
        for h in range(HEADS):
            span = pl.ds(TOK * h, TOK)
            bias = jnp.concatenate([bias_ref[pl.ds(h, TOK, stride=8), :], btail_ref[h, 0:TOK, 0:16]], axis=1)
            scores = s_ref[span, :] * SCALE + bias
            if b == 1:
                scores = jnp.where(allowed, scores, NEGATIVE)
            powers = jnp.exp(scores - jnp.max(scores, axis=0, keepdims=True))
            probs = powers * (1.0 / jnp.sum(powers, axis=0, keepdims=True))
            p_ref[b, span, :] = probs.astype(BF)
        attended = dot_tn(p_ref[b], vm_ref[b]).astype(BF)
        att_ref[b] = attended
        unit, inverse = norm_parts(dot(attended, wproj_ref[b]))
        u1_ref[b], i1_ref[b] = unit, inverse
        middle = (tokens.astype(F32) + unit * gains_ref[b, 0:1, :]).astype(BF)
        mid_ref[b] = middle
        for part in range(3):
            cols = pl.ds(256 * part, 256)
            up = dot(middle, wup_ref[b, :, cols])
            phi, density = normal(up)
            hid_ref[b, :, cols] = (up * phi).astype(BF)
            gp_ref[b, :, cols] = phi + up * density
        unit, inverse = norm_parts(dot_nt(hid_ref[b], wdown_ref[b]))
        u2_ref[b], i2_ref[b] = unit, inverse
        return (middle.astype(F32) + unit * gains_ref[b, 1:2, :]).astype(BF)

    def backward(b, grad, after_up=lambda grad_down: None, after_scores=lambda: None):
        grad = grad.astype(F32)
        grad_down = norm_back(grad * gains_ref[b, 1:2, :], u2_ref[b], i2_ref[b]).astype(BF)
        for part in range(3):
            cols = pl.ds(256 * part, 256)
            grad_hidden = dot(grad_down, wdown_ref[b, :, cols])
            gup_ref[b, :, cols] = (grad_hidden * gp_ref[b, :, cols]).astype(BF)
        grad_middle = grad + dot_nt(gup_ref[b], wup_ref[b])
        after_up(grad_down)
        grad_pre = norm_back(grad_middle * gains_ref[b, 0:1, :], u1_ref[b], i1_ref[b]).astype(BF)
        grad_att = dot_nt(grad_pre, wproj_ref[b]).astype(BF)
        q = qkv_ref[b, :, 0:C]
        s_ref[...] = dot_nt(vm_ref[b], grad_att)
        for h in range(HEADS):
            span = pl.ds(TOK * h, TOK)
            probs = p_ref[b, span, :].astype(F32)
            grad_probs = s_ref[span, :]
            grad_scores = probs * (grad_probs - jnp.sum(grad_probs * probs, axis=0, keepdims=True))
            ds_ref[span, :] = grad_scores.astype(BF)
            gall_ref[b, pl.ds(h, TOK, stride=8), :] = grad_scores[:, 0:128]
            gall_ref[b, pl.ds(8 * TAIL + h, 24, stride=8), :] = pack_tail(grad_scores[:, 128:TOK], h)
        after_scores()
        grad_q = dot_tn(ds_ref[...], km_ref[b])
        grad_k, grad_v = jnp.zeros((TOK, C), F32), jnp.zeros((TOK, C), F32)
        for h in range(HEADS):
            span = pl.ds(TOK * h, TOK)
            grad_k = jnp.where(head_lanes[h], dot(ds_ref[span, :], q), grad_k)
            grad_v = jnp.where(head_lanes[h], dot(p_ref[b, span, :], grad_att), grad_v)
        grad_qkv = jnp.concatenate([grad_q * SCALE, grad_k * SCALE, grad_v], axis=1).astype(BF)

        def grad_in():
            return (grad_middle + dot_nt(grad_qkv, wqkv_ref[b])).astype(BF)

        return grad_in, grad_down, grad_pre, grad_qkv

    def by_owner(buffer, piece):
        return buffer.at[piece % 2, piece // 8, piece // 4 % 2 * 2 + piece // 2 % 2]

    def pack(place, first_row, units):
        for tile in range(len(units) // 2):
            pair = jnp.concatenate([units[2 * tile], units[2 * tile + 1]], axis=0).astype(BF)
            row = first_row + 16 * tile
            place[row : row + 16, :] = pair

    def early_grads(b, grad_down, buffer):
        r_ref[:, 0:128] = mid_ref[b, :, 0:128]
        r_ref[:, C:256] = mid_ref[b, :, 128:C]
        for part in range(3):
            span = slice(256 * part, 256 * part + 256)
            turned = dot_nt(eye_ref[...], gup_ref[b, :, span]).astype(BF)
            grads = dot(turned, r_ref[...])
            o2_ref[span, :] = grads[:, 0:128]
            o1_ref[span, C:256] = grads[:, C:256]
        o3_ref[...] = dot(dot_nt(pd_ref[...], grad_down).astype(BF), hid_ref[b])
        for piece in range(32):
            units = [o2_ref[24 * piece + 8 * i : 24 * piece + 8 * i + 8, :] for i in range(3)]
            units += [o3_ref[8 * piece : 8 * piece + 8, 128 * i : 128 * i + 128] for i in range(6)]
            pack(by_owner(buffer, piece), 0, units + [jnp.zeros((8, 128), F32)])

    def late_grads(b, grad_pre, grad_qkv, buffer, first_row):
        turned = dot_nt(pp_ref[...], grad_pre).astype(BF)
        grads = dot(turned, att_ref[b])
        turned = dot_nt(pq_ref[...], grad_qkv).astype(BF)
        o1_ref[:, 0:C] = grads + dot(turned, x_ref[b])
        for piece in range(32):
            units = [o1_ref[24 * piece + 8 * i : 24 * piece + 8 * i + 8, 128 * m : 128 * m + 128] for m in range(2) for i in range(3)]
            pack(by_owner(buffer, piece), first_row, units)

    class Sum:
        def __init__(self, refs):
            self.sb, self.rc, self.wa, self.rx, self.wc, self.rz, self.wl = refs
            self.copies = []
            self.steps = [self.core, self.along_xy, self.along_z, self.share, self.done]
            self.z_sems = [next(sems) for _ in range(nz - 1)]
            self.lat_sems = [next(sems) for _ in range(n_lat - 1)]

        def next(self):
            if self.steps:
                self.steps.pop(0)()

        def core(self):
            self.copies = [push(self.sb.at[1 - co], self.rc, (lat, lon_pair[1][0]))]

        def along_xy(self):
            arrive(self.copies)
            self.wa[...] = (self.sb[co].astype(F32) + self.rc[...].astype(F32)).astype(BF)
            self.copies = []
            for k in range(1, 4 * ny):
                device = (xy_lats[k // 4][k % 4], xy_lons[k % 4])
                self.copies.append(push(self.wa.at[ys[k // 4], xs[k % 4]], self.rx.at[k - 1], device))

        def to_owner(self):
            slot = ((z - lat) & (nz - 1)) - 1
            return pltpu.make_async_remote_copy(
                src_ref=self.wc, dst_ref=self.rz.at[slot], send_sem=ssem.at[self.z_sems[0]],
                recv_sem=rsem.at[self.z_sems[0] + slot], device_id=(lat, lat * 4 + xl * 2 + co), device_id_type=MESH,
            )

        def from_z(self, k):
            return pltpu.make_async_remote_copy(
                src_ref=self.wc, dst_ref=self.rz.at[k - 1], send_sem=ssem.at[self.z_sems[0]],
                recv_sem=rsem.at[self.z_sems[k - 1]], device_id=(lat, z_lons[k]), device_id_type=MESH,
            )

        def to_lat(self, k):
            return pltpu.make_async_remote_copy(
                src_ref=self.wl, dst_ref=self.wl, send_sem=ssem.at[self.lat_sems[k - 1]],
                recv_sem=rsem.at[self.lat_sems[0]], device_id=(lats[k], lon), device_id_type=MESH,
            )

        def along_z(self):
            arrive(self.copies)
            total = self.wa[y, x].astype(F32)
            for k in range(4 * ny - 1):
                total = total + self.rx[k].astype(F32)
            self.wc[...] = total.astype(BF)

            @pl.when(z != lat)
            def _():
                self.to_owner().start()

        def share(self):
            @pl.when(z == lat)
            def _():
                total = self.wc[...].astype(F32)
                for k in range(1, nz):
                    self.from_z(k).wait_recv()
                    total = total + self.rz[k - 1].astype(F32)
                self.wl[...] = total.astype(BF)
                for k in range(1, n_lat):
                    self.to_lat(k).start()

        def done(self):
            @pl.when(z != lat)
            def _():
                self.to_lat(1).wait_recv()
                self.to_owner().wait_send()

            @pl.when(z == lat)
            def _():
                for k in range(1, n_lat):
                    self.to_lat(k).wait_send()

    class TableSum:
        def __init__(self):
            self.copies = []
            self.steps = [self.pair, self.along_z, self.share_z, self.share_pair, self.done]

        def next(self):
            if self.steps:
                self.steps.pop(0)()

        def pair(self):
            for part in range(26):
                row, lanes = 8 * (part // 2), slice(128 * (part % 2), 128 * (part % 2) + 128)
                both = jnp.concatenate([acc_ref[b, row : row + 8, lanes] for b in range(2)], axis=0)
                tb_ref[part // 16, part // 8 % 2, part % 8] = both.astype(BF)
            for part in range(26, 32):
                tb_ref[part // 16, part // 8 % 2, part % 8] = jnp.zeros((16, 128), BF)
            for k in range(1, 4):
                device, its_xl, its_co = lon_pair[k]
                self.copies.append(push(tb_ref.at[its_co, its_xl], tr1_ref.at[k - 1], (lat, device)))

        def along_z(self):
            arrive(self.copies)
            total = tb_ref[co, xl].astype(F32)
            for k in range(3):
                total = total + tr1_ref[k].astype(F32)
            t1_ref[...] = total.astype(BF)
            self.copies = []
            for k in range(1, nz):
                self.copies.append(push(t1_ref.at[(z + k) & (nz - 1)], tr2_ref.at[k - 1], (lat, z_lons[k])))

        def share_z(self):
            arrive(self.copies)
            total = t1_ref[z].astype(F32)
            for k in range(nz - 1):
                total = total + tr2_ref[k].astype(F32)
            t2_ref[...] = total.astype(BF)
            self.copies = []
            for k in range(1, nz):
                self.copies.append(push(t2_ref, t3_ref.at[z], (lat, z_lons[k])))
            t3_ref[z] = t2_ref[...]

        def share_pair(self):
            arrive(self.copies)
            self.copies = []
            for k in range(1, 4):
                self.copies.append(push(t3_ref, t4_ref.at[co, xl], (lat, lon_pair[k][0])))
            t4_ref[co, xl] = t3_ref[...]

        def done(self):
            arrive(self.copies)

    def send_quarters(which, devices):
        copies = []
        for quarter in range(1, 4):
            copies.append(push(hs_ref.at[which, quarter], hr_ref.at[which, quarter], devices[quarter]))
        hr_ref[which, 0] = hs_ref[which, 0]
        return copies

    pk_ref[...] = jnp.zeros_like(pk_ref)
    gall_ref[...] = jnp.zeros_like(gall_ref)
    r_ref[...] = jnp.zeros_like(r_ref)
    loads[0].wait()
    relative = rel_ref[...].astype(F32).T
    idx_ref[0:TOK, :] = relative[:, 0:128].astype(jnp.int32)
    idx_ref[TAIL : TAIL + 24, :] = pack_tail(relative[:, 128:TOK], 0).astype(jnp.int32)
    idx_ref[TAIL + 18 : ROWS, :] = jnp.full((ROWS - TAIL - 18, 128), -1, jnp.int32)
    low = (idx_ref[pl.ds(pl.multiple_of(co * half, 8), half), :] & 255).astype(F32).T
    for i in range(half // 8):
        low_ref[i] = low[:, 8 * i : 8 * i + 8]
    loads[1].wait()
    tabf_ref[...] = jnp.zeros_like(tabf_ref)
    for b in range(2):
        for part in range(13):
            width = min(256, POS - 256 * part)
            tabf_ref[b, 8 * part : 8 * part + 6, 0:width] = table_ref[6 * b : 6 * b + 6, 0, 256 * part : 256 * part + width]
        table = tabf_ref[b]
        coarse = table.astype(BF)
        tab_ref[b, 0:104, :] = coarse
        tab_ref[b, 104:208, :] = (table - coarse.astype(F32)).astype(BF)
    gather_bias(0)
    for load in loads[2:]:
        load.wait()
    x_ref[0] = moved(onehot(TOK, TOK, 0), tok_ref[...].reshape(TOK, C))
    hs_ref[0] = moved(onehot(192, TOK, 10), gmix_ref[...].reshape(TOK, C)).reshape(4, 48, C)

    first = forward(0)
    hs_ref[1] = moved(onehot(192, TOK, 2), first).reshape(4, 48, C)
    pl.semaphore_wait(barrier, len(greeted))
    copies_x = send_quarters(1, ahead)
    copies_g = send_quarters(0, ahead)
    gather_bias(1)
    acc_ref[...] = jnp.zeros_like(acc_ref)
    arrive(copies_x)
    arrive(copies_g)
    come = onehot(TOK, 192, 3)
    x_ref[1] = moved(come, hr_ref[1].reshape(192, C))
    grad_shifted = moved(come, hr_ref[0].reshape(192, C))

    second = forward(1)
    hs_ref[2] = moved(onehot(192, TOK, 4), second).reshape(4, 48, C)
    grad_second, *rest = backward(1, grad_shifted)
    hs_ref[3] = moved(onehot(192, TOK, 4), grad_second()).reshape(4, 48, C)
    copies_s = send_quarters(3, back)
    copies_m = send_quarters(2, back)
    copies_two = share_scores(1)
    grad_down, grad_pre, grad_qkv = rest
    early_grads(1, grad_down, second_refs[0])
    late_grads(1, grad_pre, grad_qkv, second_refs[0], 80)
    sum_two, sum_early, sum_late = Sum(second_refs), Sum(early_refs), Sum(late_refs)
    sum_two.next()

    arrive(copies_s)
    grad_first = moved(onehot(TOK, 192, 5), hr_ref[3].reshape(192, C))
    sum_two.next()
    sum_table = TableSum()

    def after_up(grad_down):
        early_grads(0, grad_down, early_refs[0])
        sum_early.next()

    def after_scores():
        copies_one = share_scores(0)
        sum_early.next()
        fold_table(1, copies_two)
        fold_table(0, copies_one)
        sum_table.next()

    grad_in, _, grad_pre, grad_qkv = backward(0, grad_first, after_up, after_scores)
    late_grads(0, grad_pre, grad_qkv, late_refs[0], 0)
    sum_late.next()
    sum_table.next()
    sum_two.next()
    sum_late.next()
    gtok_ref[...] = moved(onehot(TOK, TOK, 1), grad_in()).reshape(72, 2, C)
    arrive(copies_m)
    mixed_ref[...] = moved(onehot(TOK, 192, 6), hr_ref[2].reshape(192, C)).reshape(72, 2, C)
    sum_table.next()
    sum_early.next()
    sum_two.next()
    sum_table.next()
    sum_late.next()
    sum_early.next()
    sum_late.next()
    sum_table.next()
    tgrad_ref[...] = t4_ref[...]
    sum_two.next()
    wg_ref[1] = second_refs[-1][...]
    sum_early.next()
    wg_ref[0, 0:80, :] = early_refs[-1][...]
    sum_late.next()
    wg_ref[0, 80:128, :] = late_refs[-1][...]
    for copy in sent:
        copy.wait_send()


def finish(mixed_in, gtok_in, wg_in, table_in, mixed_ref, gtok_ref, qkv_ref, proj_ref, up_ref, down_ref, table_ref):
    mixed_ref[...] = mixed_in[...]
    gtok_ref[...] = gtok_in[...]
    for b in range(2):
        rows = wg_in[b].astype(F32)
        up_ref[b, :, 0:128] = rows[0:24, :]
        up_ref[b, :, 128:C] = rows[104:128, 64:128]
        qkv_ref[:, b, 0:128] = rows[80:98, :]
        qkv_ref[:, b, 128:C] = rows[104:122, 0:64]
        proj_ref[:, b, 0:128] = rows[98:104, :]
        proj_ref[:, b, 128:C] = rows[122:128, 0:64]
        for i in range(6):
            down_ref[:, b, 128 * i : 128 * i + 128] = rows[24 + 8 * i : 30 + 8 * i, :]
    for part in range(26):
        tile = table_in[part // 16, part // 8 % 2, part % 8].astype(F32)
        width = min(128, POS - 128 * part)
        for b in range(2):
            table_ref[6 * b : 6 * b + 6, 0, 128 * part : 128 * part + width] = tile[8 * b : 8 * b + 6, 0:width]


def per_device(tokens, grad_mixed, w_qkv, w_proj, w_up, w_down, gains, bias_table, rel_index, mask_ids):
    n_lat, n_lon = lax.axis_size("lat"), lax.axis_size("lon")
    ny, nz = n_lat // 2, n_lon // 4
    vmem = pl.BlockSpec(memory_space=pltpu.VMEM)
    smem = pl.BlockSpec(memory_space=pltpu.SMEM)

    def buf(*shape, dtype=BF):
        return pltpu.VMEM(shape, dtype)

    def stream(rows):
        return (
            buf(2, ny, 4, rows, 128), buf(ny, 4, rows, 128), buf(ny, 4, rows, 128), buf(4 * ny - 1, rows, 128),
            buf(rows, 128), buf(nz - 1, rows, 128), buf(rows, 128),
        )

    scratch = [
        buf(TOK, TOK, dtype=jnp.int32), buf(12, 1, POS, dtype=F32), buf(16, 768, dtype=jnp.int32),
        buf(72, 2, C), buf(72, 2, C), buf(2, C, 3 * C), buf(2, C, C), buf(2, 2, C, dtype=F32), buf(2, C, 768), buf(2, C, 768),
        buf(768, 3 * C), buf(768, C), buf(256, C), buf(256, 256),
        pltpu.SemaphoreType.DMA((14,)),
        buf(2, TOK, C), buf(2, TOK, 3 * C), buf(2, 6 * TOK, C), buf(2, 6 * TOK, C), buf(6 * TOK, TOK, dtype=F32),
        buf(2, 6 * TOK, TOK), buf(2, TOK, C), buf(2, TOK, C, dtype=F32), buf(2, TOK, 1, dtype=F32), buf(2, TOK, C),
        buf(2, TOK, 768, dtype=F32), buf(2, TOK, 768), buf(2, TOK, C, dtype=F32), buf(2, TOK, 1, dtype=F32),
        buf(2, TOK, 768), buf(6 * TOK, TOK),
        buf(ROWS, 128, dtype=jnp.int32), buf(ROWS // 16, 128, 8, dtype=F32), buf(2, 104, 256, dtype=F32), buf(2, 208, 256),
        buf(8 * 168, 128, dtype=F32), buf(6, 192, 128, dtype=F32), buf(6, 192, 128, dtype=F32),
        buf(2, 8 * ROWS, 128, dtype=F32), buf(2, 4 * ROWS, 128), buf(2, 4 * ROWS, 128),
        buf(4 * ROWS, 128, dtype=F32), buf(64 * ROWS, 256), buf(2, 104, 256, dtype=F32),
        buf(TOK, 256), buf(768, 256, dtype=F32), buf(768, 128, dtype=F32), buf(256, 768, dtype=F32),
        buf(4, 4, 48, C), buf(4, 4, 48, C),
        stream(128), stream(80), stream(48),
        buf(2, 2, 8, 16, 128), buf(3, 8, 16, 128), buf(8, 16, 128), buf(7, 16, 128), buf(16, 128),
        buf(8, 16, 128), buf(2, 2, 8, 16, 128),
        pltpu.SemaphoreType.DMA((N_SEMS,)), pltpu.SemaphoreType.DMA((N_SEMS,)),
    ]
    shapes = (
        jax.ShapeDtypeStruct((72, 2, C), BF),
        jax.ShapeDtypeStruct((72, 2, C), BF),
        jax.ShapeDtypeStruct((18, 2, C), F32),
        jax.ShapeDtypeStruct((6, 2, C), F32),
        jax.ShapeDtypeStruct((2, 24, C), F32),
        jax.ShapeDtypeStruct((6, 2, 768), F32),
        jax.ShapeDtypeStruct((12, 1, POS), F32),
    )
    results = pl.pallas_call(
        functools.partial(kernel, n_lat, n_lon),
        out_shape=(
            jax.ShapeDtypeStruct((72, 2, C), BF),
            jax.ShapeDtypeStruct((72, 2, C), BF),
            jax.ShapeDtypeStruct((2, 128, 128), BF),
            jax.ShapeDtypeStruct((2, 2, 8, 16, 128), BF),
        ),
        in_specs=[pl.BlockSpec(memory_space=pltpu.HBM)] * 14 + [smem],
        out_specs=[vmem] * 4,
        scratch_shapes=scratch,
        compiler_params=pltpu.CompilerParams(
            collective_id=0, has_side_effects=True, vmem_limit_bytes=60 * 1024 * 1024
        ),
    )(
        rel_index,
        bias_table.reshape(12, 1, POS),
        jnp.asarray(index_rows()),
        tokens.transpose(1, 2, 0, 3).reshape(72, 2, C),
        grad_mixed.transpose(1, 2, 0, 3).reshape(72, 2, C),
        w_qkv, w_proj, gains, w_up, w_down.transpose(0, 2, 1),
        *permutations(),
        mask_ids,
    )
    mixed, grad_tokens, qkv, proj, up, down, table = pl.pallas_call(
        finish,
        out_shape=shapes,
        in_specs=[vmem] * 4,
        out_specs=[vmem] * 7,
        compiler_params=pltpu.CompilerParams(vmem_limit_bytes=60 * 1024 * 1024),
    )(*results)

    def field(value):
        return value.reshape(6, 12, 2, C).transpose(2, 0, 1, 3)

    return (
        field(mixed),
        field(grad_tokens),
        qkv.transpose(1, 2, 0),
        proj.transpose(1, 2, 0),
        up.transpose(0, 2, 1),
        down.transpose(1, 2, 0),
        table.reshape(2, 1, 1, 6, POS),
    )


def solution(mesh):
    field = P(None, "lat", "lon", None)
    table = P(None, None, "lat", None, None)
    in_specs = (field, field, P(), P(), P(), P(), P(), table, P(), P("lat"))
    columns = P(None, None, "lon")
    out_specs = (field, field, columns, columns, columns, columns, table)
    return jax.shard_map(per_device, mesh=mesh, in_specs=in_specs, out_specs=out_specs, check_vma=False)
```

```python
import functools

import jax
import jax.numpy as jnp
import numpy as np
from jax import lax
from jax.experimental import pallas as pl
from jax.experimental.pallas import tpu as pltpu
from jax.sharding import PartitionSpec as P

HEADS = 6
C = 192
TOK = 144
POS = 3312
EPS = 1e-05
NEGATIVE = -1e30
SCALE = 32 ** -0.5
BF = jnp.bfloat16
F32 = jnp.float32
MESH = pl.DeviceIdType.MESH
ROWS = 192
TAIL = 144
N_SEMS = 132


def index_rows():
    rows = np.full((16, 768), -1, np.int32)
    tok = np.arange(TOK)
    level, row, col = tok // 72, tok // 12 % 6, tok % 12
    place = 24 * row + 2 * col + level
    own = 18 * level + row % 3 * 6 + col % 6
    other = 18 * (1 - level) + row % 3 * 6 + col % 6
    low = 48 * (2 * (row // 3) + col // 6)
    high = 48 * (2 * (1 - row // 3) + 1 - col // 6)
    rows[0, place] = tok
    rows[1, tok] = place
    rows[2, tok] = high + own
    rows[3, low + other] = tok
    rows[4, tok] = low + own
    rows[5, high + other] = tok
    rows[6, high + other] = place
    rows[10, place] = high + own
    return rows


def permutations():
    qkv = np.zeros((3 * C, 768), np.float32)
    proj = np.zeros((C, 768), np.float32)
    down = np.zeros((C, 256), np.float32)
    for piece in range(32):
        for i in range(18):
            qkv[18 * piece + i, 24 * piece + i] = 1
        for i in range(6):
            proj[6 * piece + i, 24 * piece + 18 + i] = 1
            down[6 * piece + i, 8 * piece + i] = 1
    return tuple(jnp.asarray(matrix, BF) for matrix in (qkv, proj, down))


def dot(a, b):
    return jnp.dot(a, b, preferred_element_type=F32)


def dot_nt(a, b):
    return lax.dot_general(a, b, (((1,), (1,)), ((), ())), preferred_element_type=F32)


def dot_tn(a, b):
    return lax.dot_general(a, b, (((0,), (0,)), ((), ())), preferred_element_type=F32)


def normal(u):
    power = jnp.exp(u * u * -0.5)
    place = 1.0 / (1.0 + jnp.abs(u) * (0.3275911 * 0.5**0.5))
    upper = 0.5 * 1.061405429
    for term in (-1.453152027, 1.421413741, -0.284496736, 0.254829592):
        upper = upper * place + 0.5 * term
    upper = upper * place * power
    return jnp.where(u < 0.0, upper, 1.0 - upper), power * 0.3989422804014327


def norm_parts(v):
    center = v - jnp.mean(v, axis=-1, keepdims=True)
    spread = jnp.mean(center * center, axis=-1, keepdims=True)
    inverse = lax.rsqrt(spread + EPS)
    return center * inverse, inverse


def norm_back(grad, unit, inverse):
    along = jnp.mean(grad * unit, axis=-1, keepdims=True)
    return inverse * (grad - jnp.mean(grad, axis=-1, keepdims=True) - unit * along)


def kernel(
    n_lat, n_lon,
    rel_hbm, table_hbm, const_hbm, tok_hbm, gmix_hbm, wqkv_hbm, wproj_hbm, gains_hbm, wup_hbm, wdown_hbm, pq_hbm, pp_hbm, pd_hbm, ids_ref,
    mixed_ref, gtok_ref, wg_ref, tgrad_ref,
    rel_ref, table_ref, const_ref, tok_ref, gmix_ref, wqkv_ref, wproj_ref, gains_ref, wup_ref, wdown_ref, pq_ref, pp_ref, pd_ref, load_sem,
    x_ref, qkv_ref, km_ref, vm_ref, s_ref, p_ref, att_ref, u1_ref, i1_ref, mid_ref, gp_ref, hid_ref, u2_ref, i2_ref,
    gup_ref, ds_ref, idx_ref, low_ref, tabf_ref, tab_ref, bias_ref, btail_ref, pk_ref, gall_ref, gsend_ref, grecv_ref, gx_ref, acc_ref,
    l_ref, r_ref, o1_ref, o2_ref, o3_ref,
    hs_ref, hr_ref,
    second_refs, early_refs, late_refs,
    tb_ref, tr1_ref, t1_ref, tr2_ref, t2_ref, t3_ref, t4_ref,
    ssem, rsem,
):
    loads = [
        pltpu.make_async_copy(src, dst, load_sem.at[k])
        for k, (src, dst) in enumerate([
            (rel_hbm, rel_ref), (table_hbm, table_ref), (const_hbm, const_ref), (tok_hbm, tok_ref), (gmix_hbm, gmix_ref),
            (wqkv_hbm, wqkv_ref), (wproj_hbm, wproj_ref), (gains_hbm, gains_ref), (wup_hbm, wup_ref), (wdown_hbm, wdown_ref),
            (pq_hbm, pq_ref), (pp_hbm, pp_ref), (pd_hbm, pd_ref),
        ])
    ]
    for load in loads:
        load.start()
    ny, nz = n_lat // 2, n_lon // 4
    lat, lon = lax.axis_index("lat"), lax.axis_index("lon")
    y, xh = lat >> 1, lat & 1
    z, xl, co = lon >> 2, (lon >> 1) & 1, lon & 1
    x = xh * 2 + xl
    lon_pair = [(lon ^ k, xl ^ (k >> 1), co ^ (k & 1)) for k in range(4)]
    lats = [(lat + k) & (n_lat - 1) for k in range(n_lat)]
    ahead = [((lat - a) & (n_lat - 1), (lon - b) & (n_lon - 1)) for a in (0, 1) for b in (0, 1)]
    back = [((lat + a) & (n_lat - 1), (lon + b) & (n_lon - 1)) for a in (0, 1) for b in (0, 1)]
    z_lons = [(lon + 4 * k) & (n_lon - 1) for k in range(nz)]
    ys, xs = [(y + k) & (ny - 1) for k in range(ny)], [(x + k) & 3 for k in range(4)]
    xy_lons = [lon - xl * 2 + (its_x & 1) * 2 for its_x in xs]
    xy_lats = [[its_y * 2 + (its_x >> 1) for its_x in xs] for its_y in ys]

    greeted = [(lats[k], lon) for k in range(1, n_lat)]
    greeted += [(lat, z_lons[k]) for k in range(1, nz)]
    greeted += [(lat, lon_pair[k][0]) for k in (1, 3)]
    greeted += [(lats[k], lon_pair[2][0]) for k in range(n_lat)]
    greeted += [ahead[1], ahead[3], back[1], back[3]]
    barrier = pltpu.get_barrier_semaphore()
    for device in greeted:
        pl.semaphore_signal(barrier, inc=1, device_id=device, device_id_type=MESH)

    sems = iter(range(N_SEMS))
    sent = []

    def push(src, dst, device):
        k = next(sems)
        copy = pltpu.make_async_remote_copy(
            src_ref=src, dst_ref=dst, send_sem=ssem.at[k], recv_sem=rsem.at[k], device_id=device, device_id_type=MESH
        )
        copy.start()
        sent.append(copy)
        return copy

    def arrive(copies):
        for copy in copies:
            copy.wait_recv()

    def onehot(n_rows, n_lanes, which):
        place = lax.broadcasted_iota(jnp.int32, (n_rows, n_lanes), 0)
        return jnp.where(place == const_ref[which : which + 1, :n_lanes], 1.0, 0.0).astype(BF)

    def moved(matrix, value):
        return dot(matrix, value).astype(BF)

    lane = lax.broadcasted_iota(jnp.int32, (1, C), 1)
    head_lanes = [(lane >= 32 * h) & (lane < 32 * h + 32) for h in range(HEADS)]

    def of_head(value, h):
        return jnp.where(head_lanes[h], value, jnp.zeros_like(value))

    def pack_tail(value, h):
        pk_ref[h, 0:TOK, 0:16] = value
        total = pk_ref[h, pl.ds(0, 24, stride=8), :]
        for j in range(1, 8):
            total = total + pltpu.roll(pk_ref[h, pl.ds(j, 24, stride=8), :], 16 * j, 1)
        return total

    def unpack_tail(value, k):
        for j in range(8):
            rolled = pltpu.roll(value, (128 - 16 * j) % 128, 1)
            btail_ref[k, pl.ds(j, 24, stride=8), :] = rolled

    def gather_bias(b):
        place = lax.broadcasted_iota(jnp.int32, (256, 128), 0).astype(BF)
        one, zero = jnp.ones((256, 128), BF), jnp.zeros((256, 128), BF)

        def step(i, carry):
            for m in range(7):
                group = i * 7 + m
                index = idx_ref[pl.ds(pl.multiple_of(group * 8, 8), 8), :]
                low, high = (index & 255).astype(F32), index >> 8
                picks = []
                for r in range(8):
                    row = jnp.broadcast_to(low[r : r + 1, :], (16, 128)).astype(BF)
                    picks.append(jnp.where(place == jnp.concatenate([row] * 16, axis=0), one, zero))
                rows = dot(tab_ref[b], jnp.concatenate(picks, axis=1))
                for r in range(8):
                    high_row = jnp.broadcast_to(high[r : r + 1, :], (8, 128))
                    found = jnp.zeros((8, 128), F32)
                    for part in range(13):
                        coarse = rows[8 * part : 8 * part + 8, 128 * r : 128 * r + 128]
                        fine = rows[104 + 8 * part : 112 + 8 * part, 128 * r : 128 * r + 128]
                        found = jnp.where(high_row == part, coarse + fine, found)
                    bias_ref[pl.ds(pl.multiple_of(group * 64 + r * 8, 8), 8), :] = found
            return carry

        lax.fori_loop(0, 3, step, 0)
        for h in range(HEADS):
            unpack_tail(bias_ref[pl.ds(8 * TAIL + h, 24, stride=8), :], h)

    half = ROWS // 2

    def share_scores(b):
        gsend_ref[b] = gall_ref[b, pl.ds((1 - co) * 8 * half, 8 * half), :].astype(BF)
        return [push(gsend_ref.at[b], grecv_ref.at[b], (lat, lon_pair[1][0]))]

    def add_scores(copies):
        both = []
        for b in range(2):
            arrive(copies[b])
            total = gall_ref[b, pl.ds(co * 8 * half, 8 * half), :] + grecv_ref[b].astype(F32)
            both.append(total.reshape(half, 8, 128))
        gx_ref[...] = jnp.concatenate(both, axis=1).astype(BF)

    def fold_tables():
        place = lax.broadcasted_iota(jnp.int32, (128, 256), 1).astype(BF)
        one, zero = jnp.ones((128, 256), BF), jnp.zeros((128, 256), BF)
        nothing = jnp.zeros((16, 128), BF)

        def step(i, carry):
            total = acc_ref[...]
            for m in range(6):
                group = i * 6 + m
                start = pl.multiple_of(co * half + group * 8, 8)
                high = (idx_ref[pl.ds(start, 8), :] >> 8).astype(F32)
                block = low_ref[group]
                left, right = [[] for _ in range(13)], []
                for r in range(8):
                    high_row = jnp.broadcast_to(high[r : r + 1, :], (16, 128)).astype(BF)
                    grads = gx_ref[group * 8 + r]
                    for part in range(13):
                        left[part].append(jnp.where(high_row == jnp.full((16, 128), part, BF), grads, nothing))
                    column = jnp.broadcast_to(block[:, r : r + 1], (128, 128)).astype(BF)
                    right.append(jnp.where(place == jnp.concatenate([column] * 2, axis=1), one, zero))
                left = jnp.concatenate([jnp.concatenate(rows, axis=1) for rows in left], axis=0)
                total = total + dot(left, jnp.concatenate(right, axis=0))
            acc_ref[...] = total
            return carry

        lax.fori_loop(0, 2, step, 0)

    def region_codes(place):
        code = jnp.zeros_like(place)
        for part in range(12):
            value = ids_ref[part % 6] + 64 * (part // 6)
            code = jnp.where(place >= 12 * part, value, code)
        return code

    def forward(b):
        tokens = x_ref[b]
        qkv_ref[b] = dot(tokens, wqkv_ref[b]).astype(BF)
        q, k, v = (qkv_ref[b, :, C * i : C * i + C] for i in range(3))
        for h in range(HEADS):
            km_ref[b, TOK * h : TOK * h + TOK, :] = of_head(k, h)
            vm_ref[b, TOK * h : TOK * h + TOK, :] = of_head(v, h)
        s_ref[...] = dot_nt(km_ref[b], q)
        if b == 1:
            codes_t = region_codes(lax.broadcasted_iota(jnp.int32, (TOK, 1), 0))
            codes_s = region_codes(lax.broadcasted_iota(jnp.int32, (1, TOK), 1))
            allowed = codes_s == codes_t
        for h in range(HEADS):
            span = pl.ds(TOK * h, TOK)
            bias = jnp.concatenate([bias_ref[pl.ds(h, TOK, stride=8), :], btail_ref[h, 0:TOK, 0:16]], axis=1)
            scores = s_ref[span, :] * SCALE + bias
            if b == 1:
                scores = jnp.where(allowed, scores, NEGATIVE)
            powers = jnp.exp(scores - jnp.max(scores, axis=0, keepdims=True))
            probs = powers * (1.0 / jnp.sum(powers, axis=0, keepdims=True))
            p_ref[b, span, :] = probs.astype(BF)
        attended = dot_tn(p_ref[b], vm_ref[b]).astype(BF)
        att_ref[b] = attended
        unit, inverse = norm_parts(dot(attended, wproj_ref[b]))
        u1_ref[b], i1_ref[b] = unit, inverse
        middle = (tokens.astype(F32) + unit * gains_ref[b, 0:1, :]).astype(BF)
        mid_ref[b] = middle
        for part in range(3):
            cols = pl.ds(256 * part, 256)
            up = dot(middle, wup_ref[b, :, cols])
            phi, density = normal(up)
            hid_ref[b, :, cols] = (up * phi).astype(BF)
            gp_ref[b, :, cols] = phi + up * density
        unit, inverse = norm_parts(dot_nt(hid_ref[b], wdown_ref[b]))
        u2_ref[b], i2_ref[b] = unit, inverse
        return (middle.astype(F32) + unit * gains_ref[b, 1:2, :]).astype(BF)

    def backward(b, grad, after_up=lambda grad_down: None, after_scores=lambda: None):
        grad = grad.astype(F32)
        grad_down = norm_back(grad * gains_ref[b, 1:2, :], u2_ref[b], i2_ref[b]).astype(BF)
        for part in range(3):
            cols = pl.ds(256 * part, 256)
            grad_hidden = dot(grad_down, wdown_ref[b, :, cols])
            gup_ref[b, :, cols] = (grad_hidden * gp_ref[b, :, cols]).astype(BF)
        grad_middle = grad + dot_nt(gup_ref[b], wup_ref[b])
        after_up(grad_down)
        grad_pre = norm_back(grad_middle * gains_ref[b, 0:1, :], u1_ref[b], i1_ref[b]).astype(BF)
        grad_att = dot_nt(grad_pre, wproj_ref[b]).astype(BF)
        q = qkv_ref[b, :, 0:C]
        s_ref[...] = dot_nt(vm_ref[b], grad_att)
        for h in range(HEADS):
            span = pl.ds(TOK * h, TOK)
            probs = p_ref[b, span, :].astype(F32)
            grad_probs = s_ref[span, :]
            grad_scores = probs * (grad_probs - jnp.sum(grad_probs * probs, axis=0, keepdims=True))
            ds_ref[span, :] = grad_scores.astype(BF)
            gall_ref[b, pl.ds(h, TOK, stride=8), :] = grad_scores[:, 0:128]
            gall_ref[b, pl.ds(8 * TAIL + h, 24, stride=8), :] = pack_tail(grad_scores[:, 128:TOK], h)
        after_scores()
        grad_q = dot_tn(ds_ref[...], km_ref[b])
        grad_k, grad_v = jnp.zeros((TOK, C), F32), jnp.zeros((TOK, C), F32)
        for h in range(HEADS):
            span = pl.ds(TOK * h, TOK)
            grad_k = jnp.where(head_lanes[h], dot(ds_ref[span, :], q), grad_k)
            grad_v = jnp.where(head_lanes[h], dot(p_ref[b, span, :], grad_att), grad_v)
        grad_qkv = jnp.concatenate([grad_q * SCALE, grad_k * SCALE, grad_v], axis=1).astype(BF)
        grad_in = (grad_middle + dot_nt(grad_qkv, wqkv_ref[b])).astype(BF)
        return grad_in, grad_down, grad_pre, grad_qkv

    def pack(buffer, piece, first_row, units):
        z_of = piece // 4
        for tile in range(len(units) // 2):
            pair = jnp.concatenate([units[2 * tile], units[2 * tile + 1]], axis=0).astype(BF)
            row = first_row + 16 * tile
            buffer[piece % 2, z_of // 2, z_of % 2 * 2 + piece // 2 % 2, row : row + 16, :] = pair

    def early_grads(b, grad_down, buffer):
        o2_ref[...] = dot_tn(gup_ref[b], mid_ref[b, :, 0:128])
        o3_ref[...] = dot_tn(moved(grad_down, pd_ref[...]), hid_ref[b])
        for piece in range(32):
            units = [o2_ref[24 * piece + 8 * i : 24 * piece + 8 * i + 8, :] for i in range(3)]
            units += [o3_ref[8 * piece : 8 * piece + 8, 128 * i : 128 * i + 128] for i in range(6)]
            pack(buffer, piece, 0, units + [jnp.zeros((8, 128), F32)])

    def late_grads(b, grad_pre, grad_qkv, buffer, first_row):
        l_ref[0:TOK, :] = moved(grad_qkv, pq_ref[...])
        l_ref[TOK : 2 * TOK, :] = moved(grad_pre, pp_ref[...])
        l_ref[2 * TOK : 3 * TOK, :] = gup_ref[b]
        r_ref[0:TOK, 0:192] = x_ref[b]
        r_ref[TOK : 2 * TOK, 0:192] = att_ref[b]
        r_ref[2 * TOK : 3 * TOK, 192:256] = mid_ref[b, :, 128:C]
        o1_ref[...] = dot_tn(l_ref[...], r_ref[...])
        for piece in range(32):
            units = [o1_ref[24 * piece + 8 * i : 24 * piece + 8 * i + 8, 128 * m : 128 * m + 128] for m in range(2) for i in range(3)]
            pack(buffer, piece, first_row, units)

    class Sum:
        def __init__(self, refs, out):
            self.sb, self.rc, self.wa, self.rx, self.wc, self.rz, self.wl = refs
            self.out = out
            self.copies = []
            self.steps = [self.core, self.along_xy, self.along_z, self.share, self.done]
            self.z_sems = [next(sems) for _ in range(nz - 1)]
            self.lat_sems = [next(sems) for _ in range(n_lat - 1)]

        def next(self):
            if self.steps:
                self.steps.pop(0)()

        def core(self):
            self.copies = [push(self.sb.at[1 - co], self.rc, (lat, lon_pair[1][0]))]

        def along_xy(self):
            arrive(self.copies)
            self.wa[...] = (self.sb[co].astype(F32) + self.rc[...].astype(F32)).astype(BF)
            self.copies = []
            for k in range(1, 4 * ny):
                device = (xy_lats[k // 4][k % 4], xy_lons[k % 4])
                self.copies.append(push(self.wa.at[ys[k // 4], xs[k % 4]], self.rx.at[k - 1], device))

        def to_owner(self):
            slot = ((z - lat) & (nz - 1)) - 1
            return pltpu.make_async_remote_copy(
                src_ref=self.wc, dst_ref=self.rz.at[slot], send_sem=ssem.at[self.z_sems[0]],
                recv_sem=rsem.at[self.z_sems[0] + slot], device_id=(lat, lat * 4 + xl * 2 + co), device_id_type=MESH,
            )

        def from_z(self, k):
            return pltpu.make_async_remote_copy(
                src_ref=self.wc, dst_ref=self.rz.at[k - 1], send_sem=ssem.at[self.z_sems[0]],
                recv_sem=rsem.at[self.z_sems[k - 1]], device_id=(lat, z_lons[k]), device_id_type=MESH,
            )

        def to_lat(self, k):
            return pltpu.make_async_remote_copy(
                src_ref=self.wl, dst_ref=self.wl, send_sem=ssem.at[self.lat_sems[k - 1]],
                recv_sem=rsem.at[self.lat_sems[0]], device_id=(lats[k], lon), device_id_type=MESH,
            )

        def along_z(self):
            arrive(self.copies)
            total = self.wa[y, x].astype(F32)
            for k in range(4 * ny - 1):
                total = total + self.rx[k].astype(F32)
            self.wc[...] = total.astype(BF)

            @pl.when(z != lat)
            def _():
                self.to_owner().start()

        def share(self):
            @pl.when(z == lat)
            def _():
                total = self.wc[...].astype(F32)
                for k in range(1, nz):
                    self.from_z(k).wait_recv()
                    total = total + self.rz[k - 1].astype(F32)
                self.wl[...] = total.astype(BF)
                for k in range(1, n_lat):
                    self.to_lat(k).start()

        def done(self):
            @pl.when(z != lat)
            def _():
                self.to_lat(1).wait_recv()
                self.to_owner().wait_send()

            self.out[...] = self.wl[...]

            @pl.when(z == lat)
            def _():
                for k in range(1, n_lat):
                    self.to_lat(k).wait_send()

    class TableSum:
        def __init__(self):
            self.copies = []
            self.steps = [self.pair, self.along_z, self.share_z, self.share_pair, self.done]

        def next(self):
            if self.steps:
                self.steps.pop(0)()

        def pair(self):
            for part in range(26):
                row, lanes = 16 * (part // 2), slice(128 * (part % 2), 128 * (part % 2) + 128)
                both = acc_ref[row : row + 16, lanes]
                tb_ref[part // 16, part // 8 % 2, part % 8] = both.astype(BF)
            for part in range(26, 32):
                tb_ref[part // 16, part // 8 % 2, part % 8] = jnp.zeros((16, 128), BF)
            for k in range(1, 4):
                device, its_xl, its_co = lon_pair[k]
                self.copies.append(push(tb_ref.at[its_co, its_xl], tr1_ref.at[k - 1], (lat, device)))

        def along_z(self):
            arrive(self.copies)
            total = tb_ref[co, xl].astype(F32)
            for k in range(3):
                total = total + tr1_ref[k].astype(F32)
            t1_ref[...] = total.astype(BF)
            self.copies = []
            for k in range(1, nz):
                self.copies.append(push(t1_ref.at[(z + k) & (nz - 1)], tr2_ref.at[k - 1], (lat, z_lons[k])))

        def share_z(self):
            arrive(self.copies)
            total = t1_ref[z].astype(F32)
            for k in range(nz - 1):
                total = total + tr2_ref[k].astype(F32)
            t2_ref[...] = total.astype(BF)
            self.copies = []
            for k in range(1, nz):
                self.copies.append(push(t2_ref, t3_ref.at[z], (lat, z_lons[k])))
            t3_ref[z] = t2_ref[...]

        def share_pair(self):
            arrive(self.copies)
            self.copies = []
            for k in range(1, 4):
                self.copies.append(push(t3_ref, t4_ref.at[co, xl], (lat, lon_pair[k][0])))
            t4_ref[co, xl] = t3_ref[...]

        def done(self):
            arrive(self.copies)
            tgrad_ref[...] = t4_ref[...]

    def send_quarters(which, devices):
        copies = []
        for quarter in range(1, 4):
            copies.append(push(hs_ref.at[which, quarter], hr_ref.at[which, quarter], devices[quarter]))
        hr_ref[which, 0] = hs_ref[which, 0]
        return copies

    pk_ref[...] = jnp.zeros_like(pk_ref)
    gall_ref[...] = jnp.zeros_like(gall_ref)
    r_ref[...] = jnp.zeros_like(r_ref)
    loads[0].wait()
    relative = rel_ref[...].astype(F32).T
    idx_ref[0:TOK, :] = relative[:, 0:128].astype(jnp.int32)
    idx_ref[TAIL : TAIL + 24, :] = pack_tail(relative[:, 128:TOK], 0).astype(jnp.int32)
    idx_ref[TAIL + 18 : ROWS, :] = jnp.full((ROWS - TAIL - 18, 128), -1, jnp.int32)
    low = (idx_ref[pl.ds(pl.multiple_of(co * half, 8), half), :] & 255).astype(F32).T
    for i in range(half // 8):
        low_ref[i] = low[:, 8 * i : 8 * i + 8]
    loads[1].wait()
    tabf_ref[...] = jnp.zeros_like(tabf_ref)
    for b in range(2):
        for part in range(13):
            width = min(256, POS - 256 * part)
            tabf_ref[b, 8 * part : 8 * part + 6, 0:width] = table_ref[6 * b : 6 * b + 6, 0, 256 * part : 256 * part + width]
        table = tabf_ref[b]
        coarse = table.astype(BF)
        tab_ref[b, 0:104, :] = coarse
        tab_ref[b, 104:208, :] = (table - coarse.astype(F32)).astype(BF)
    gather_bias(0)
    for load in loads[2:]:
        load.wait()
    x_ref[0] = moved(onehot(TOK, TOK, 0), tok_ref[...].reshape(TOK, C))
    hs_ref[0] = moved(onehot(192, TOK, 10), gmix_ref[...].reshape(TOK, C)).reshape(4, 48, C)

    first = forward(0)
    hs_ref[1] = moved(onehot(192, TOK, 2), first).reshape(4, 48, C)
    pl.semaphore_wait(barrier, len(greeted))
    copies_x = send_quarters(1, ahead)
    copies_g = send_quarters(0, ahead)
    gather_bias(1)
    acc_ref[...] = jnp.zeros_like(acc_ref)
    arrive(copies_x)
    arrive(copies_g)
    come = onehot(TOK, 192, 3)
    x_ref[1] = moved(come, hr_ref[1].reshape(192, C))
    grad_shifted = moved(come, hr_ref[0].reshape(192, C))

    second = forward(1)
    hs_ref[2] = moved(onehot(192, TOK, 4), second).reshape(4, 48, C)
    grad_second, *rest = backward(1, grad_shifted)
    hs_ref[3] = moved(onehot(192, TOK, 4), grad_second).reshape(4, 48, C)
    copies_s = send_quarters(3, back)
    copies_m = send_quarters(2, back)
    copies_two = share_scores(1)
    grad_down, grad_pre, grad_qkv = rest
    early_grads(1, grad_down, second_refs[0])
    late_grads(1, grad_pre, grad_qkv, second_refs[0], 80)
    sum_two = Sum(second_refs, wg_ref.at[1])
    sum_early = Sum(early_refs, wg_ref.at[0, 0:80])
    sum_late = Sum(late_refs, wg_ref.at[0, 80:128])
    sum_two.next()

    arrive(copies_s)
    grad_first = moved(onehot(TOK, 192, 5), hr_ref[3].reshape(192, C))
    sum_two.next()

    def after_up(grad_down):
        early_grads(0, grad_down, early_refs[0])
        sum_early.next()

    copies_one = []

    def after_scores():
        copies_one.extend(share_scores(0))
        sum_early.next()

    grad_in, _, grad_pre, grad_qkv = backward(0, grad_first, after_up, after_scores)
    add_scores([copies_one, copies_two])
    fold_tables()
    sum_table = TableSum()
    sum_table.next()
    late_grads(0, grad_pre, grad_qkv, late_refs[0], 0)
    sum_late.next()
    sum_two.next()
    sum_table.next()
    sum_late.next()
    arrive(copies_m)
    mixed_ref[...] = moved(onehot(TOK, 192, 6), hr_ref[2].reshape(192, C)).reshape(72, 2, C)
    gtok_ref[...] = moved(onehot(TOK, TOK, 1), grad_in).reshape(72, 2, C)
    sum_early.next()
    sum_table.next()
    sum_two.next()
    sum_late.next()
    sum_table.next()
    sum_early.next()
    sum_late.next()
    sum_table.next()
    sum_two.next()
    sum_early.next()
    sum_late.next()
    for copy in sent:
        copy.wait_send()


def finish(mixed_in, gtok_in, wg_in, table_in, mixed_ref, gtok_ref, qkv_ref, proj_ref, up_ref, down_ref, table_ref):
    mixed_ref[...] = mixed_in[...]
    gtok_ref[...] = gtok_in[...]
    for b in range(2):
        rows = wg_in[b].astype(F32)
        up_ref[b, :, 0:128] = rows[0:24, :]
        up_ref[b, :, 128:C] = rows[104:128, 64:128]
        qkv_ref[:, b, 0:128] = rows[80:98, :]
        qkv_ref[:, b, 128:C] = rows[104:122, 0:64]
        proj_ref[:, b, 0:128] = rows[98:104, :]
        proj_ref[:, b, 128:C] = rows[122:128, 0:64]
        for i in range(6):
            down_ref[:, b, 128 * i : 128 * i + 128] = rows[24 + 8 * i : 30 + 8 * i, :]
    for part in range(26):
        tile = table_in[part // 16, part // 8 % 2, part % 8].astype(F32)
        width = min(128, POS - 128 * part)
        for b in range(2):
            table_ref[6 * b : 6 * b + 6, 0, 128 * part : 128 * part + width] = tile[8 * b : 8 * b + 6, 0:width]


def per_device(tokens, grad_mixed, w_qkv, w_proj, w_up, w_down, gains, bias_table, rel_index, mask_ids):
    n_lat, n_lon = lax.axis_size("lat"), lax.axis_size("lon")
    ny, nz = n_lat // 2, n_lon // 4
    vmem = pl.BlockSpec(memory_space=pltpu.VMEM)
    smem = pl.BlockSpec(memory_space=pltpu.SMEM)

    def buf(*shape, dtype=BF):
        return pltpu.VMEM(shape, dtype)

    def stream(rows):
        return (
            buf(2, ny, 4, rows, 128), buf(ny, 4, rows, 128), buf(ny, 4, rows, 128), buf(4 * ny - 1, rows, 128),
            buf(rows, 128), buf(nz - 1, rows, 128), buf(rows, 128),
        )

    scratch = [
        buf(TOK, TOK, dtype=jnp.int32), buf(12, 1, POS, dtype=F32), buf(16, 768, dtype=jnp.int32),
        buf(72, 2, C), buf(72, 2, C), buf(2, C, 3 * C), buf(2, C, C), buf(2, 2, C, dtype=F32), buf(2, C, 768), buf(2, C, 768),
        buf(3 * C, 768), buf(C, 768), buf(C, 256),
        pltpu.SemaphoreType.DMA((13,)),
        buf(2, TOK, C), buf(2, TOK, 3 * C), buf(2, 6 * TOK, C), buf(2, 6 * TOK, C), buf(6 * TOK, TOK, dtype=F32),
        buf(2, 6 * TOK, TOK), buf(2, TOK, C), buf(2, TOK, C, dtype=F32), buf(2, TOK, 1, dtype=F32), buf(2, TOK, C),
        buf(2, TOK, 768, dtype=F32), buf(2, TOK, 768), buf(2, TOK, C, dtype=F32), buf(2, TOK, 1, dtype=F32),
        buf(2, TOK, 768), buf(6 * TOK, TOK),
        buf(ROWS, 128, dtype=jnp.int32), buf(ROWS // 16, 128, 8, dtype=F32), buf(2, 104, 256, dtype=F32), buf(2, 208, 256),
        buf(8 * 168, 128, dtype=F32), buf(6, 192, 128, dtype=F32), buf(6, 192, 128, dtype=F32),
        buf(2, 8 * ROWS, 128, dtype=F32), buf(2, 4 * ROWS, 128), buf(2, 4 * ROWS, 128),
        buf(ROWS // 2, 16, 128), buf(208, 256, dtype=F32),
        buf(3 * TOK, 768), buf(3 * TOK, 256), buf(768, 256, dtype=F32), buf(768, 128, dtype=F32), buf(256, 768, dtype=F32),
        buf(4, 4, 48, C), buf(4, 4, 48, C),
        stream(128), stream(80), stream(48),
        buf(2, 2, 8, 16, 128), buf(3, 8, 16, 128), buf(8, 16, 128), buf(7, 16, 128), buf(16, 128),
        buf(8, 16, 128), buf(2, 2, 8, 16, 128),
        pltpu.SemaphoreType.DMA((N_SEMS,)), pltpu.SemaphoreType.DMA((N_SEMS,)),
    ]
    results = pl.pallas_call(
        functools.partial(kernel, n_lat, n_lon),
        out_shape=(
            jax.ShapeDtypeStruct((72, 2, C), BF),
            jax.ShapeDtypeStruct((72, 2, C), BF),
            jax.ShapeDtypeStruct((2, 128, 128), BF),
            jax.ShapeDtypeStruct((2, 2, 8, 16, 128), BF),
        ),
        in_specs=[pl.BlockSpec(memory_space=pltpu.HBM)] * 13 + [smem],
        out_specs=[vmem] * 4,
        scratch_shapes=scratch,
        compiler_params=pltpu.CompilerParams(
            collective_id=0, has_side_effects=True, vmem_limit_bytes=60 * 1024 * 1024
        ),
    )(
        rel_index,
        bias_table.reshape(12, 1, POS),
        jnp.asarray(index_rows()),
        tokens.transpose(1, 2, 0, 3).reshape(72, 2, C),
        grad_mixed.transpose(1, 2, 0, 3).reshape(72, 2, C),
        w_qkv, w_proj, gains, w_up, w_down.transpose(0, 2, 1),
        *permutations(),
        mask_ids,
    )
    mixed, grad_tokens, qkv, proj, up, down, table = pl.pallas_call(
        finish,
        out_shape=(
            jax.ShapeDtypeStruct((72, 2, C), BF),
            jax.ShapeDtypeStruct((72, 2, C), BF),
            jax.ShapeDtypeStruct((18, 2, C), F32),
            jax.ShapeDtypeStruct((6, 2, C), F32),
            jax.ShapeDtypeStruct((2, 24, C), F32),
            jax.ShapeDtypeStruct((6, 2, 768), F32),
            jax.ShapeDtypeStruct((12, 1, POS), F32),
        ),
        in_specs=[vmem] * 4,
        out_specs=[vmem] * 7,
        compiler_params=pltpu.CompilerParams(vmem_limit_bytes=60 * 1024 * 1024),
    )(*results)

    def field(value):
        return value.reshape(6, 12, 2, C).transpose(2, 0, 1, 3)

    return (
        field(mixed),
        field(grad_tokens),
        qkv.transpose(1, 2, 0),
        proj.transpose(1, 2, 0),
        up.transpose(0, 2, 1),
        down.transpose(1, 2, 0),
        table.reshape(2, 1, 1, 6, POS),
    )


def solution(mesh):
    field = P(None, "lat", "lon", None)
    table = P(None, None, "lat", None, None)
    in_specs = (field, field, P(), P(), P(), P(), P(), table, P(), P("lat"))
    columns = P(None, None, "lon")
    out_specs = (field, field, columns, columns, columns, columns, table)
    return jax.shard_map(per_device, mesh=mesh, in_specs=in_specs, out_specs=out_specs, check_vma=False)
```
